32 devices in a mesh: space: 8 (over y, x, core), filt: 4 (over z).
Axes of the slice: x: 2, y: 2, z: 4, core: 2. Of those that a mesh axis runs over, the one named last changes fastest.
Arguments:
- volume: bfloat16 [4, 32, 64, 512], P(None, 'space', 'filt'), may hold values from -6 to 6
- stem_weight: bfloat16 [27, 4, 32], replicated, may hold values from -0.625 to 0.625
- middle_weight: bfloat16 [27, 32, 64], P(None, None, 'filt'), may hold values from -0.21875 to 0.21875
- cotangent: bfloat16 [64, 8, 16, 128], P('filt', 'space'), may hold values from -6 to 6
Outputs:
- features: bfloat16 [64, 8, 16, 128], P('filt', 'space')
- middle_gradient: float32 [27, 32, 64], P(None, None, 'filt')
- stem_gradient: float32 [27, 4, 32], replicated
The draws below stay inside these ranges and needn't reach their ends.
All inputs are finite; a program needn't handle non-finite values.
Results may differ from the reference program's by a relative error of at most 0.019.
Values may be sent and summed in bfloat16 or wider, within the bound.
No kernel may reach another device: no remote copies, remote signals or barrier semaphores. Data moves between devices by JAX's collectives and lax.ppermute only.
A program may use at most 64 MiB of HBM per device.

```python
import math
import jax
import jax.numpy as jnp
from jax import lax

C_IN = 4
C1 = 32
C2 = 64
NZ = 512
NX = 32
NY = 64


def shard_levels(own_key, dims, cuts, smallest, high):
    def one(position, shards_of):
        steps = jax.random.uniform(jax.random.fold_in(jax.random.fold_in(own_key, 6), position), (shards_of,), jnp.float32, smallest / len(cuts), high / len(cuts))
        return jnp.repeat(jnp.exp(steps), dims[position] // shards_of).reshape((-1,) + (1,) * (len(dims) - position - 1))

    level = one(*cuts[0])
    for cut in cuts[1:]:
        level = level * one(*cut)
    return level


def centred(rng, extent, width, bound, split=(), held_as=jnp.bfloat16):
    values = width * jax.random.normal(rng, extent, jnp.float32)
    if split:
        values = values * shard_levels(rng, extent, split, -0.22, 0.18)
    return jnp.clip(values, -bound, bound).astype(held_as)


def setup_inputs(seed: int = 0) -> dict:
    seeds = jax.random.split(jax.random.key(seed), 5)
    return {
        "volume": centred(seeds[0], (C_IN, NX, NY, NZ), 1.0, 6.0, ((1, 8), (2, 4))),
        "stem_weight": centred(seeds[1], (27, C_IN, C1), (27 * C_IN) ** -0.5, 0.625),
        "middle_weight": centred(seeds[2], (27, C1, C2), (27 * C1) ** -0.5, 0.21875, ((2, 4),)),
        "cotangent": centred(seeds[3], (C2, NX // 4, NY // 4, NZ // 4), 1.0, 6.0, ((0, 4), (1, 8))),
    }


def smooth_leaky(values):
    return 0.3 * values + 0.7 * jax.nn.softplus(values)

def leaky_slope(values):
    return 0.3 + 0.7 * jax.nn.sigmoid(values)

def conv_forward(padded, weight):
    kernel = weight.reshape(3, 3, 3, weight.shape[1], weight.shape[2])
    result = lax.conv_general_dilated(padded[None], kernel, (2, 2, 2), 'VALID', dimension_numbers=('NCDHW', 'DHWIO', 'NCDHW'), preferred_element_type=jnp.float32)
    return result[0]

def conv_input(delta, weight):
    kernel = weight.reshape(3, 3, 3, weight.shape[1], weight.shape[2])[::-1, ::-1, ::-1].transpose(0, 1, 2, 4, 3)
    result = lax.conv_general_dilated(delta[None], kernel, (1, 1, 1), ((2, 2), (2, 2), (2, 2)), lhs_dilation=(2, 2, 2), dimension_numbers=('NCDHW', 'DHWIO', 'NCDHW'), preferred_element_type=jnp.float32)
    return result[0]

def conv_kernel(padded, delta):
    result = lax.conv_general_dilated(padded[None], delta[None], (1, 1, 1), 'VALID', rhs_dilation=(2, 2, 2), dimension_numbers=('CNDHW', 'IODHW', 'NCDHW'), preferred_element_type=jnp.float32)
    return result.transpose(2, 3, 4, 0, 1).reshape(27, padded.shape[0], delta.shape[0])

def reference(volume, stem_weight, middle_weight, cotangent):
    padding = ((0, 0), (1, 0), (1, 0), (1, 0))
    stem_padded = jnp.pad(volume, padding)
    stem_pre = conv_forward(stem_padded, stem_weight)
    stem_act = lax.optimization_barrier(smooth_leaky(stem_pre).astype(jnp.bfloat16))
    middle_padded = jnp.pad(stem_act, padding)
    middle_pre = conv_forward(middle_padded, middle_weight)
    features = smooth_leaky(middle_pre).astype(jnp.bfloat16)
    middle_delta = (cotangent.astype(jnp.float32) * leaky_slope(middle_pre)).astype(jnp.bfloat16)
    middle_cells = NX // 4 * (NY // 4) * (NZ // 4)
    middle_gradient = conv_kernel(middle_padded, middle_delta) / math.sqrt(middle_cells)
    padded_gradient = conv_input(middle_delta, middle_weight)
    stem_delta = (padded_gradient[:, 1:, 1:, 1:] * leaky_slope(stem_pre)).astype(jnp.bfloat16)
    stem_cells = NX // 2 * (NY // 2) * (NZ // 2)
    stem_gradient = conv_kernel(stem_padded, stem_delta) / math.sqrt(stem_cells)
    return (features, middle_gradient, stem_gradient)
```

```python
import functools
import math

import jax
import jax.numpy as jnp
import numpy as np
from jax import lax
from jax.experimental import pallas as pl
from jax.experimental.pallas import tpu as pltpu
from jax.sharding import PartitionSpec as P

F32 = jnp.float32
BF16 = jnp.bfloat16
LANES = 128
STEM_ROWS = 288


def nn(a, b):
    return lax.dot_general(a, b, (((1,), (0,)), ((), ())), preferred_element_type=F32)


def nt(a, b):
    return lax.dot_general(a, b, (((1,), (1,)), ((), ())), preferred_element_type=F32)


def place_table():
    table = np.zeros((2, LANES, STEM_ROWS), np.float32)
    for even_odd in range(2):
        for a in range(3):
            for b in range(3):
                for d in range(3):
                    q = 2 * even_odd + d - 1
                    shifted, phase = (1, 3) if q < 0 else (0, q)
                    for c in range(4):
                        column = 96 * a + 48 * shifted + 16 * b + 4 * phase + c
                        table[even_odd, 4 * (9 * a + 3 * b + d) + c, column] = 1.0
    return table


def rows_lanes(shape):
    return lax.broadcasted_iota(jnp.int32, shape, 0), lax.broadcasted_iota(jnp.int32, shape, 1)


def regroup_kernel(volume, own, slab_x, slab_y, corner):
    channels, planes, width, depth = volume.shape
    z, column = rows_lanes((depth, depth))
    select = (z == 4 * (column & (LANES - 1)) + (column // LANES)).astype(F32).astype(BF16)
    row, column = rows_lanes((16 * width, 16 * width))
    turn = ((row & 15) * 16 + (row // 16) == column).astype(F32).astype(BF16)
    picked = nn(volume[...].reshape(channels * planes * width, depth), select).astype(BF16)
    for x in range(planes):
        parts = []
        for phase in range(4):
            for c in range(channels):
                start = (c * planes + x) * width
                parts.append(picked[start : start + width, phase * LANES : (phase + 1) * LANES])
        plane = nn(turn, jnp.concatenate(parts, axis=0)).astype(BF16)
        own[x] = plane
        slab_y[x] = plane[-48:]
        if x > 0:
            slab_x[x - 1] = plane
            corner[x - 1] = plane[-48:]


def softplus_sigmoid(values):
    small = jnp.exp(-jnp.abs(values))
    inverse = 1.0 / (1.0 + small)
    soft = jnp.maximum(values, 0.0) + jnp.log(1.0 + small)
    return soft, jnp.where(values >= 0.0, inverse, small * inverse)


def roll_lanes(values, amount):
    lane = lax.broadcasted_iota(jnp.int32, values.shape, 1)
    edge = 0 if amount == 1 else LANES - 1
    rolled = pltpu.roll(values, amount % LANES, 1)
    return jnp.where(lane == edge, 0.0, rolled)


def main_kernel(
    own, slab_x, slab_y, corner, stem_w, place, gathered, features, slots, cols, mid_cols, slope, stem_back, odd_cols,
):
    blocks = gathered.shape[0]
    keep_x = jnp.where(lax.axis_index("space") > 0, 1.0, 0.0).astype(F32)
    keep_y = jnp.where(lax.axis_index("filt") > 0, 1.0, 0.0).astype(F32)

    for x in range(7):
        low = corner[x] if x < 3 else slab_y[x - 3]
        high = slab_x[x] if x < 3 else own[x - 3]
        plane = jnp.concatenate([low, high], axis=0)
        shifted = roll_lanes(plane.astype(F32), 1).astype(BF16)
        for j in range(9):
            lanes = pl.ds(j * LANES, LANES)
            cols[x, 0:48, lanes] = plane[32 * j : 32 * j + 48]
            cols[x, 48:96, lanes] = shifted[32 * j : 32 * j + 48]

    weights = jnp.concatenate([nn(stem_w[...], place[0]), nn(stem_w[...], place[1])], axis=0).astype(BF16)
    for i in range(3):
        pre = nn(weights, cols[2 * i : 2 * i + 3].reshape(STEM_ROWS, 9 * LANES))
        soft, sig = softplus_sigmoid(pre)
        act = 0.3 * pre + 0.7 * soft
        lean = 0.3 + 0.7 * sig
        keep = jnp.where(lax.broadcasted_iota(jnp.int32, pre.shape, 1) < LANES, keep_y, 1.0)
        if i == 0:
            keep = keep * keep_x
        slope[i] = lean * keep
        act = act * keep
        for j in range(9):
            even = act[0:32, j * LANES : (j + 1) * LANES]
            odd = act[32:64, j * LANES : (j + 1) * LANES]
            for d, part in ((0, roll_lanes(odd, 1)), (1, even), (2, odd)):
                part = part.astype(BF16)
                for b in range(3):
                    if (j - b) % 2 == 0 and 0 <= (j - b) // 2 < 4:
                        row = 32 * (9 * i + 3 * b + d)
                        mid_cols[row : row + 32, pl.ds((j - b) // 2 * LANES, LANES)] = part

    mid_w = gathered[:, :, 0:896].reshape(blocks * 16, 896)
    cotangent = gathered[:, :, 896:1408].reshape(blocks * 16, 512)
    pre = nn(mid_w[:, 0:864], mid_cols[...])
    soft, sig = softplus_sigmoid(pre)
    features[...] = (0.3 * pre + 0.7 * soft).astype(BF16).reshape(features.shape)
    delta = cotangent.astype(F32) * (0.3 + 0.7 * sig)
    delta_low = delta.astype(BF16)
    mid_grad = nt(delta_low, mid_cols[...])

    turned = jnp.concatenate(
        [mid_w[:, t * LANES : (t + 1) * LANES].astype(F32).T for t in range(7)], axis=0
    ).astype(BF16)
    zero = jnp.zeros((32, blocks * 16), BF16)

    def block(a, b, d):
        row = 32 * (9 * a + 3 * b + d)
        return turned[row : row + 32]

    def wide(a, b):
        even = jnp.concatenate([block(a, b, 1), zero], axis=1)
        odd = jnp.concatenate([block(a, b, 2), block(a, b, 0)], axis=1)
        return jnp.concatenate([even, odd], axis=0)

    both = jnp.concatenate(
        [delta_low]
        + [
            jnp.concatenate(
                [roll_lanes(delta[:, j * LANES : (j + 1) * LANES], -1) for j in range(4)], axis=1
            ).astype(BF16)
        ],
        axis=0,
    )
    nothing = jnp.zeros((2 * blocks * 16, LANES), BF16)
    pair = jnp.concatenate(
        [jnp.concatenate([both, nothing], axis=1), jnp.concatenate([nothing, both], axis=1)], axis=0
    )
    stem_grad = jnp.zeros((64, STEM_ROWS), F32)
    for i in range(3):
        odd_back = nn(wide(i, 1), both)
        even_back = nn(jnp.concatenate([wide(i, 0), wide(i, 2)], axis=1), pair)
        for j in range(9):
            source = even_back if j % 2 == 0 else odd_back
            part = source[:, (j // 2) * LANES : (j // 2 + 1) * LANES]
            lanes = pl.ds(j * LANES, LANES)
            stem_back[i, :, lanes] = (part * slope[i, :, lanes]).astype(BF16)
        stem_grad += nt(stem_back[i], cols[2 * i : 2 * i + 3].reshape(STEM_ROWS, 9 * LANES))
    high = stem_grad.astype(BF16)
    low = (stem_grad - high.astype(F32)).astype(BF16)
    taken = sum(
        nt(part[32 * e : 32 * e + 32], place[e]) for part in (high, low) for e in range(2)
    )
    high = taken.astype(BF16)
    low = (taken - high.astype(F32)).astype(BF16)

    mid_low = mid_grad.astype(BF16)
    mid_low = jnp.concatenate([mid_low, jnp.zeros((blocks * 16, 32), BF16)], axis=1)
    per = slots.shape[2]
    pieces = 11
    for f in range(blocks):
        for u in range(slots.shape[0] * per):
            if u < 7:
                value = mid_low[16 * f : 16 * f + 16, u * LANES : (u + 1) * LANES]
            elif u < pieces:
                value = (high, low)[(u - 7) // 2][16 * ((u - 7) % 2) : 16 * ((u - 7) % 2) + 16]
            else:
                value = jnp.zeros((16, LANES), BF16)
            slots[u // per, f, u % per] = value


def whole(count):
    return [pl.BlockSpec(memory_space=pltpu.VMEM)] * count


def body(volume, stem_weight, middle_weight, cotangent):
    spaces, filts = lax.axis_size("space"), lax.axis_size("filt")
    channels, planes, width, depth = volume.shape
    stem_cells = (planes // 2) * spaces * (width // 2) * filts * (depth // 2)
    middle_cells = stem_cells // 8
    limit = pltpu.CompilerParams(vmem_limit_bytes=48 * 1024 * 1024)

    mid_w = middle_weight.transpose(2, 0, 1).reshape(16, 864)
    mid_w = jnp.pad(mid_w, ((0, 0), (0, 32)))
    cot = cotangent.reshape(16, filts, 512).transpose(1, 0, 2)
    packed = jnp.concatenate([jnp.broadcast_to(mid_w[None], (filts, 16, 896)), cot], axis=2)
    gathered = lax.all_to_all(packed, "filt", 0, 0, tiled=True)

    own, slab_x, slab_y, corner = pl.pallas_call(
        regroup_kernel,
        out_shape=[
            jax.ShapeDtypeStruct((planes, 16 * width, LANES), BF16),
            jax.ShapeDtypeStruct((planes - 1, 16 * width, LANES), BF16),
            jax.ShapeDtypeStruct((planes, 48, LANES), BF16),
            jax.ShapeDtypeStruct((planes - 1, 48, LANES), BF16),
        ],
        in_specs=whole(1),
        out_specs=whole(4),
        compiler_params=limit,
        name="regroup",
    )(volume)
    route_x = [(s - 1, s) for s in range(1, spaces)]
    route_y = [(f - 1, f) for f in range(1, filts)]
    route_xy = [
        ((s - 1) * filts + f - 1, s * filts + f) for s in range(1, spaces) for f in range(1, filts)
    ]
    slab_x = lax.ppermute(slab_x, "space", route_x)
    slab_y = lax.ppermute(slab_y, "filt", route_y)
    corner = lax.ppermute(corner, ("space", "filt"), route_xy)

    stem_w = jnp.pad(stem_weight.reshape(108, 32).T, ((0, 0), (0, 20)))
    place = jnp.asarray(place_table(), BF16)
    per = -(-11 // spaces)
    features, slots = pl.pallas_call(
        main_kernel,
        out_shape=[
            jax.ShapeDtypeStruct((filts, 16, 512), BF16),
            jax.ShapeDtypeStruct((spaces, filts, per, 16, LANES), BF16),
        ],
        in_specs=whole(7),
        out_specs=whole(2),
        scratch_shapes=[
            pltpu.VMEM((7, 96, 9 * LANES), BF16),
            pltpu.VMEM((864, 512), BF16),
            pltpu.VMEM((3, 64, 9 * LANES), F32),
            pltpu.VMEM((3, 64, 9 * LANES), BF16),
            pltpu.VMEM((8, LANES), F32),
        ],
        compiler_params=limit,
        name="sections",
    )(own, slab_x, slab_y, corner, stem_w, place, gathered)

    features = lax.all_to_all(features, "filt", 0, 0, tiled=True)
    features = features.transpose(1, 0, 2).reshape(16, 1, 4 * filts, LANES)

    slots = slots.reshape(spaces * filts, per, 16, LANES)
    parts = lax.all_to_all(slots, ("space", "filt"), 0, 0, tiled=True)
    total = parts.astype(F32).sum(0)
    total = lax.all_to_all(
        jnp.broadcast_to(total[None], (spaces, per, 16, LANES)), "space", 0, 0, tiled=True
    ).reshape(spaces * per, 16, LANES)
    middle = total[:7].transpose(1, 0, 2).reshape(16, 896)[:, :864] / math.sqrt(middle_cells)
    middle = middle.reshape(16, 27, 32).transpose(1, 2, 0)
    stem = (total[7:9] + total[9:11]).reshape(32, LANES)[:, :108] / math.sqrt(stem_cells)
    stem = stem.T.reshape(27, 4, 32)
    return features, middle, stem


def solution(mesh):
    in_specs = (
        P(None, "space", "filt", None),
        P(),
        P(None, None, "filt"),
        P("filt", "space", None, None),
    )
    out_specs = (P("filt", "space", None, None), P(None, None, "filt"), P())
    return jax.shard_map(body, mesh=mesh, in_specs=in_specs, out_specs=out_specs, check_vma=False)
```

```python
import functools

import jax
import jax.numpy as jnp
import numpy as np
from jax import lax
from jax.experimental import pallas as pl
from jax.experimental.pallas import tpu as pltpu
from jax.sharding import PartitionSpec as P

F32 = jnp.float32
BF16 = jnp.bfloat16
LANES = 128
STEM_ROWS = 288


def nn(a, b):
    return lax.dot_general(a, b, (((1,), (0,)), ((), ())), preferred_element_type=F32)


def nt(a, b):
    return lax.dot_general(a, b, (((1,), (1,)), ((), ())), preferred_element_type=F32)


def place_table():
    table = np.zeros((2, LANES, STEM_ROWS), np.float32)
    for even_odd in range(2):
        for a in range(3):
            for b in range(3):
                for d in range(3):
                    q = 2 * even_odd + d - 1
                    shifted, phase = (1, 3) if q < 0 else (0, q)
                    for c in range(4):
                        column = 96 * a + 48 * shifted + 16 * b + 4 * phase + c
                        table[even_odd, 4 * (9 * a + 3 * b + d) + c, column] = 1.0
    return table


def rows_lanes(shape):
    return lax.broadcasted_iota(jnp.int32, shape, 0), lax.broadcasted_iota(jnp.int32, shape, 1)


def turn_matrix(count):
    row, column = rows_lanes((count * count, count * count))
    return ((row % count) * count + (row // count) == column).astype(F32).astype(BF16)


def regroup_kernel(volume, weight, cotangent, own, slab_x, packed):
    channels, planes, width, depth = volume.shape
    z, column = rows_lanes((depth, depth))
    select = (z == 4 * (column % LANES) + (column // LANES)).astype(F32).astype(BF16)
    turn = turn_matrix(16)
    picked = nn(volume[...].reshape(channels * planes * width, depth), select).astype(BF16)
    for x in range(planes):
        parts = []
        for phase in range(4):
            for c in range(channels):
                start = (c * planes + x) * width
                parts.append(picked[start : start + width, phase * LANES : (phase + 1) * LANES])
        plane = nn(turn, jnp.concatenate(parts, axis=0)).astype(BF16)
        own[x] = plane
        if x > 0:
            slab_x[x - 1] = plane

    blank = jnp.zeros((16, 32), BF16)
    taps = [weight[t] if t < 27 else blank for t in range(28)]
    turned = nn(turn, cotangent[...].reshape(256, LANES)).astype(BF16)
    for t in range(7):
        tile = jnp.concatenate(taps[4 * t : 4 * t + 4], axis=1)
        for f in range(packed.shape[0]):
            packed[f, t] = tile
    for f in range(packed.shape[0]):
        for j in range(4):
            row = 16 * (4 * f + j)
            packed[f, 7 + j] = turned[row : row + 16]


def border_kernel(slab_x, own, border):
    for x in range(3):
        border[x] = slab_x[x, -48:]
    for x in range(4):
        border[3 + x] = own[x, -48:]


def softplus_sigmoid(values):
    small = jnp.exp(-jnp.abs(values))
    inverse = 1.0 / (1.0 + small)
    soft = jnp.maximum(values, 0.0) + jnp.log(1.0 + small)
    return soft, jnp.where(values >= 0.0, inverse, small * inverse)


def roll_lanes(values, amount):
    lane = lax.broadcasted_iota(jnp.int32, values.shape, 1)
    edge = 0 if amount == 1 else LANES - 1
    rolled = pltpu.roll(values, amount % LANES, 1)
    return jnp.where(lane == edge, 0.0, rolled)


def slot_kinds(spaces):
    kinds = [("middle", u) for u in range(7)] + [("none", 0)]
    kinds += [("stem", u) for u in range(4)] + [("features", u) for u in range(4)]
    return kinds + [("none", 0)] * (-len(kinds) % spaces)


def slot_widths(spaces):
    kinds = [kind for kind, _ in slot_kinds(spaces)]
    widths = []
    for t in range(len(kinds) // spaces):
        mine = kinds[t * spaces : (t + 1) * spaces]
        widths.append(4 if "features" in mine else 2 if "stem" in mine else 1)
    return widths


def main_kernel(own, slab_x, border, stem_w, place, gathered, slots, cols, mid_w, mid_cols, slope, stem_back):
    blocks = gathered.shape[0]
    keep_x = jnp.where(lax.axis_index("space") > 0, 1.0, 0.0).astype(F32)
    keep_y = jnp.where(lax.axis_index("filt") > 0, 1.0, 0.0).astype(F32)

    for x in range(7):
        plane = jnp.concatenate([border[x], slab_x[x] if x < 3 else own[x - 3]], axis=0)
        shifted = roll_lanes(plane.astype(F32), 1).astype(BF16)
        for j in range(9):
            lanes = pl.ds(j * LANES, LANES)
            cols[x, 0:48, lanes] = plane[32 * j : 32 * j + 48]
            cols[x, 48:96, lanes] = shifted[32 * j : 32 * j + 48]

    weights = jnp.concatenate([nn(stem_w[...], place[0]), nn(stem_w[...], place[1])], axis=0).astype(BF16)
    for i in range(3):
        pre = nn(weights, cols[2 * i : 2 * i + 3].reshape(STEM_ROWS, 9 * LANES))
        soft, sig = softplus_sigmoid(pre)
        act = 0.3 * pre + 0.7 * soft
        lean = 0.3 + 0.7 * sig
        keep = jnp.where(lax.broadcasted_iota(jnp.int32, pre.shape, 1) < LANES, keep_y, 1.0)
        if i == 0:
            keep = keep * keep_x
        slope[i] = lean * keep
        act = act * keep
        for j in range(9):
            even = act[0:32, j * LANES : (j + 1) * LANES]
            odd = act[32:64, j * LANES : (j + 1) * LANES]
            for d, part in ((0, roll_lanes(odd, 1)), (1, even), (2, odd)):
                part = part.astype(BF16)
                for b in range(3):
                    if (j - b) % 2 == 0 and 0 <= (j - b) // 2 < 4:
                        row = 32 * (9 * i + 3 * b + d)
                        mid_cols[row : row + 32, pl.ds((j - b) // 2 * LANES, LANES)] = part

    for f in range(blocks):
        for t in range(7):
            mid_w[16 * f : 16 * f + 16, t * LANES : (t + 1) * LANES] = gathered[f, t]
    cotangent = jnp.concatenate(
        [
            jnp.concatenate([gathered[f, 7 + j] for j in range(4)], axis=1)
            for f in range(blocks)
        ],
        axis=0,
    )
    pre = nn(mid_w[:, 0:864], mid_cols[...])
    soft, sig = softplus_sigmoid(pre)
    features = (0.3 * pre + 0.7 * soft).astype(BF16)
    delta = cotangent.astype(F32) * (0.3 + 0.7 * sig)
    delta_low = delta.astype(BF16)
    mid_grad = nt(delta_low, mid_cols[...])

    turned = jnp.concatenate(
        [mid_w[:, t * LANES : (t + 1) * LANES].astype(F32).T for t in range(7)], axis=0
    ).astype(BF16)
    zero = jnp.zeros((32, blocks * 16), BF16)

    def block(a, b, d):
        row = 32 * (9 * a + 3 * b + d)
        return turned[row : row + 32]

    def wide(a, b):
        even = jnp.concatenate([block(a, b, 1), zero], axis=1)
        odd = jnp.concatenate([block(a, b, 2), block(a, b, 0)], axis=1)
        return jnp.concatenate([even, odd], axis=0)

    both = jnp.concatenate(
        [delta_low]
        + [
            jnp.concatenate(
                [roll_lanes(delta[:, j * LANES : (j + 1) * LANES], -1) for j in range(4)], axis=1
            ).astype(BF16)
        ],
        axis=0,
    )
    nothing = jnp.zeros((2 * blocks * 16, LANES), BF16)
    pair = jnp.concatenate(
        [jnp.concatenate([both, nothing], axis=1), jnp.concatenate([nothing, both], axis=1)], axis=0
    )
    stem_grad = jnp.zeros((64, STEM_ROWS), F32)
    for i in range(3):
        odd_back = nn(wide(i, 1), both)
        even_back = nn(jnp.concatenate([wide(i, 0), wide(i, 2)], axis=1), pair)
        for j in range(9):
            source = even_back if j % 2 == 0 else odd_back
            part = source[:, (j // 2) * LANES : (j // 2 + 1) * LANES]
            lanes = pl.ds(j * LANES, LANES)
            stem_back[i, :, lanes] = (part * slope[i, :, lanes]).astype(BF16)
        stem_grad += nt(stem_back[i], cols[2 * i : 2 * i + 3].reshape(STEM_ROWS, 9 * LANES))
    high = stem_grad.astype(BF16)
    low = (stem_grad - high.astype(F32)).astype(BF16)
    taken = sum(
        nt(part[32 * e : 32 * e + 32], place[e]) for part in (high, low) for e in range(2)
    )
    high = taken.astype(BF16)
    low = (taken - high.astype(F32)).astype(BF16)

    mid_low = mid_grad.astype(BF16)
    mid_low = jnp.concatenate([mid_low, jnp.zeros((blocks * 16, 32), BF16)], axis=1)
    blank = jnp.zeros((16, LANES), BF16)
    spaces = slots.shape[0]
    for f in range(blocks):
        rows = slice(16 * f, 16 * f + 16)
        for u, (kind, which) in enumerate(slot_kinds(spaces)):
            lanes = slice(which * LANES, (which + 1) * LANES)
            if kind == "middle":
                value = mid_low[rows, lanes]
            elif kind == "stem":
                value = (high, low)[which // 2][16 * (which % 2) : 16 * (which % 2) + 16]
            elif kind == "features":
                value = features[rows, lanes]
            else:
                value = blank
            slots[u % spaces, f, u // spaces] = value


def sum_kernel(parts, chunks):
    spaces = chunks.shape[0]
    filts = parts.shape[0] // spaces
    me = lax.axis_index("space")
    kinds = [kind for kind, _ in slot_kinds(spaces)]
    base = 0
    for t, width in enumerate(slot_widths(spaces)):
        total = jnp.sum(parts[:, t].astype(F32), axis=0)
        high = total.astype(BF16)
        tiles = [high]
        if width > 1:
            tiles.append((total - high.astype(F32)).astype(BF16))
        first = kinds.index("features") - t * spaces
        forward = jnp.logical_and(me >= first, me < first + 4)
        for s in range(spaces):
            for k in range(width):
                if width < 4:
                    chunks[s, base + k] = tiles[k]
                    continue
                here = parts[s * filts + k, t].astype(F32)
                other = tiles[k].astype(F32) if k < 2 else jnp.zeros_like(here)
                chunks[s, base + k] = jnp.where(forward, here, other).astype(BF16)
        base += width


def unpack_kernel(middle_scale, stem_scale, chunks, features, middle, stem):
    spaces = chunks.shape[0]
    widths = slot_widths(spaces)
    found = {}
    for u, (kind, which) in enumerate(slot_kinds(spaces)):
        found[kind, which] = (u % spaces, sum(widths[: u // spaces]))
    for t in range(27):
        s, base = found["middle", t // 4]
        start = 32 * (t % 4)
        middle[t] = chunks[s, base][:, start : start + 32].astype(F32) * middle_scale
    total = []
    for half in range(2):
        tiles = [found["stem", half], found["stem", 2 + half]]
        total.append(sum(chunks[s, base + k].astype(F32) for s, base in tiles for k in range(2)))
    total = jnp.concatenate(total, axis=0).T * stem_scale
    for t in range(27):
        stem[t] = total[4 * t : 4 * t + 4]
    rows = []
    for y in range(16):
        s, base = found["features", y % 4]
        rows.append(chunks[s, base + y // 4])
    turned = nn(turn_matrix(16), jnp.concatenate(rows, axis=0)).astype(BF16)
    features[...] = turned.reshape(16, 16, LANES)


def whole(count):
    return [pl.BlockSpec(memory_space=pltpu.VMEM)] * count


def body(volume, stem_weight, middle_weight, cotangent):
    spaces, filts = lax.axis_size("space"), lax.axis_size("filt")
    channels, planes, width, depth = volume.shape
    stem_cells = (planes // 2) * spaces * (width // 2) * filts * (depth // 2)
    middle_cells = stem_cells // 8
    limit = pltpu.CompilerParams(vmem_limit_bytes=48 * 1024 * 1024)

    own, slab_x, packed = pl.pallas_call(
        regroup_kernel,
        out_shape=[
            jax.ShapeDtypeStruct((planes, 16 * width, LANES), BF16),
            jax.ShapeDtypeStruct((planes - 1, 16 * width, LANES), BF16),
            jax.ShapeDtypeStruct((filts, 11, 16, LANES), BF16),
        ],
        in_specs=whole(3),
        out_specs=whole(3),
        compiler_params=limit,
        name="regroup",
    )(volume, middle_weight.transpose(0, 2, 1), cotangent.reshape(16, 16, LANES))
    slab_x = lax.ppermute(slab_x, "space", [(s - 1, s) for s in range(1, spaces)])
    gathered = lax.all_to_all(packed, "filt", 0, 0, tiled=True)
    border = pl.pallas_call(
        border_kernel,
        out_shape=jax.ShapeDtypeStruct((7, 48, LANES), BF16),
        in_specs=whole(2),
        out_specs=whole(1)[0],
        compiler_params=limit,
        name="border",
    )(slab_x, own)
    border = lax.ppermute(border, "filt", [(f - 1, f) for f in range(1, filts)])

    stem_w = jnp.pad(stem_weight.reshape(108, 32).T, ((0, 0), (0, 20)))
    place = jnp.asarray(place_table(), BF16)
    widths = slot_widths(spaces)
    slots = pl.pallas_call(
        main_kernel,
        out_shape=jax.ShapeDtypeStruct((spaces, filts, len(widths), 16, LANES), BF16),
        in_specs=whole(6),
        out_specs=whole(1)[0],
        scratch_shapes=[
            pltpu.VMEM((7, 96, 9 * LANES), BF16),
            pltpu.VMEM((64, 896), BF16),
            pltpu.VMEM((864, 512), BF16),
            pltpu.VMEM((3, 64, 9 * LANES), F32),
            pltpu.VMEM((3, 64, 9 * LANES), BF16),
        ],
        compiler_params=limit,
        name="sections",
    )(own, slab_x, border, stem_w, place, gathered)

    slots = slots.reshape(spaces * filts, len(widths), 16, LANES)
    parts = lax.all_to_all(slots, ("space", "filt"), 0, 0, tiled=True)
    chunks = pl.pallas_call(
        sum_kernel,
        out_shape=jax.ShapeDtypeStruct((spaces, sum(widths), 16, LANES), BF16),
        in_specs=whole(1),
        out_specs=whole(1)[0],
        compiler_params=limit,
        name="sums",
    )(parts)
    chunks = lax.all_to_all(chunks, "space", 0, 0, tiled=True)
    features, middle, stem = pl.pallas_call(
        functools.partial(unpack_kernel, middle_cells**-0.5, stem_cells**-0.5),
        out_shape=[
            jax.ShapeDtypeStruct((16, 16, LANES), BF16),
            jax.ShapeDtypeStruct((27, 16, 32), F32),
            jax.ShapeDtypeStruct((27, 4, 32), F32),
        ],
        in_specs=whole(1),
        out_specs=whole(3),
        compiler_params=limit,
        name="unpack",
    )(chunks)
    return features.reshape(16, 1, 16, LANES), middle.transpose(0, 2, 1), stem


def solution(mesh):
    in_specs = (
        P(None, "space", "filt", None),
        P(),
        P(None, None, "filt"),
        P("filt", "space", None, None),
    )
    out_specs = (P("filt", "space", None, None), P(None, None, "filt"), P())
    return jax.shard_map(body, mesh=mesh, in_specs=in_specs, out_specs=out_specs, check_vma=False)
```

```python
import functools

import jax
import jax.numpy as jnp
import numpy as np
from jax import lax
from jax.experimental import pallas as pl
from jax.experimental.pallas import tpu as pltpu
from jax.sharding import PartitionSpec as P

F32 = jnp.float32
BF16 = jnp.bfloat16
LANES = 128
STEM_ROWS = 144


def nn(a, b):
    return lax.dot_general(a, b, (((1,), (0,)), ((), ())), preferred_element_type=F32)


def nt(a, b):
    return lax.dot_general(a, b, (((1,), (1,)), ((), ())), preferred_element_type=F32)


def place_table():
    table = np.zeros((3, LANES, STEM_ROWS), np.float32)
    for even_odd in range(2):
        for a in range(3):
            for b in range(3):
                for d in range(3):
                    q = 2 * even_odd + d - 1
                    group, phase = (2, 3) if q < 0 else (even_odd, q)
                    for c in range(4):
                        column = 48 * a + 16 * b + 4 * phase + c
                        table[group, 4 * (9 * a + 3 * b + d) + c, column] = 1.0
    return table


def rows_lanes(shape):
    return lax.broadcasted_iota(jnp.int32, shape, 0), lax.broadcasted_iota(jnp.int32, shape, 1)


def turn_matrix():
    row, column = rows_lanes((256, 256))
    source = lax.shift_left(row & 15, 4) + lax.shift_right_logical(row, 4)
    return (source == column).astype(F32).astype(BF16)


def regroup_kernel(volume_in, weight_in, cotangent_in, own, slab_x, packed, volume, weight, cotangent, sems):
    copies = [
        pltpu.make_async_copy(source, target, sems.at[k])
        for k, (source, target) in enumerate(
            [(volume_in, volume), (weight_in, weight), (cotangent_in, cotangent)]
        )
    ]
    for copy in copies:
        copy.start()
    channels, planes, width, depth = volume.shape
    z, column = rows_lanes((depth, depth))
    source = lax.shift_left(column & (LANES - 1), 2) + lax.shift_right_logical(column, 7)
    select = (z == source).astype(F32).astype(BF16)
    turn = turn_matrix()
    copies[0].wait()
    picked = nn(volume[...].reshape(channels * planes * width, depth), select).astype(BF16)
    grouped = []
    for x in range(planes):
        parts = []
        for phase in range(4):
            for c in range(channels):
                start = (c * planes + x) * width
                parts.append(picked[start : start + width, phase * LANES : (phase + 1) * LANES])
        grouped.append(jnp.concatenate(parts, axis=0))
    copies[1].wait()
    copies[2].wait()
    grouped.append(cotangent[...].reshape(256, LANES))
    turned = nn(turn, jnp.concatenate(grouped, axis=1)).astype(BF16)
    for x in range(planes):
        plane = turned[:, x * LANES : (x + 1) * LANES]
        own[x] = plane
        if x > 0:
            slab_x[x - 1] = plane

    blank = jnp.zeros((16, 32), BF16)
    taps = [weight[t] if t < 27 else blank for t in range(28)]
    for t in range(7):
        tile = jnp.concatenate(taps[4 * t : 4 * t + 4], axis=1)
        for f in range(packed.shape[0]):
            packed[f, t] = tile
    for f in range(packed.shape[0]):
        for j in range(4):
            row = 16 * (4 * f + j)
            packed[f, 7 + j] = turned[row : row + 16, planes * LANES :]


def border_kernel(slab_x, own, border):
    for x in range(3):
        border[x] = slab_x[x, -48:]
    for x in range(4):
        border[3 + x] = own[x, -48:]


def softplus_sigmoid(values):
    small = jnp.exp(-jnp.abs(values))
    inverse = 1.0 / (1.0 + small)
    soft = jnp.maximum(values, 0.0) + jnp.log(1.0 + small)
    return soft, jnp.where(values >= 0.0, inverse, small * inverse)


def roll_blocks(values, amount):
    blocks = []
    for start in range(0, values.shape[1], LANES):
        block = values[:, start : start + LANES]
        lane = lax.broadcasted_iota(jnp.int32, block.shape, 1)
        edge = 0 if amount == 1 else LANES - 1
        blocks.append(jnp.where(lane == edge, 0.0, pltpu.roll(block, amount % LANES, 1)))
    return jnp.concatenate(blocks, axis=1)


def slot_kinds(spaces):
    kinds = [("middle", u) for u in range(7)] + [("none", 0)]
    kinds += [("stem", u) for u in range(4)] + [("features", u) for u in range(4)]
    return kinds + [("none", 0)] * (-len(kinds) % spaces)


def slot_widths(spaces):
    kinds = [kind for kind, _ in slot_kinds(spaces)]
    widths = []
    for t in range(len(kinds) // spaces):
        mine = kinds[t * spaces : (t + 1) * spaces]
        widths.append(4 if "features" in mine else 2 if "stem" in mine else 1)
    return widths


def main_kernel(own, slab_x, border, stem_w, place, gathered, slots, cols, mid_w, mid_cols, slope, stem_back):
    blocks = gathered.shape[0]
    keep_x = jnp.where(lax.axis_index("space") > 0, 1.0, 0.0).astype(F32)
    keep_y = jnp.where(lax.axis_index("filt") > 0, 1.0, 0.0).astype(F32)

    for x in range(7):
        plane = jnp.concatenate([border[x], slab_x[x] if x < 3 else own[x - 3]], axis=0)
        for j in range(9):
            cols[x, :, pl.ds(j * LANES, LANES)] = plane[32 * j : 32 * j + 48]

    weights = jnp.concatenate([nn(stem_w[...], place[g]) for g in range(3)], axis=0).astype(BF16)
    for i in range(3):
        pre = nn(weights, cols[2 * i : 2 * i + 3].reshape(STEM_ROWS, 9 * LANES))
        pre = jnp.concatenate([pre[0:32] + roll_blocks(pre[64:96], 1), pre[32:64]], axis=0)
        soft, sig = softplus_sigmoid(pre)
        act = 0.3 * pre + 0.7 * soft
        lean = 0.3 + 0.7 * sig
        keep = jnp.where(lax.broadcasted_iota(jnp.int32, pre.shape, 1) < LANES, keep_y, 1.0)
        if i == 0:
            keep = keep * keep_x
        slope[i] = lean * keep
        act = act * keep
        for j in range(9):
            even = act[0:32, j * LANES : (j + 1) * LANES]
            odd = act[32:64, j * LANES : (j + 1) * LANES]
            for d, part in ((0, roll_blocks(odd, 1)), (1, even), (2, odd)):
                part = part.astype(BF16)
                for b in range(3):
                    if (j - b) % 2 == 0 and 0 <= (j - b) // 2 < 4:
                        row = 32 * (9 * i + 3 * b + d)
                        mid_cols[row : row + 32, pl.ds((j - b) // 2 * LANES, LANES)] = part

    for f in range(blocks):
        for t in range(7):
            mid_w[16 * f : 16 * f + 16, t * LANES : (t + 1) * LANES] = gathered[f, t]
    cotangent = jnp.concatenate(
        [
            jnp.concatenate([gathered[f, 7 + j] for j in range(4)], axis=1)
            for f in range(blocks)
        ],
        axis=0,
    )
    pre = nn(mid_w[:, 0:864], mid_cols[...])
    soft, sig = softplus_sigmoid(pre)
    features = (0.3 * pre + 0.7 * soft).astype(BF16)
    delta = cotangent.astype(F32) * (0.3 + 0.7 * sig)
    delta_low = delta.astype(BF16)
    mid_grad = nt(delta_low, mid_cols[...])

    turned = jnp.concatenate(
        [mid_w[:, t * LANES : (t + 1) * LANES].astype(F32).T for t in range(7)], axis=0
    ).astype(BF16)
    zero = jnp.zeros((32, blocks * 16), BF16)

    def block(a, b, d):
        row = 32 * (9 * a + 3 * b + d)
        return turned[row : row + 32]

    def wide(a, b):
        even = jnp.concatenate([block(a, b, 1), zero], axis=1)
        odd = jnp.concatenate([block(a, b, 2), block(a, b, 0)], axis=1)
        return jnp.concatenate([even, odd], axis=0)

    both = jnp.concatenate([delta_low, roll_blocks(delta, -1).astype(BF16)], axis=0)
    nothing = jnp.zeros((2 * blocks * 16, LANES), BF16)
    pair = jnp.concatenate(
        [jnp.concatenate([both, nothing], axis=1), jnp.concatenate([nothing, both], axis=1)], axis=0
    )
    odd_back = nn(jnp.concatenate([wide(i, 1) for i in range(3)], axis=0), both)
    even_back = nn(
        jnp.concatenate([jnp.concatenate([wide(i, 0), wide(i, 2)], axis=1) for i in range(3)], axis=0), pair
    )
    stem_grad = jnp.zeros((96, STEM_ROWS), F32)
    for i in range(3):
        for j in range(9):
            source = even_back if j % 2 == 0 else odd_back
            part = source[64 * i : 64 * i + 64, (j // 2) * LANES : (j // 2 + 1) * LANES]
            lanes = pl.ds(j * LANES, LANES)
            part = part * slope[i, :, lanes]
            stem_back[i, 0:64, lanes] = part.astype(BF16)
            stem_back[i, 64:96, lanes] = roll_blocks(part[0:32], -1).astype(BF16)
        stem_grad += nt(stem_back[i], cols[2 * i : 2 * i + 3].reshape(STEM_ROWS, 9 * LANES))
    high = stem_grad.astype(BF16)
    low = (stem_grad - high.astype(F32)).astype(BF16)
    taken = sum(
        nt(part[32 * g : 32 * g + 32], place[g]) for part in (high, low) for g in range(3)
    )
    high = taken.astype(BF16)
    low = (taken - high.astype(F32)).astype(BF16)

    mid_low = mid_grad.astype(BF16)
    mid_low = jnp.concatenate([mid_low, jnp.zeros((blocks * 16, 32), BF16)], axis=1)
    blank = jnp.zeros((16, LANES), BF16)
    spaces = slots.shape[0]
    for f in range(blocks):
        rows = slice(16 * f, 16 * f + 16)
        for u, (kind, which) in enumerate(slot_kinds(spaces)):
            lanes = slice(which * LANES, (which + 1) * LANES)
            if kind == "middle":
                value = mid_low[rows, lanes]
            elif kind == "stem":
                value = (high, low)[which // 2][16 * (which % 2) : 16 * (which % 2) + 16]
            elif kind == "features":
                value = features[rows, lanes]
            else:
                value = blank
            slots[u % spaces, f, u // spaces] = value


def sum_kernel(parts, chunks):
    spaces = chunks.shape[0]
    filts = parts.shape[0] // spaces
    me = lax.axis_index("space")
    kinds = [kind for kind, _ in slot_kinds(spaces)]
    base = 0
    for t, width in enumerate(slot_widths(spaces)):
        total = jnp.sum(parts[:, t].astype(F32), axis=0)
        high = total.astype(BF16)
        tiles = [high]
        if width > 1:
            tiles.append((total - high.astype(F32)).astype(BF16))
        first = kinds.index("features") - t * spaces
        forward = jnp.logical_and(me >= first, me < first + 4)
        for s in range(spaces):
            for k in range(width):
                if width < 4:
                    chunks[s, base + k] = tiles[k]
                    continue
                here = parts[s * filts + k, t].astype(F32)
                other = tiles[k].astype(F32) if k < 2 else jnp.zeros_like(here)
                chunks[s, base + k] = jnp.where(forward, here, other).astype(BF16)
        base += width


def unpack_kernel(middle_scale, stem_scale, chunks, features, middle, stem):
    spaces = chunks.shape[0]
    widths = slot_widths(spaces)
    found = {}
    for u, (kind, which) in enumerate(slot_kinds(spaces)):
        found[kind, which] = (u % spaces, sum(widths[: u // spaces]))
    for t in range(27):
        s, base = found["middle", t // 4]
        start = 32 * (t % 4)
        middle[t] = chunks[s, base][:, start : start + 32].astype(F32) * middle_scale
    total = []
    for half in range(2):
        tiles = [found["stem", half], found["stem", 2 + half]]
        total.append(sum(chunks[s, base + k].astype(F32) for s, base in tiles for k in range(2)))
    total = jnp.concatenate(total, axis=0).T * stem_scale
    for t in range(27):
        stem[t] = total[4 * t : 4 * t + 4]
    rows = []
    for y in range(16):
        s, base = found["features", y % 4]
        rows.append(chunks[s, base + y // 4])
    turned = nn(turn_matrix(), jnp.concatenate(rows, axis=0)).astype(BF16)
    features[...] = turned.reshape(16, 16, LANES)


def whole(count):
    return [pl.BlockSpec(memory_space=pltpu.VMEM)] * count


def body(volume, stem_weight, middle_weight, cotangent):
    spaces, filts = lax.axis_size("space"), lax.axis_size("filt")
    channels, planes, width, depth = volume.shape
    stem_cells = (planes // 2) * spaces * (width // 2) * filts * (depth // 2)
    middle_cells = stem_cells // 8
    limit = pltpu.CompilerParams(vmem_limit_bytes=48 * 1024 * 1024)

    own, slab_x, packed = pl.pallas_call(
        regroup_kernel,
        out_shape=[
            jax.ShapeDtypeStruct((planes, 16 * width, LANES), BF16),
            jax.ShapeDtypeStruct((planes - 1, 16 * width, LANES), BF16),
            jax.ShapeDtypeStruct((filts, 11, 16, LANES), BF16),
        ],
        in_specs=[pl.BlockSpec(memory_space=pl.ANY)] * 3,
        out_specs=whole(3),
        scratch_shapes=[
            pltpu.VMEM(volume.shape, BF16),
            pltpu.VMEM((27, 16, 32), BF16),
            pltpu.VMEM((16, 16, LANES), BF16),
            pltpu.SemaphoreType.DMA((3,)),
        ],
        compiler_params=limit,
        name="regroup",
    )(volume, middle_weight.transpose(0, 2, 1), cotangent.reshape(16, 16, LANES))
    slab_x = lax.ppermute(slab_x, "space", [(s - 1, s) for s in range(1, spaces)])
    gathered = lax.all_to_all(packed, "filt", 0, 0, tiled=True)
    border = pl.pallas_call(
        border_kernel,
        out_shape=jax.ShapeDtypeStruct((7, 48, LANES), BF16),
        in_specs=whole(2),
        out_specs=whole(1)[0],
        compiler_params=limit,
        name="border",
    )(slab_x, own)
    border = lax.ppermute(border, "filt", [(f - 1, f) for f in range(1, filts)])

    stem_w = jnp.pad(stem_weight.reshape(108, 32).T, ((0, 0), (0, 20)))
    place = jnp.asarray(place_table(), BF16)
    widths = slot_widths(spaces)
    slots = pl.pallas_call(
        main_kernel,
        out_shape=jax.ShapeDtypeStruct((spaces, filts, len(widths), 16, LANES), BF16),
        in_specs=whole(6),
        out_specs=whole(1)[0],
        scratch_shapes=[
            pltpu.VMEM((7, 48, 9 * LANES), BF16),
            pltpu.VMEM((64, 896), BF16),
            pltpu.VMEM((864, 512), BF16),
            pltpu.VMEM((3, 64, 9 * LANES), F32),
            pltpu.VMEM((3, 96, 9 * LANES), BF16),
        ],
        compiler_params=limit,
        name="sections",
    )(own, slab_x, border, stem_w, place, gathered)

    slots = slots.reshape(spaces * filts, len(widths), 16, LANES)
    parts = lax.all_to_all(slots, ("space", "filt"), 0, 0, tiled=True)
    chunks = pl.pallas_call(
        sum_kernel,
        out_shape=jax.ShapeDtypeStruct((spaces, sum(widths), 16, LANES), BF16),
        in_specs=whole(1),
        out_specs=whole(1)[0],
        compiler_params=limit,
        name="sums",
    )(parts)
    chunks = lax.all_to_all(chunks, "space", 0, 0, tiled=True)
    features, middle, stem = pl.pallas_call(
        functools.partial(unpack_kernel, middle_cells**-0.5, stem_cells**-0.5),
        out_shape=[
            jax.ShapeDtypeStruct((16, 16, LANES), BF16),
            jax.ShapeDtypeStruct((27, 16, 32), F32),
            jax.ShapeDtypeStruct((27, 4, 32), F32),
        ],
        in_specs=whole(1),
        out_specs=whole(3),
        compiler_params=limit,
        name="unpack",
    )(chunks)
    return features.reshape(16, 1, 16, LANES), middle.transpose(0, 2, 1), stem


def solution(mesh):
    in_specs = (
        P(None, "space", "filt", None),
        P(),
        P(None, None, "filt"),
        P("filt", "space", None, None),
    )
    out_specs = (P("filt", "space", None, None), P(None, None, "filt"), P())
    return jax.shard_map(body, mesh=mesh, in_specs=in_specs, out_specs=out_specs, check_vma=False)
```

```python
import functools

import jax
import jax.numpy as jnp
import numpy as np
from jax import lax
from jax.experimental import pallas as pl
from jax.experimental.pallas import tpu as pltpu
from jax.sharding import PartitionSpec as P

F32 = jnp.float32
BF16 = jnp.bfloat16
LANES = 128
STEM_ROWS = 144


def nn(a, b):
    return lax.dot_general(a, b, (((1,), (0,)), ((), ())), preferred_element_type=F32)


def nt(a, b):
    return lax.dot_general(a, b, (((1,), (1,)), ((), ())), preferred_element_type=F32)


def place_table():
    table = np.zeros((3, LANES, STEM_ROWS), np.float32)
    for even_odd in range(2):
        for a in range(3):
            for b in range(3):
                for d in range(3):
                    q = 2 * even_odd + d - 1
                    group, phase = (2, 3) if q < 0 else (even_odd, q)
                    for c in range(4):
                        column = 48 * a + 16 * b + 4 * phase + c
                        table[group, 4 * (9 * a + 3 * b + d) + c, column] = 1.0
    return table


def rows_lanes(shape):
    return lax.broadcasted_iota(jnp.int32, shape, 0), lax.broadcasted_iota(jnp.int32, shape, 1)


def turn_matrix():
    row, column = rows_lanes((256, 256))
    source = lax.shift_left(row & 15, 4) + lax.shift_right_logical(row, 4)
    return (source == column).astype(F32).astype(BF16)


def regroup_kernel(volume_in, weight_in, cotangent_in, own, slab_x, packed, volume, weight, cotangent, sems):
    copies = [
        pltpu.make_async_copy(source, target, sems.at[k])
        for k, (source, target) in enumerate(
            [(volume_in, volume), (weight_in, weight), (cotangent_in, cotangent)]
        )
    ]
    for copy in copies:
        copy.start()
    channels, planes, width, depth = volume.shape
    z, column = rows_lanes((depth, depth))
    source = lax.shift_left(column & (LANES - 1), 2) + lax.shift_right_logical(column, 7)
    select = (z == source).astype(F32).astype(BF16)
    turn = turn_matrix()
    copies[0].wait()
    picked = nn(volume[...].reshape(channels * planes * width, depth), select).astype(BF16)
    grouped = []
    for x in range(planes):
        parts = []
        for phase in range(4):
            for c in range(channels):
                start = (c * planes + x) * width
                parts.append(picked[start : start + width, phase * LANES : (phase + 1) * LANES])
        grouped.append(jnp.concatenate(parts, axis=0))
    copies[1].wait()
    copies[2].wait()
    grouped.append(cotangent[...].reshape(256, LANES))
    turned = nn(turn, jnp.concatenate(grouped, axis=1)).astype(BF16)
    for x in range(planes):
        plane = turned[:, x * LANES : (x + 1) * LANES]
        own[x] = plane
        if x > 0:
            slab_x[x - 1] = plane

    blank = jnp.zeros((16, 32), BF16)
    taps = [weight[t] if t < 27 else blank for t in range(28)]
    for t in range(7):
        tile = jnp.concatenate(taps[4 * t : 4 * t + 4], axis=1)
        for f in range(packed.shape[0]):
            packed[f, t] = tile
    for f in range(packed.shape[0]):
        for j in range(4):
            row = 16 * (4 * f + j)
            packed[f, 7 + j] = turned[row : row + 16, planes * LANES :]


def border_kernel(slab_x, own, border):
    for x in range(3):
        border[x] = slab_x[x, -48:]
    for x in range(4):
        border[3 + x] = own[x, -48:]


def softplus_sigmoid(values):
    small = jnp.exp(-jnp.abs(values))
    inverse = 1.0 / (1.0 + small)
    soft = jnp.maximum(values, 0.0) + jnp.log(1.0 + small)
    return soft, jnp.where(values >= 0.0, inverse, small * inverse)


def roll_blocks(values, amount):
    blocks = []
    for start in range(0, values.shape[1], LANES):
        block = values[:, start : start + LANES]
        lane = lax.broadcasted_iota(jnp.int32, block.shape, 1)
        edge = 0 if amount == 1 else LANES - 1
        blocks.append(jnp.where(lane == edge, 0.0, pltpu.roll(block, amount % LANES, 1)))
    return jnp.concatenate(blocks, axis=1)


def main_kernel(own, slab_x, border, stem_w, place, gathered, parts, cols, mid_w, mid_cols, slope, stem_back):
    blocks = gathered.shape[0]
    keep_x = jnp.where(lax.axis_index("space") > 0, 1.0, 0.0).astype(F32)
    keep_y = jnp.where(lax.axis_index("filt") > 0, 1.0, 0.0).astype(F32)

    for x in range(7):
        plane = jnp.concatenate([border[x], slab_x[x] if x < 3 else own[x - 3]], axis=0)
        for j in range(9):
            cols[x, :, pl.ds(j * LANES, LANES)] = plane[32 * j : 32 * j + 48]

    weights = jnp.concatenate([nn(stem_w[...], place[g]) for g in range(3)], axis=0).astype(BF16)
    for i in range(3):
        pre = nn(weights, cols[2 * i : 2 * i + 3].reshape(STEM_ROWS, 9 * LANES))
        pre = jnp.concatenate([pre[0:32] + roll_blocks(pre[64:96], 1), pre[32:64]], axis=0)
        soft, sig = softplus_sigmoid(pre)
        act = 0.3 * pre + 0.7 * soft
        lean = 0.3 + 0.7 * sig
        keep = jnp.where(lax.broadcasted_iota(jnp.int32, pre.shape, 1) < LANES, keep_y, 1.0)
        if i == 0:
            keep = keep * keep_x
        slope[i] = lean * keep
        act = act * keep
        for j in range(9):
            even = act[0:32, j * LANES : (j + 1) * LANES]
            odd = act[32:64, j * LANES : (j + 1) * LANES]
            for d, part in ((0, roll_blocks(odd, 1)), (1, even), (2, odd)):
                part = part.astype(BF16)
                for b in range(3):
                    if (j - b) % 2 == 0 and 0 <= (j - b) // 2 < 4:
                        row = 32 * (9 * i + 3 * b + d)
                        mid_cols[row : row + 32, pl.ds((j - b) // 2 * LANES, LANES)] = part

    for f in range(blocks):
        for t in range(7):
            mid_w[16 * f : 16 * f + 16, t * LANES : (t + 1) * LANES] = gathered[f, t]
    cotangent = jnp.concatenate(
        [
            jnp.concatenate([gathered[f, 7 + j] for j in range(4)], axis=1)
            for f in range(blocks)
        ],
        axis=0,
    )
    pre = nn(mid_w[:, 0:864], mid_cols[...])
    soft, sig = softplus_sigmoid(pre)
    features = (0.3 * pre + 0.7 * soft).astype(BF16)
    delta = cotangent.astype(F32) * (0.3 + 0.7 * sig)
    delta_low = delta.astype(BF16)
    mid_grad = nt(delta_low, mid_cols[...])

    turned = jnp.concatenate(
        [mid_w[:, t * LANES : (t + 1) * LANES].astype(F32).T for t in range(7)], axis=0
    ).astype(BF16)
    zero = jnp.zeros((32, blocks * 16), BF16)

    def block(a, b, d):
        row = 32 * (9 * a + 3 * b + d)
        return turned[row : row + 32]

    def wide(a, b):
        even = jnp.concatenate([block(a, b, 1), zero], axis=1)
        odd = jnp.concatenate([block(a, b, 2), block(a, b, 0)], axis=1)
        return jnp.concatenate([even, odd], axis=0)

    both = jnp.concatenate([delta_low, roll_blocks(delta, -1).astype(BF16)], axis=0)
    nothing = jnp.zeros((2 * blocks * 16, LANES), BF16)
    pair = jnp.concatenate(
        [jnp.concatenate([both, nothing], axis=1), jnp.concatenate([nothing, both], axis=1)], axis=0
    )
    odd_back = nn(jnp.concatenate([wide(i, 1) for i in range(3)], axis=0), both)
    even_back = nn(
        jnp.concatenate([jnp.concatenate([wide(i, 0), wide(i, 2)], axis=1) for i in range(3)], axis=0), pair
    )
    stem_grad = jnp.zeros((96, STEM_ROWS), F32)
    for i in range(3):
        for j in range(9):
            source = even_back if j % 2 == 0 else odd_back
            part = source[64 * i : 64 * i + 64, (j // 2) * LANES : (j // 2 + 1) * LANES]
            lanes = pl.ds(j * LANES, LANES)
            part = part * slope[i, :, lanes]
            stem_back[i, 0:64, lanes] = part.astype(BF16)
            stem_back[i, 64:96, lanes] = roll_blocks(part[0:32], -1).astype(BF16)
        stem_grad += nt(stem_back[i], cols[2 * i : 2 * i + 3].reshape(STEM_ROWS, 9 * LANES))
    high = stem_grad.astype(BF16)
    low = (stem_grad - high.astype(F32)).astype(BF16)
    stem = sum(
        nt(part[32 * g : 32 * g + 32], place[g]) for part in (high, low) for g in range(3)
    ).astype(BF16)

    middle = mid_grad.astype(BF16)
    middle = jnp.concatenate([middle, jnp.zeros((blocks * 16, 32), BF16)], axis=1)
    for f in range(blocks):
        rows = slice(16 * f, 16 * f + 16)
        for t in range(7):
            parts[f, t] = middle[rows, t * LANES : (t + 1) * LANES]
        for half in range(2):
            parts[f, 7 + half] = stem[16 * half : 16 * half + 16]
        for j in range(4):
            parts[f, 9 + j] = features[rows, j * LANES : (j + 1) * LANES]


def sum_kernel(parts, sums, features):
    total = jnp.sum(parts[:, 0:9].astype(F32), axis=0).astype(BF16)
    for s in range(sums.shape[0]):
        sums[s] = total
    rows = [parts[f, 9 + j] for f in range(parts.shape[0]) for j in range(4)]
    features[...] = nn(turn_matrix(), jnp.concatenate(rows, axis=0)).astype(BF16).reshape(16, 16, LANES)


def unpack_kernel(middle_scale, stem_scale, sums, middle, stem):
    total = jnp.sum(sums[...].astype(F32), axis=0)
    for t in range(27):
        start = 32 * (t % 4)
        middle[t] = total[t // 4, :, start : start + 32] * middle_scale
    turned = jnp.concatenate([total[7], total[8]], axis=0).T * stem_scale
    for t in range(27):
        stem[t] = turned[4 * t : 4 * t + 4]


def whole(count):
    return [pl.BlockSpec(memory_space=pltpu.VMEM)] * count


def body(volume, stem_weight, middle_weight, cotangent):
    spaces, filts = lax.axis_size("space"), lax.axis_size("filt")
    channels, planes, width, depth = volume.shape
    stem_cells = (planes // 2) * spaces * (width // 2) * filts * (depth // 2)
    middle_cells = stem_cells // 8
    limit = pltpu.CompilerParams(vmem_limit_bytes=48 * 1024 * 1024)

    raw = (volume, middle_weight.transpose(0, 2, 1), cotangent.reshape(16, 16, LANES))
    own, slab_x, packed = pl.pallas_call(
        regroup_kernel,
        out_shape=[
            jax.ShapeDtypeStruct((planes, 16 * width, LANES), BF16),
            jax.ShapeDtypeStruct((planes - 1, 16 * width, LANES), BF16),
            jax.ShapeDtypeStruct((filts, 11, 16, LANES), BF16),
        ],
        in_specs=[pl.BlockSpec(memory_space=pltpu.HBM)] * 3,
        out_specs=whole(3),
        scratch_shapes=[
            pltpu.VMEM(volume.shape, BF16),
            pltpu.VMEM((27, 16, 32), BF16),
            pltpu.VMEM((16, 16, LANES), BF16),
            pltpu.SemaphoreType.DMA((3,)),
        ],
        compiler_params=limit,
        name="regroup",
    )(*[pltpu.with_memory_space_constraint(x, pltpu.HBM) for x in raw])
    slab_x = lax.ppermute(slab_x, "space", [(s - 1, s) for s in range(1, spaces)])
    gathered = lax.all_to_all(packed, "filt", 0, 0, tiled=True)
    border = pl.pallas_call(
        border_kernel,
        out_shape=jax.ShapeDtypeStruct((7, 48, LANES), BF16),
        in_specs=whole(2),
        out_specs=whole(1)[0],
        compiler_params=limit,
        name="border",
    )(slab_x, own)
    border = lax.ppermute(border, "filt", [(f - 1, f) for f in range(1, filts)])

    stem_w = jnp.pad(stem_weight.reshape(108, 32).T, ((0, 0), (0, 20)))
    place = jnp.asarray(place_table(), BF16)
    parts = pl.pallas_call(
        main_kernel,
        out_shape=jax.ShapeDtypeStruct((filts, 13, 16, LANES), BF16),
        in_specs=whole(6),
        out_specs=whole(1)[0],
        scratch_shapes=[
            pltpu.VMEM((7, 48, 9 * LANES), BF16),
            pltpu.VMEM((64, 896), BF16),
            pltpu.VMEM((864, 512), BF16),
            pltpu.VMEM((3, 64, 9 * LANES), F32),
            pltpu.VMEM((3, 96, 9 * LANES), BF16),
        ],
        compiler_params=limit,
        name="sections",
    )(own, slab_x, border, stem_w, place, gathered)

    parts = lax.all_to_all(parts, "filt", 0, 0, tiled=True)
    sums, features = pl.pallas_call(
        sum_kernel,
        out_shape=[
            jax.ShapeDtypeStruct((spaces, 9, 16, LANES), BF16),
            jax.ShapeDtypeStruct((16, 16, LANES), BF16),
        ],
        in_specs=whole(1),
        out_specs=whole(2),
        compiler_params=limit,
        name="sums",
    )(parts)
    sums = lax.all_to_all(sums, "space", 0, 0, tiled=True)
    middle, stem = pl.pallas_call(
        functools.partial(unpack_kernel, middle_cells**-0.5, stem_cells**-0.5),
        out_shape=[
            jax.ShapeDtypeStruct((27, 16, 32), F32),
            jax.ShapeDtypeStruct((27, 4, 32), F32),
        ],
        in_specs=whole(1),
        out_specs=whole(2),
        compiler_params=limit,
        name="unpack",
    )(sums)
    return features.reshape(16, 1, 16, LANES), middle.transpose(0, 2, 1), stem


def solution(mesh):
    in_specs = (
        P(None, "space", "filt", None),
        P(),
        P(None, None, "filt"),
        P("filt", "space", None, None),
    )
    out_specs = (P("filt", "space", None, None), P(None, None, "filt"), P())
    return jax.shard_map(body, mesh=mesh, in_specs=in_specs, out_specs=out_specs, check_vma=False)
```

```python
import functools

import jax
import jax.numpy as jnp
import numpy as np
from jax import lax
from jax.experimental import pallas as pl
from jax.experimental.pallas import tpu as pltpu
from jax.sharding import PartitionSpec as P

F32 = jnp.float32
BF16 = jnp.bfloat16
LANES = 128
STEM_ROWS = 144


def nn(a, b):
    return lax.dot_general(a, b, (((1,), (0,)), ((), ())), preferred_element_type=F32)


def nt(a, b):
    return lax.dot_general(a, b, (((1,), (1,)), ((), ())), preferred_element_type=F32)


def place_table():
    table = np.zeros((3, LANES, STEM_ROWS), np.float32)
    for even_odd in range(2):
        for a in range(3):
            for b in range(3):
                for d in range(3):
                    q = 2 * even_odd + d - 1
                    group, phase = (2, 3) if q < 0 else (even_odd, q)
                    for c in range(4):
                        column = 48 * a + 16 * b + 4 * phase + c
                        table[group, 4 * (9 * a + 3 * b + d) + c, column] = 1.0
    return table


def rows_lanes(shape):
    return lax.broadcasted_iota(jnp.int32, shape, 0), lax.broadcasted_iota(jnp.int32, shape, 1)


def turn_matrix():
    row, column = rows_lanes((256, 256))
    source = lax.shift_left(row & 15, 4) + lax.shift_right_logical(row, 4)
    return (source == column).astype(F32).astype(BF16)


def regroup_kernel(volume_in, weight_in, cotangent_in, own, slab_x, packed, volume, weight, cotangent, sems):
    copies = [
        pltpu.make_async_copy(source, target, sems.at[k])
        for k, (source, target) in enumerate(
            [(volume_in, volume), (weight_in, weight), (cotangent_in, cotangent)]
        )
    ]
    for copy in copies:
        copy.start()
    channels, planes, width, depth = volume.shape
    z, column = rows_lanes((depth, depth))
    source = lax.shift_left(column & (LANES - 1), 2) + lax.shift_right_logical(column, 7)
    select = (z == source).astype(F32).astype(BF16)
    turn = turn_matrix()
    copies[0].wait()
    picked = nn(volume[...].reshape(channels * planes * width, depth), select).astype(BF16)
    grouped = []
    for x in range(planes):
        parts = []
        for phase in range(4):
            for c in range(channels):
                start = (c * planes + x) * width
                parts.append(picked[start : start + width, phase * LANES : (phase + 1) * LANES])
        grouped.append(jnp.concatenate(parts, axis=0))
    copies[1].wait()
    copies[2].wait()
    grouped.append(cotangent[...].reshape(256, LANES))
    turned = nn(turn, jnp.concatenate(grouped, axis=1)).astype(BF16)
    for x in range(planes):
        plane = turned[:, x * LANES : (x + 1) * LANES]
        own[x] = plane
        if x > 0:
            slab_x[x - 1] = plane

    blank = jnp.zeros((16, 32), BF16)
    taps = [weight[t] if t < 27 else blank for t in range(28)]
    for t in range(7):
        tile = jnp.concatenate(taps[4 * t : 4 * t + 4], axis=1)
        for f in range(packed.shape[0]):
            packed[f, t] = tile
    for f in range(packed.shape[0]):
        for j in range(4):
            row = 16 * (4 * f + j)
            packed[f, 7 + j] = turned[row : row + 16, planes * LANES :]


def border_kernel(slab_x, own, border):
    for x in range(3):
        border[x] = slab_x[x, -48:]
    for x in range(4):
        border[3 + x] = own[x, -48:]


def softplus_sigmoid(values):
    small = jnp.exp(-jnp.abs(values))
    inverse = 1.0 / (1.0 + small)
    soft = jnp.maximum(values, 0.0) + jnp.log(1.0 + small)
    return soft, jnp.where(values >= 0.0, inverse, small * inverse)


def roll_blocks(values, amount):
    blocks = []
    for start in range(0, values.shape[1], LANES):
        block = values[:, start : start + LANES]
        lane = lax.broadcasted_iota(jnp.int32, block.shape, 1)
        edge = 0 if amount == 1 else LANES - 1
        blocks.append(jnp.where(lane == edge, 0.0, pltpu.roll(block, amount % LANES, 1)))
    return jnp.concatenate(blocks, axis=1)


def fill_columns(cols, planes, count):
    for x, plane in enumerate(planes):
        for j in range(count):
            cols[x, :, pl.ds(j * LANES, LANES)] = plane[32 * j : 32 * j + 48]


def stem_forward(weights, cols, i, keep):
    pre = nn(weights, cols[2 * i : 2 * i + 3].reshape(STEM_ROWS, cols.shape[2]))
    pre = jnp.concatenate([pre[0:32] + roll_blocks(pre[64:96], 1), pre[32:64]], axis=0)
    soft, sig = softplus_sigmoid(pre)
    act = (0.3 * pre + 0.7 * soft) * keep
    taps = jnp.concatenate([roll_blocks(act[32:64], 1), act], axis=0).astype(BF16)
    return (0.3 + 0.7 * sig) * keep, taps


def keep_space():
    return jnp.where(lax.axis_index("space") > 0, 1.0, 0.0).astype(F32)


def inner_kernel(own, slab_x, stem_w, place, weights, cols, slope, taps):
    weights[...] = jnp.concatenate([nn(stem_w[...], place[g]) for g in range(3)], axis=0).astype(BF16)
    planes = [slab_x[x, 16:256] if x < 3 else own[x - 3, 16:256] for x in range(7)]
    fill_columns(cols, planes, 7)
    for i in range(3):
        slope[i], taps[i] = stem_forward(weights[...], cols, i, keep_space() if i == 0 else 1.0)


def main_kernel(
    own, slab_x, border, place, gathered, weights, cols, slope, taps, parts, low_cols, mid_w, mid_cols, stem_back, low_back,
):
    blocks = gathered.shape[0]
    keep_y = jnp.where(lax.axis_index("filt") > 0, 1.0, 0.0).astype(F32)
    planes = [
        jnp.concatenate([border[x], slab_x[x, 0:32] if x < 3 else own[x - 3, 0:32]], axis=0)
        for x in range(7)
    ]
    fill_columns(low_cols, planes, 2)
    low_slope = []
    for i in range(3):
        keep = jnp.where(lax.broadcasted_iota(jnp.int32, (64, 2 * LANES), 1) < LANES, keep_y, 1.0)
        if i == 0:
            keep = keep * keep_space()
        one_slope, low_taps = stem_forward(weights[...], low_cols, i, keep)
        low_slope.append(one_slope)
        for j in range(9):
            if j < 2:
                part = low_taps[:, j * LANES : (j + 1) * LANES]
            else:
                part = taps[i, :, pl.ds((j - 2) * LANES, LANES)]
            for b in range(3):
                if (j - b) % 2 == 0 and 0 <= (j - b) // 2 < 4:
                    row = 96 * (3 * i + b)
                    mid_cols[row : row + 96, pl.ds((j - b) // 2 * LANES, LANES)] = part

    for f in range(blocks):
        for t in range(7):
            mid_w[16 * f : 16 * f + 16, t * LANES : (t + 1) * LANES] = gathered[f, t]
    cotangent = jnp.concatenate(
        [
            jnp.concatenate([gathered[f, 7 + j] for j in range(4)], axis=1)
            for f in range(blocks)
        ],
        axis=0,
    )
    pre = nn(mid_w[:, 0:864], mid_cols[...])
    soft, sig = softplus_sigmoid(pre)
    features = (0.3 * pre + 0.7 * soft).astype(BF16)
    delta = cotangent.astype(F32) * (0.3 + 0.7 * sig)
    delta_low = delta.astype(BF16)
    mid_grad = nt(delta_low, mid_cols[...])

    turned = jnp.concatenate(
        [mid_w[:, t * LANES : (t + 1) * LANES].astype(F32).T for t in range(7)], axis=0
    ).astype(BF16)
    zero = jnp.zeros((32, blocks * 16), BF16)

    def block(a, b, d):
        row = 32 * (9 * a + 3 * b + d)
        return turned[row : row + 32]

    def wide(a, b):
        even = jnp.concatenate([block(a, b, 1), zero], axis=1)
        odd = jnp.concatenate([block(a, b, 2), block(a, b, 0)], axis=1)
        return jnp.concatenate([even, odd], axis=0)

    both = jnp.concatenate([delta_low, roll_blocks(delta, -1).astype(BF16)], axis=0)
    nothing = jnp.zeros((2 * blocks * 16, LANES), BF16)
    pair = jnp.concatenate(
        [jnp.concatenate([both, nothing], axis=1), jnp.concatenate([nothing, both], axis=1)], axis=0
    )
    odd_back = nn(jnp.concatenate([wide(i, 1) for i in range(3)], axis=0), both)
    even_back = nn(
        jnp.concatenate([jnp.concatenate([wide(i, 0), wide(i, 2)], axis=1) for i in range(3)], axis=0), pair
    )
    stem_grad = jnp.zeros((96, STEM_ROWS), F32)
    for i in range(3):
        for j in range(9):
            source = even_back if j % 2 == 0 else odd_back
            part = source[64 * i : 64 * i + 64, (j // 2) * LANES : (j // 2 + 1) * LANES]
            if j < 2:
                target, lanes = low_back, pl.ds(j * LANES, LANES)
                part = part * low_slope[i][:, j * LANES : (j + 1) * LANES]
            else:
                target, lanes = stem_back, pl.ds((j - 2) * LANES, LANES)
                part = part * slope[i, :, lanes]
            target[i, 0:64, lanes] = part.astype(BF16)
            target[i, 64:96, lanes] = roll_blocks(part[0:32], -1).astype(BF16)
        stem_grad += nt(stem_back[i], cols[2 * i : 2 * i + 3].reshape(STEM_ROWS, 7 * LANES))
        stem_grad += nt(low_back[i], low_cols[2 * i : 2 * i + 3].reshape(STEM_ROWS, 2 * LANES))
    high = stem_grad.astype(BF16)
    low = (stem_grad - high.astype(F32)).astype(BF16)
    stem = sum(
        nt(part[32 * g : 32 * g + 32], place[g]) for part in (high, low) for g in range(3)
    ).astype(BF16)

    middle = mid_grad.astype(BF16)
    middle = jnp.concatenate([middle, jnp.zeros((blocks * 16, 32), BF16)], axis=1)
    for f in range(blocks):
        rows = slice(16 * f, 16 * f + 16)
        for t in range(7):
            parts[f, t] = middle[rows, t * LANES : (t + 1) * LANES]
        for half in range(2):
            parts[f, 7 + half] = stem[16 * half : 16 * half + 16]
        for j in range(4):
            parts[f, 9 + j] = features[rows, j * LANES : (j + 1) * LANES]


def sum_kernel(parts, sums):
    total = jnp.sum(parts[:, 0:9].astype(F32), axis=0).astype(BF16)
    for s in range(sums.shape[0]):
        sums[s] = total


def features_kernel(parts, features):
    rows = [parts[f, 9 + j] for f in range(parts.shape[0]) for j in range(4)]
    features[...] = nn(turn_matrix(), jnp.concatenate(rows, axis=0)).astype(BF16).reshape(16, 16, LANES)


def unpack_kernel(middle_scale, stem_scale, sums, middle, stem):
    total = jnp.sum(sums[...].astype(F32), axis=0)
    for t in range(27):
        start = 32 * (t % 4)
        middle[t] = total[t // 4, :, start : start + 32] * middle_scale
    turned = jnp.concatenate([total[7], total[8]], axis=0).T * stem_scale
    for t in range(27):
        stem[t] = turned[4 * t : 4 * t + 4]


def whole(count):
    return [pl.BlockSpec(memory_space=pltpu.VMEM)] * count


def body(volume, stem_weight, middle_weight, cotangent):
    spaces, filts = lax.axis_size("space"), lax.axis_size("filt")
    channels, planes, width, depth = volume.shape
    stem_cells = (planes // 2) * spaces * (width // 2) * filts * (depth // 2)
    middle_cells = stem_cells // 8
    limit = pltpu.CompilerParams(vmem_limit_bytes=48 * 1024 * 1024)

    raw = (volume, middle_weight.transpose(0, 2, 1), cotangent.reshape(16, 16, LANES))
    own, slab_x, packed = pl.pallas_call(
        regroup_kernel,
        out_shape=[
            jax.ShapeDtypeStruct((planes, 16 * width, LANES), BF16),
            jax.ShapeDtypeStruct((planes - 1, 16 * width, LANES), BF16),
            jax.ShapeDtypeStruct((filts, 11, 16, LANES), BF16),
        ],
        in_specs=[pl.BlockSpec(memory_space=pltpu.HBM)] * 3,
        out_specs=whole(3),
        scratch_shapes=[
            pltpu.VMEM(volume.shape, BF16),
            pltpu.VMEM((27, 16, 32), BF16),
            pltpu.VMEM((16, 16, LANES), BF16),
            pltpu.SemaphoreType.DMA((3,)),
        ],
        compiler_params=limit,
        name="regroup",
    )(*[pltpu.with_memory_space_constraint(x, pltpu.HBM) for x in raw])
    slab_x = lax.ppermute(slab_x, "space", [(s - 1, s) for s in range(1, spaces)])
    gathered = lax.all_to_all(packed, "filt", 0, 0, tiled=True)
    border = pl.pallas_call(
        border_kernel,
        out_shape=jax.ShapeDtypeStruct((7, 48, LANES), BF16),
        in_specs=whole(2),
        out_specs=whole(1)[0],
        compiler_params=limit,
        name="border",
    )(slab_x, own)
    border = lax.ppermute(border, "filt", [(f - 1, f) for f in range(1, filts)])

    stem_w = jnp.pad(stem_weight.reshape(108, 32).T, ((0, 0), (0, 20)))
    place = jnp.asarray(place_table(), BF16)
    weights, cols, slope, taps = pl.pallas_call(
        inner_kernel,
        out_shape=[
            jax.ShapeDtypeStruct((96, STEM_ROWS), BF16),
            jax.ShapeDtypeStruct((7, 48, 7 * LANES), BF16),
            jax.ShapeDtypeStruct((3, 64, 7 * LANES), F32),
            jax.ShapeDtypeStruct((3, 96, 7 * LANES), BF16),
        ],
        in_specs=whole(4),
        out_specs=whole(4),
        compiler_params=limit,
        cost_estimate=pl.CostEstimate(flops=200_000_000, bytes_accessed=4_000_000, transcendentals=500_000),
        name="stem_inner",
    )(own, slab_x, stem_w, place)
    parts = pl.pallas_call(
        main_kernel,
        out_shape=jax.ShapeDtypeStruct((filts, 13, 16, LANES), BF16),
        in_specs=whole(9),
        out_specs=whole(1)[0],
        scratch_shapes=[
            pltpu.VMEM((7, 48, 2 * LANES), BF16),
            pltpu.VMEM((64, 896), BF16),
            pltpu.VMEM((864, 512), BF16),
            pltpu.VMEM((3, 96, 7 * LANES), BF16),
            pltpu.VMEM((3, 96, 2 * LANES), BF16),
        ],
        compiler_params=limit,
        name="sections",
    )(own, slab_x, border, place, gathered, weights, cols, slope, taps)

    parts = lax.all_to_all(parts, "filt", 0, 0, tiled=True)
    sums = pl.pallas_call(
        sum_kernel,
        out_shape=jax.ShapeDtypeStruct((spaces, 9, 16, LANES), BF16),
        in_specs=whole(1),
        out_specs=whole(1)[0],
        compiler_params=limit,
        name="sums",
    )(parts)
    features = pl.pallas_call(
        features_kernel,
        out_shape=jax.ShapeDtypeStruct((16, 16, LANES), BF16),
        in_specs=whole(1),
        out_specs=whole(1)[0],
        compiler_params=limit,
        cost_estimate=pl.CostEstimate(flops=20_000_000, bytes_accessed=2_000_000, transcendentals=0),
        name="features",
    )(parts)
    sums = lax.all_to_all(sums, "space", 0, 0, tiled=True)
    middle, stem = pl.pallas_call(
        functools.partial(unpack_kernel, middle_cells**-0.5, stem_cells**-0.5),
        out_shape=[
            jax.ShapeDtypeStruct((27, 16, 32), F32),
            jax.ShapeDtypeStruct((27, 4, 32), F32),
        ],
        in_specs=whole(1),
        out_specs=whole(2),
        compiler_params=limit,
        name="unpack",
    )(sums)
    return features.reshape(16, 1, 16, LANES), middle.transpose(0, 2, 1), stem


def solution(mesh):
    in_specs = (
        P(None, "space", "filt", None),
        P(),
        P(None, None, "filt"),
        P("filt", "space", None, None),
    )
    out_specs = (P("filt", "space", None, None), P(None, None, "filt"), P())
    return jax.shard_map(body, mesh=mesh, in_specs=in_specs, out_specs=out_specs, check_vma=False)
```

```python
import functools

import jax
import jax.numpy as jnp
import numpy as np
from jax import lax
from jax.experimental import pallas as pl
from jax.experimental.pallas import tpu as pltpu
from jax.sharding import PartitionSpec as P

F32 = jnp.float32
BF16 = jnp.bfloat16
LANES = 128
STEM_ROWS = 144


def nn(a, b):
    return lax.dot_general(a, b, (((1,), (0,)), ((), ())), preferred_element_type=F32)


def nt(a, b):
    return lax.dot_general(a, b, (((1,), (1,)), ((), ())), preferred_element_type=F32)


def place_table():
    table = np.zeros((3, LANES, STEM_ROWS), np.float32)
    for even_odd in range(2):
        for a in range(3):
            for b in range(3):
                for d in range(3):
                    q = 2 * even_odd + d - 1
                    group, phase = (2, 3) if q < 0 else (even_odd, q)
                    for c in range(4):
                        column = 48 * a + 16 * b + 4 * phase + c
                        table[group, 4 * (9 * a + 3 * b + d) + c, column] = 1.0
    return table


def rows_lanes(shape):
    return lax.broadcasted_iota(jnp.int32, shape, 0), lax.broadcasted_iota(jnp.int32, shape, 1)


def turn_matrix():
    row, column = rows_lanes((256, 256))
    source = lax.shift_left(row & 15, 4) + lax.shift_right_logical(row, 4)
    return (source == column).astype(F32).astype(BF16)


def regroup_kernel(volume_in, weight_in, cotangent_in, own, slab_x, packed_out, volume, weight, cotangent, packed, sems):
    copies = [
        pltpu.make_async_copy(source, target, sems.at[k])
        for k, (source, target) in enumerate(
            [(weight_in, weight), (cotangent_in, cotangent), (volume_in, volume), (packed, packed_out)]
        )
    ]
    for copy in copies[:3]:
        copy.start()
    channels, planes, width, depth = volume.shape
    z, column = rows_lanes((depth, depth))
    source = lax.shift_left(column & (LANES - 1), 2) + lax.shift_right_logical(column, 7)
    select = (z == source).astype(F32).astype(BF16)
    turn = turn_matrix()

    blank = jnp.zeros((16, 32), BF16)
    copies[0].wait()
    taps = [weight[t] if t < 27 else blank for t in range(28)]
    for t in range(7):
        tile = jnp.concatenate(taps[4 * t : 4 * t + 4], axis=1)
        for f in range(packed.shape[0]):
            packed[f, t] = tile
    copies[1].wait()
    turned = nn(turn, cotangent[...].reshape(256, LANES)).astype(BF16)
    for f in range(packed.shape[0]):
        for j in range(4):
            row = 16 * (4 * f + j)
            packed[f, 7 + j] = turned[row : row + 16]
    copies[3].start()

    copies[2].wait()
    picked = nn(volume[...].reshape(channels * planes * width, depth), select).astype(BF16)
    grouped = []
    for x in range(planes):
        parts = []
        for phase in range(4):
            for c in range(channels):
                start = (c * planes + x) * width
                parts.append(picked[start : start + width, phase * LANES : (phase + 1) * LANES])
        grouped.append(jnp.concatenate(parts, axis=0))
    turned = nn(turn, jnp.concatenate(grouped, axis=1)).astype(BF16)
    for x in range(planes):
        plane = turned[:, x * LANES : (x + 1) * LANES]
        own[x] = plane
        if x > 0:
            slab_x[x - 1] = plane
    copies[3].wait()


def border_kernel(slab_x, own, border):
    for x in range(3):
        border[x] = slab_x[x, -48:]
    for x in range(4):
        border[3 + x] = own[x, -48:]


def softplus_sigmoid(values):
    small = jnp.exp(-jnp.abs(values))
    inverse = 1.0 / (1.0 + small)
    soft = jnp.maximum(values, 0.0) + jnp.log(1.0 + small)
    return soft, jnp.where(values >= 0.0, inverse, small * inverse)


def roll_blocks(values, amount):
    blocks = []
    for start in range(0, values.shape[1], LANES):
        block = values[:, start : start + LANES]
        lane = lax.broadcasted_iota(jnp.int32, block.shape, 1)
        edge = 0 if amount == 1 else LANES - 1
        blocks.append(jnp.where(lane == edge, 0.0, pltpu.roll(block, amount % LANES, 1)))
    return jnp.concatenate(blocks, axis=1)


def fill_columns(cols, planes, count):
    for x, plane in enumerate(planes):
        for j in range(count):
            cols[x, :, pl.ds(j * LANES, LANES)] = plane[32 * j : 32 * j + 48]


def stem_forward(weights, cols, i, keep):
    pre = nn(weights, cols[2 * i : 2 * i + 3].reshape(STEM_ROWS, cols.shape[2]))
    pre = jnp.concatenate([pre[0:32] + roll_blocks(pre[64:96], 1), pre[32:64]], axis=0)
    soft, sig = softplus_sigmoid(pre)
    act = (0.3 * pre + 0.7 * soft) * keep
    taps = jnp.concatenate([roll_blocks(act[32:64], 1), act], axis=0).astype(BF16)
    return (0.3 + 0.7 * sig) * keep, taps


def keep_space():
    return jnp.where(lax.axis_index("space") > 0, 1.0, 0.0).astype(F32)


def inner_kernel(own, slab_x, stem_w, place, weights, cols, slope, taps):
    weights[...] = jnp.concatenate([nn(stem_w[...], place[g]) for g in range(3)], axis=0).astype(BF16)
    planes = [slab_x[x, 16:256] if x < 3 else own[x - 3, 16:256] for x in range(7)]
    fill_columns(cols, planes, 7)
    for i in range(3):
        slope[i], taps[i] = stem_forward(weights[...], cols, i, keep_space() if i == 0 else 1.0)


def main_kernel(
    own, slab_x, border, place, gathered, weights, cols, slope, taps, parts, low_cols, mid_w, mid_cols, stem_back, low_back,
):
    blocks = gathered.shape[0]
    keep_y = jnp.where(lax.axis_index("filt") > 0, 1.0, 0.0).astype(F32)
    planes = [
        jnp.concatenate([border[x], slab_x[x, 0:32] if x < 3 else own[x - 3, 0:32]], axis=0)
        for x in range(7)
    ]
    fill_columns(low_cols, planes, 2)
    low_slope = []
    for i in range(3):
        keep = jnp.where(lax.broadcasted_iota(jnp.int32, (64, 2 * LANES), 1) < LANES, keep_y, 1.0)
        if i == 0:
            keep = keep * keep_space()
        one_slope, low_taps = stem_forward(weights[...], low_cols, i, keep)
        low_slope.append(one_slope)
        for j in range(9):
            if j < 2:
                part = low_taps[:, j * LANES : (j + 1) * LANES]
            else:
                part = taps[i, :, pl.ds((j - 2) * LANES, LANES)]
            for b in range(3):
                if (j - b) % 2 == 0 and 0 <= (j - b) // 2 < 4:
                    row = 96 * (3 * i + b)
                    mid_cols[row : row + 96, pl.ds((j - b) // 2 * LANES, LANES)] = part

    for f in range(blocks):
        for t in range(7):
            mid_w[16 * f : 16 * f + 16, t * LANES : (t + 1) * LANES] = gathered[f, t]
    cotangent = jnp.concatenate(
        [
            jnp.concatenate([gathered[f, 7 + j] for j in range(4)], axis=1)
            for f in range(blocks)
        ],
        axis=0,
    )
    pre = nn(mid_w[:, 0:864], mid_cols[...])
    soft, sig = softplus_sigmoid(pre)
    features = (0.3 * pre + 0.7 * soft).astype(BF16)
    delta = cotangent.astype(F32) * (0.3 + 0.7 * sig)
    delta_low = delta.astype(BF16)
    mid_grad = nt(delta_low, mid_cols[...])

    turned = jnp.concatenate(
        [mid_w[:, t * LANES : (t + 1) * LANES].astype(F32).T for t in range(7)], axis=0
    ).astype(BF16)
    zero = jnp.zeros((32, blocks * 16), BF16)

    def block(a, b, d):
        row = 32 * (9 * a + 3 * b + d)
        return turned[row : row + 32]

    def wide(a, b):
        even = jnp.concatenate([block(a, b, 1), zero], axis=1)
        odd = jnp.concatenate([block(a, b, 2), block(a, b, 0)], axis=1)
        return jnp.concatenate([even, odd], axis=0)

    both = jnp.concatenate([delta_low, roll_blocks(delta, -1).astype(BF16)], axis=0)
    nothing = jnp.zeros((2 * blocks * 16, LANES), BF16)
    pair = jnp.concatenate(
        [jnp.concatenate([both, nothing], axis=1), jnp.concatenate([nothing, both], axis=1)], axis=0
    )
    odd_back = nn(jnp.concatenate([wide(i, 1) for i in range(3)], axis=0), both)
    even_back = nn(
        jnp.concatenate([jnp.concatenate([wide(i, 0), wide(i, 2)], axis=1) for i in range(3)], axis=0), pair
    )
    stem_grad = jnp.zeros((96, STEM_ROWS), F32)
    for i in range(3):
        for j in range(9):
            source = even_back if j % 2 == 0 else odd_back
            part = source[64 * i : 64 * i + 64, (j // 2) * LANES : (j // 2 + 1) * LANES]
            if j < 2:
                target, lanes = low_back, pl.ds(j * LANES, LANES)
                part = part * low_slope[i][:, j * LANES : (j + 1) * LANES]
            else:
                target, lanes = stem_back, pl.ds((j - 2) * LANES, LANES)
                part = part * slope[i, :, lanes]
            target[i, 0:64, lanes] = part.astype(BF16)
            target[i, 64:96, lanes] = roll_blocks(part[0:32], -1).astype(BF16)
        stem_grad += nt(stem_back[i], cols[2 * i : 2 * i + 3].reshape(STEM_ROWS, 7 * LANES))
        stem_grad += nt(low_back[i], low_cols[2 * i : 2 * i + 3].reshape(STEM_ROWS, 2 * LANES))
    high = stem_grad.astype(BF16)
    low = (stem_grad - high.astype(F32)).astype(BF16)
    stem = sum(
        nt(part[32 * g : 32 * g + 32], place[g]) for part in (high, low) for g in range(3)
    ).astype(BF16)

    middle = mid_grad.astype(BF16)
    middle = jnp.concatenate([middle, jnp.zeros((blocks * 16, 32), BF16)], axis=1)
    for f in range(blocks):
        rows = slice(16 * f, 16 * f + 16)
        for t in range(7):
            parts[f, t] = middle[rows, t * LANES : (t + 1) * LANES]
        for half in range(2):
            parts[f, 7 + half] = stem[16 * half : 16 * half + 16]
        for j in range(4):
            parts[f, 9 + j] = features[rows, j * LANES : (j + 1) * LANES]


def sum_kernel(parts, sums):
    total = jnp.sum(parts[:, 0:9].astype(F32), axis=0).astype(BF16)
    for s in range(sums.shape[0]):
        sums[s] = total


def unpack_kernel(middle_scale, stem_scale, sums, parts, features, middle, stem):
    rows = [parts[f, 9 + j] for f in range(parts.shape[0]) for j in range(4)]
    features[...] = nn(turn_matrix(), jnp.concatenate(rows, axis=0)).astype(BF16).reshape(16, 16, LANES)
    total = jnp.sum(sums[...].astype(F32), axis=0)
    for t in range(27):
        start = 32 * (t % 4)
        middle[t] = total[t // 4, :, start : start + 32] * middle_scale
    turned = jnp.concatenate([total[7], total[8]], axis=0).T * stem_scale
    for t in range(27):
        stem[t] = turned[4 * t : 4 * t + 4]


def whole(count):
    return [pl.BlockSpec(memory_space=pltpu.VMEM)] * count


def body(volume, stem_weight, middle_weight, cotangent):
    spaces, filts = lax.axis_size("space"), lax.axis_size("filt")
    channels, planes, width, depth = volume.shape
    stem_cells = (planes // 2) * spaces * (width // 2) * filts * (depth // 2)
    middle_cells = stem_cells // 8
    limit = pltpu.CompilerParams(vmem_limit_bytes=48 * 1024 * 1024)

    raw = (volume, middle_weight.transpose(0, 2, 1), cotangent.reshape(16, 16, LANES))
    own, slab_x, packed = pl.pallas_call(
        regroup_kernel,
        out_shape=[
            jax.ShapeDtypeStruct((planes, 16 * width, LANES), BF16),
            jax.ShapeDtypeStruct((planes - 1, 16 * width, LANES), BF16),
            jax.ShapeDtypeStruct((filts, 11, 16, LANES), BF16),
        ],
        in_specs=[pl.BlockSpec(memory_space=pltpu.HBM)] * 3,
        out_specs=whole(2) + [pl.BlockSpec(memory_space=pl.ANY)],
        scratch_shapes=[
            pltpu.VMEM(volume.shape, BF16),
            pltpu.VMEM((27, 16, 32), BF16),
            pltpu.VMEM((16, 16, LANES), BF16),
            pltpu.VMEM((filts, 11, 16, LANES), BF16),
            pltpu.SemaphoreType.DMA((4,)),
        ],
        compiler_params=limit,
        name="regroup",
    )(*[pltpu.with_memory_space_constraint(x, pltpu.HBM) for x in raw])
    slab_x = lax.ppermute(slab_x, "space", [(s - 1, s) for s in range(1, spaces)])
    gathered = lax.all_to_all(packed, "filt", 0, 0, tiled=True)
    border = pl.pallas_call(
        border_kernel,
        out_shape=jax.ShapeDtypeStruct((7, 48, LANES), BF16),
        in_specs=whole(2),
        out_specs=whole(1)[0],
        compiler_params=limit,
        name="border",
    )(slab_x, own)
    border = lax.ppermute(border, "filt", [(f - 1, f) for f in range(1, filts)])

    stem_w = jnp.pad(stem_weight.reshape(108, 32).T, ((0, 0), (0, 20)))
    place = jnp.asarray(place_table(), BF16)
    weights, cols, slope, taps = pl.pallas_call(
        inner_kernel,
        out_shape=[
            jax.ShapeDtypeStruct((96, STEM_ROWS), BF16),
            jax.ShapeDtypeStruct((7, 48, 7 * LANES), BF16),
            jax.ShapeDtypeStruct((3, 64, 7 * LANES), F32),
            jax.ShapeDtypeStruct((3, 96, 7 * LANES), BF16),
        ],
        in_specs=whole(4),
        out_specs=whole(4),
        compiler_params=limit,
        cost_estimate=pl.CostEstimate(flops=200_000_000, bytes_accessed=4_000_000, transcendentals=500_000),
        name="stem_inner",
    )(own, slab_x, stem_w, place)
    parts = pl.pallas_call(
        main_kernel,
        out_shape=jax.ShapeDtypeStruct((filts, 13, 16, LANES), BF16),
        in_specs=whole(9),
        out_specs=whole(1)[0],
        scratch_shapes=[
            pltpu.VMEM((7, 48, 2 * LANES), BF16),
            pltpu.VMEM((64, 896), BF16),
            pltpu.VMEM((864, 512), BF16),
            pltpu.VMEM((3, 96, 7 * LANES), BF16),
            pltpu.VMEM((3, 96, 2 * LANES), BF16),
        ],
        compiler_params=limit,
        name="sections",
    )(own, slab_x, border, place, gathered, weights, cols, slope, taps)

    parts = lax.all_to_all(parts, "filt", 0, 0, tiled=True)
    sums = pl.pallas_call(
        sum_kernel,
        out_shape=jax.ShapeDtypeStruct((spaces, 9, 16, LANES), BF16),
        in_specs=whole(1),
        out_specs=whole(1)[0],
        compiler_params=limit,
        name="sums",
    )(parts)
    sums = lax.all_to_all(sums, "space", 0, 0, tiled=True)
    features, middle, stem = pl.pallas_call(
        functools.partial(unpack_kernel, middle_cells**-0.5, stem_cells**-0.5),
        out_shape=[
            jax.ShapeDtypeStruct((16, 16, LANES), BF16),
            jax.ShapeDtypeStruct((27, 16, 32), F32),
            jax.ShapeDtypeStruct((27, 4, 32), F32),
        ],
        in_specs=whole(2),
        out_specs=whole(3),
        compiler_params=limit,
        name="unpack",
    )(sums, parts)
    return features.reshape(16, 1, 16, LANES), middle.transpose(0, 2, 1), stem


def solution(mesh):
    in_specs = (
        P(None, "space", "filt", None),
        P(),
        P(None, None, "filt"),
        P("filt", "space", None, None),
    )
    out_specs = (P("filt", "space", None, None), P(None, None, "filt"), P())
    return jax.shard_map(body, mesh=mesh, in_specs=in_specs, out_specs=out_specs, check_vma=False)
```

```python
import functools

import jax
import jax.numpy as jnp
import numpy as np
from jax import lax
from jax.experimental import pallas as pl
from jax.experimental.pallas import tpu as pltpu
from jax.sharding import PartitionSpec as P

F32 = jnp.float32
BF16 = jnp.bfloat16
LANES = 128
STEM_ROWS = 144


def nn(a, b):
    return lax.dot_general(a, b, (((1,), (0,)), ((), ())), preferred_element_type=F32)


def nt(a, b):
    return lax.dot_general(a, b, (((1,), (1,)), ((), ())), preferred_element_type=F32)


def place_table():
    table = np.zeros((3, LANES, STEM_ROWS), np.float32)
    for even_odd in range(2):
        for a in range(3):
            for b in range(3):
                for d in range(3):
                    q = 2 * even_odd + d - 1
                    group, phase = (2, 3) if q < 0 else (even_odd, q)
                    for c in range(4):
                        column = 48 * a + 16 * b + 4 * phase + c
                        table[group, 4 * (9 * a + 3 * b + d) + c, column] = 1.0
    return table


def rows_lanes(shape):
    return lax.broadcasted_iota(jnp.int32, shape, 0), lax.broadcasted_iota(jnp.int32, shape, 1)


def turn_matrix():
    row, column = rows_lanes((256, 256))
    source = lax.shift_left(row & 15, 4) + lax.shift_right_logical(row, 4)
    return (source == column).astype(F32).astype(BF16)


def regroup_kernel(volume_in, weight_in, cotangent_in, own, slab_x, packed_out, volume, weight, cotangent, packed, sems):
    channels, planes, width, depth = volume.shape
    pairs = [(weight_in, weight), (cotangent_in, cotangent), (packed, packed_out)]
    pairs += [(volume_in.at[c], volume.at[c]) for c in range(channels)]
    copies = [pltpu.make_async_copy(*pair, sems.at[k]) for k, pair in enumerate(pairs)]
    for copy in copies[:2] + copies[3:]:
        copy.start()
    z, column = rows_lanes((depth, depth))
    source = lax.shift_left(column & (LANES - 1), 2) + lax.shift_right_logical(column, 7)
    select = (z == source).astype(F32).astype(BF16)
    turn = turn_matrix()

    blank = jnp.zeros((16, 32), BF16)
    copies[0].wait()
    taps = [weight[t] if t < 27 else blank for t in range(28)]
    for t in range(7):
        tile = jnp.concatenate(taps[4 * t : 4 * t + 4], axis=1)
        for f in range(packed.shape[0]):
            packed[f, t] = tile
    copies[1].wait()
    turned = nn(turn, cotangent[...].reshape(256, LANES)).astype(BF16)
    for f in range(packed.shape[0]):
        for j in range(4):
            row = 16 * (4 * f + j)
            packed[f, 7 + j] = turned[row : row + 16]
    copies[2].start()

    for copy in copies[3:]:
        copy.wait()
    picked = nn(volume[...].reshape(channels * planes * width, depth), select).astype(BF16)
    grouped = []
    for x in range(planes):
        parts = []
        for phase in range(4):
            for c in range(channels):
                start = (c * planes + x) * width
                parts.append(picked[start : start + width, phase * LANES : (phase + 1) * LANES])
        grouped.append(jnp.concatenate(parts, axis=0))
    turned = nn(turn, jnp.concatenate(grouped, axis=1)).astype(BF16)
    for x in range(planes):
        plane = turned[:, x * LANES : (x + 1) * LANES]
        own[x] = plane
        if x > 0:
            slab_x[x - 1] = plane
    copies[2].wait()


def border_kernel(slab_x, own, border):
    for x in range(3):
        border[x] = slab_x[x, -48:]
    for x in range(4):
        border[3 + x] = own[x, -48:]


def softplus_sigmoid(values):
    small = jnp.exp(-jnp.abs(values))
    inverse = 1.0 / (1.0 + small)
    soft = jnp.maximum(values, 0.0) + jnp.log(1.0 + small)
    return soft, jnp.where(values >= 0.0, inverse, small * inverse)


def roll_blocks(values, amount):
    blocks = []
    for start in range(0, values.shape[1], LANES):
        block = values[:, start : start + LANES]
        lane = lax.broadcasted_iota(jnp.int32, block.shape, 1)
        edge = 0 if amount == 1 else LANES - 1
        blocks.append(jnp.where(lane == edge, 0.0, pltpu.roll(block, amount % LANES, 1)))
    return jnp.concatenate(blocks, axis=1)


def fill_columns(cols, planes, count):
    for x, plane in enumerate(planes):
        for j in range(count):
            cols[x, :, pl.ds(j * LANES, LANES)] = plane[32 * j : 32 * j + 48]


def stem_forward(weights, cols, i, keep):
    pre = nn(weights, cols[2 * i : 2 * i + 3].reshape(STEM_ROWS, cols.shape[2]))
    pre = jnp.concatenate([pre[0:32] + roll_blocks(pre[64:96], 1), pre[32:64]], axis=0)
    soft, sig = softplus_sigmoid(pre)
    act = (0.3 * pre + 0.7 * soft) * keep
    taps = jnp.concatenate([roll_blocks(act[32:64], 1), act], axis=0).astype(BF16)
    return (0.3 + 0.7 * sig) * keep, taps


def keep_space():
    return jnp.where(lax.axis_index("space") > 0, 1.0, 0.0).astype(F32)


def inner_kernel(own, slab_x, stem_w, place, weights, cols, slope, taps):
    weights[...] = jnp.concatenate([nn(stem_w[...], place[g]) for g in range(3)], axis=0).astype(BF16)
    planes = [slab_x[x, 16:256] if x < 3 else own[x - 3, 16:256] for x in range(7)]
    fill_columns(cols, planes, 7)
    for i in range(3):
        slope[i], taps[i] = stem_forward(weights[...], cols, i, keep_space() if i == 0 else 1.0)


def fill_taps(mid_cols, part, i, j, first, count):
    for b in range(3):
        if (j - b) % 2 == 0 and first <= (j - b) // 2 < first + count:
            row = 96 * (3 * i + b)
            mid_cols[row : row + 96, pl.ds(((j - b) // 2 - first) * LANES, LANES)] = part


def middle_cells_step(mid_w, mid_cols, cotangent):
    pre = nn(mid_w[:, 0:864], mid_cols[...])
    soft, sig = softplus_sigmoid(pre)
    delta = cotangent.astype(F32) * (0.3 + 0.7 * sig)
    delta_low = delta.astype(BF16)
    mid_grad = nt(delta_low, mid_cols[...])
    both = jnp.concatenate([delta_low, roll_blocks(delta, -1).astype(BF16)], axis=0)
    return (0.3 * pre + 0.7 * soft).astype(BF16), mid_grad, both


def put_back(target, i, start, part):
    lanes = pl.ds(start, LANES)
    target[i, 0:64, lanes] = part.astype(BF16)
    target[i, 64:96, lanes] = roll_blocks(part[0:32], -1).astype(BF16)


def upper_kernel(
    gathered, cols, slope, taps, features, mid_grad, stem_grad, mid_w, odd_w, even_w, mid_cols, stem_back,
):
    blocks = gathered.shape[0]
    for f in range(blocks):
        for t in range(7):
            mid_w[16 * f : 16 * f + 16, t * LANES : (t + 1) * LANES] = gathered[f, t]
    for i in range(3):
        for j in range(2, 9):
            fill_taps(mid_cols, taps[i, :, pl.ds((j - 2) * LANES, LANES)], i, j, 1, 3)
    cotangent = jnp.concatenate(
        [jnp.concatenate([gathered[f, 7 + j] for j in range(1, 4)], axis=1) for f in range(blocks)], axis=0
    )
    features[...], mid_grad[...], both = middle_cells_step(mid_w, mid_cols, cotangent)

    turned = jnp.concatenate(
        [mid_w[:, t * LANES : (t + 1) * LANES].astype(F32).T for t in range(7)], axis=0
    ).astype(BF16)
    zero = jnp.zeros((32, blocks * 16), BF16)

    def block(a, b, d):
        row = 32 * (9 * a + 3 * b + d)
        return turned[row : row + 32]

    def wide(a, b):
        even = jnp.concatenate([block(a, b, 1), zero], axis=1)
        odd = jnp.concatenate([block(a, b, 2), block(a, b, 0)], axis=1)
        return jnp.concatenate([even, odd], axis=0)

    odd_w[...] = jnp.concatenate([wide(i, 1) for i in range(3)], axis=0)
    even_w[...] = jnp.concatenate(
        [jnp.concatenate([wide(i, 0), wide(i, 2)], axis=1) for i in range(3)], axis=0
    )
    nothing = jnp.zeros((2 * blocks * 16, LANES), BF16)
    pair = jnp.concatenate(
        [jnp.concatenate([both, nothing], axis=1), jnp.concatenate([nothing, both], axis=1)], axis=0
    )
    odd_back = nn(odd_w[...], both)
    even_back = nn(even_w[...], pair)
    total = jnp.zeros((96, STEM_ROWS), F32)
    for i in range(3):
        for j in range(7):
            source = even_back if j % 2 == 0 else odd_back
            part = source[64 * i : 64 * i + 64, (j // 2) * LANES : (j // 2 + 1) * LANES]
            put_back(stem_back, i, j * LANES, part * slope[i, :, pl.ds(j * LANES, LANES)])
        total += nt(stem_back[i], cols[2 * i : 2 * i + 3].reshape(STEM_ROWS, 7 * LANES))
    stem_grad[...] = total


def lower_kernel(
    own, slab_x, border, place, gathered, weights, cols, slope, taps, upper_features, upper_mid, upper_stem,
    mid_w, odd_w, even_w, parts, low_cols, mid_cols, low_back,
):
    blocks = gathered.shape[0]
    keep_y = jnp.where(lax.axis_index("filt") > 0, 1.0, 0.0).astype(F32)
    planes = [
        jnp.concatenate([border[x], slab_x[x, 0:32] if x < 3 else own[x - 3, 0:32]], axis=0)
        for x in range(7)
    ]
    fill_columns(low_cols, planes, 2)
    low_slope = []
    for i in range(3):
        keep = jnp.where(lax.broadcasted_iota(jnp.int32, (64, 2 * LANES), 1) < LANES, keep_y, 1.0)
        if i == 0:
            keep = keep * keep_space()
        one_slope, low_taps = stem_forward(weights[...], low_cols, i, keep)
        low_slope.append(one_slope)
        for j in range(2):
            fill_taps(mid_cols, low_taps[:, j * LANES : (j + 1) * LANES], i, j, 0, 1)
        fill_taps(mid_cols, taps[i, :, 0:LANES], i, 2, 0, 1)
    cotangent = jnp.concatenate([gathered[f, 7] for f in range(blocks)], axis=0)
    features, mid_grad, both = middle_cells_step(mid_w, mid_cols, cotangent)

    back = [nn(even_w[:, 0:LANES], both), nn(odd_w[...], both), nn(even_w[:, LANES:], both)]
    stem_grad = upper_stem[...]
    for i in range(3):
        for j in range(2):
            part = back[j][64 * i : 64 * i + 64] * low_slope[i][:, j * LANES : (j + 1) * LANES]
            put_back(low_back, i, j * LANES, part)
        put_back(low_back, i, 2 * LANES, back[2][64 * i : 64 * i + 64] * slope[i, :, 0:LANES])
        low = low_cols[2 * i : 2 * i + 3].reshape(STEM_ROWS, 2 * LANES)
        near = cols[2 * i : 2 * i + 3, :, 0:LANES].reshape(STEM_ROWS, LANES)
        stem_grad += nt(low_back[i], jnp.concatenate([low, near], axis=1))
    high = stem_grad.astype(BF16)
    both = jnp.concatenate([high, (stem_grad - high.astype(F32)).astype(BF16)], axis=0)
    stem = 0.0
    for g in range(3):
        rows = jnp.concatenate([both[32 * g : 32 * g + 32], both[96 + 32 * g : 128 + 32 * g]], axis=0)
        taken = nt(rows, place[g])
        stem += taken[0:32] + taken[32:64]
    stem = stem.astype(BF16)

    middle = (mid_grad + upper_mid[...]).astype(BF16)
    middle = jnp.concatenate([middle, jnp.zeros((blocks * 16, 32), BF16)], axis=1)
    for f in range(blocks):
        rows = slice(16 * f, 16 * f + 16)
        for t in range(7):
            parts[f, t] = middle[rows, t * LANES : (t + 1) * LANES]
        for half in range(2):
            parts[f, 7 + half] = stem[16 * half : 16 * half + 16]
        parts[f, 9] = features[rows]
        for j in range(3):
            parts[f, 10 + j] = upper_features[rows, j * LANES : (j + 1) * LANES]


def sum_kernel(parts, sums):
    total = jnp.sum(parts[:, 0:9].astype(F32), axis=0).astype(BF16)
    for s in range(sums.shape[0]):
        sums[s] = total


def unpack_kernel(
    middle_scale, stem_scale, sums, parts, features_out, middle_out, stem_out, features, middle, stem, sems,
):
    copies = [
        pltpu.make_async_copy(source, target, sems.at[k])
        for k, (source, target) in enumerate(
            [(middle, middle_out), (stem, stem_out), (features, features_out)]
        )
    ]
    total = jnp.sum(sums[...].astype(F32), axis=0)
    for t in range(27):
        start = 32 * (t % 4)
        middle[t] = total[t // 4, :, start : start + 32] * middle_scale
    copies[0].start()
    rows = [parts[f, 9 + j] for f in range(parts.shape[0]) for j in range(4)]
    features[...] = nn(turn_matrix(), jnp.concatenate(rows, axis=0)).astype(BF16).reshape(16, 16, LANES)
    copies[2].start()
    turned = jnp.concatenate([total[7], total[8]], axis=0).T * stem_scale
    for t in range(27):
        stem[t] = turned[4 * t : 4 * t + 4]
    copies[1].start()
    for copy in copies:
        copy.wait()


def whole(count):
    return [pl.BlockSpec(memory_space=pltpu.VMEM)] * count


def body(volume, stem_weight, middle_weight, cotangent):
    spaces, filts = lax.axis_size("space"), lax.axis_size("filt")
    channels, planes, width, depth = volume.shape
    stem_cells = (planes // 2) * spaces * (width // 2) * filts * (depth // 2)
    middle_cells = stem_cells // 8
    limit = pltpu.CompilerParams(vmem_limit_bytes=48 * 1024 * 1024)

    raw = (volume, middle_weight.transpose(0, 2, 1), cotangent.reshape(16, 16, LANES))
    own, slab_x, packed = pl.pallas_call(
        regroup_kernel,
        out_shape=[
            jax.ShapeDtypeStruct((planes, 16 * width, LANES), BF16),
            jax.ShapeDtypeStruct((planes - 1, 16 * width, LANES), BF16),
            jax.ShapeDtypeStruct((filts, 11, 16, LANES), BF16),
        ],
        in_specs=[pl.BlockSpec(memory_space=pltpu.HBM)] * 3,
        out_specs=whole(2) + [pl.BlockSpec(memory_space=pl.ANY)],
        scratch_shapes=[
            pltpu.VMEM(volume.shape, BF16),
            pltpu.VMEM((27, 16, 32), BF16),
            pltpu.VMEM((16, 16, LANES), BF16),
            pltpu.VMEM((filts, 11, 16, LANES), BF16),
            pltpu.SemaphoreType.DMA((3 + channels,)),
        ],
        compiler_params=limit,
        name="regroup",
    )(*[pltpu.with_memory_space_constraint(x, pltpu.HBM) for x in raw])
    slab_x = lax.ppermute(slab_x, "space", [(s - 1, s) for s in range(1, spaces)])
    gathered = lax.all_to_all(packed, "filt", 0, 0, tiled=True)
    border = pl.pallas_call(
        border_kernel,
        out_shape=jax.ShapeDtypeStruct((7, 48, LANES), BF16),
        in_specs=whole(2),
        out_specs=whole(1)[0],
        compiler_params=limit,
        name="border",
    )(slab_x, own)
    border = lax.ppermute(border, "filt", [(f - 1, f) for f in range(1, filts)])

    stem_w = jnp.pad(stem_weight.reshape(108, 32).T, ((0, 0), (0, 20)))
    place = jnp.asarray(place_table(), BF16)
    weights, cols, slope, taps = pl.pallas_call(
        inner_kernel,
        out_shape=[
            jax.ShapeDtypeStruct((96, STEM_ROWS), BF16),
            jax.ShapeDtypeStruct((7, 48, 7 * LANES), BF16),
            jax.ShapeDtypeStruct((3, 64, 7 * LANES), F32),
            jax.ShapeDtypeStruct((3, 96, 7 * LANES), BF16),
        ],
        in_specs=whole(4),
        out_specs=whole(4),
        compiler_params=limit,
        cost_estimate=pl.CostEstimate(flops=200_000_000, bytes_accessed=4_000_000, transcendentals=500_000),
        name="stem_inner",
    )(own, slab_x, stem_w, place)
    upper = pl.pallas_call(
        upper_kernel,
        out_shape=[
            jax.ShapeDtypeStruct((64, 3 * LANES), BF16),
            jax.ShapeDtypeStruct((64, 864), F32),
            jax.ShapeDtypeStruct((96, STEM_ROWS), F32),
            jax.ShapeDtypeStruct((64, 896), BF16),
            jax.ShapeDtypeStruct((192, LANES), BF16),
            jax.ShapeDtypeStruct((192, 2 * LANES), BF16),
        ],
        in_specs=whole(4),
        out_specs=whole(6),
        scratch_shapes=[
            pltpu.VMEM((864, 3 * LANES), BF16),
            pltpu.VMEM((3, 96, 7 * LANES), BF16),
        ],
        compiler_params=limit,
        cost_estimate=pl.CostEstimate(flops=300_000_000, bytes_accessed=4_000_000, transcendentals=100_000),
        name="upper_cells",
    )(gathered, cols, slope, taps)
    parts = pl.pallas_call(
        lower_kernel,
        out_shape=jax.ShapeDtypeStruct((filts, 13, 16, LANES), BF16),
        in_specs=whole(15),
        out_specs=whole(1)[0],
        scratch_shapes=[
            pltpu.VMEM((7, 48, 2 * LANES), BF16),
            pltpu.VMEM((864, LANES), BF16),
            pltpu.VMEM((3, 96, 3 * LANES), BF16),
        ],
        compiler_params=limit,
        name="lower_cells",
    )(own, slab_x, border, place, gathered, weights, cols, slope, taps, *upper)

    parts = lax.all_to_all(parts, "filt", 0, 0, tiled=True)
    sums = pl.pallas_call(
        sum_kernel,
        out_shape=jax.ShapeDtypeStruct((spaces, 9, 16, LANES), BF16),
        in_specs=whole(1),
        out_specs=whole(1)[0],
        compiler_params=limit,
        name="sums",
    )(parts)
    sums = lax.all_to_all(sums, "space", 0, 0, tiled=True)
    features, middle, stem = pl.pallas_call(
        functools.partial(unpack_kernel, middle_cells**-0.5, stem_cells**-0.5),
        out_shape=[
            jax.ShapeDtypeStruct((16, 16, LANES), BF16),
            jax.ShapeDtypeStruct((27, 16, 32), F32),
            jax.ShapeDtypeStruct((27, 4, 32), F32),
        ],
        in_specs=whole(2),
        out_specs=[pl.BlockSpec(memory_space=pl.ANY)] * 3,
        scratch_shapes=[
            pltpu.VMEM((16, 16, LANES), BF16),
            pltpu.VMEM((27, 16, 32), F32),
            pltpu.VMEM((27, 4, 32), F32),
            pltpu.SemaphoreType.DMA((3,)),
        ],
        compiler_params=limit,
        name="unpack",
    )(sums, parts)
    return features.reshape(16, 1, 16, LANES), middle.transpose(0, 2, 1), stem


def solution(mesh):
    in_specs = (
        P(None, "space", "filt", None),
        P(),
        P(None, None, "filt"),
        P("filt", "space", None, None),
    )
    out_specs = (P("filt", "space", None, None), P(None, None, "filt"), P())
    return jax.shard_map(body, mesh=mesh, in_specs=in_specs, out_specs=out_specs, check_vma=False)
```

```python
import functools

import jax
import jax.numpy as jnp
import numpy as np
from jax import lax
from jax.experimental import pallas as pl
from jax.experimental.pallas import tpu as pltpu
from jax.sharding import PartitionSpec as P

F32 = jnp.float32
BF16 = jnp.bfloat16
LANES = 128
STEM_ROWS = 144


def nn(a, b):
    return lax.dot_general(a, b, (((1,), (0,)), ((), ())), preferred_element_type=F32)


def nt(a, b):
    return lax.dot_general(a, b, (((1,), (1,)), ((), ())), preferred_element_type=F32)


def place_table():
    table = np.zeros((3, LANES, STEM_ROWS), np.float32)
    for even_odd in range(2):
        for a in range(3):
            for b in range(3):
                for d in range(3):
                    q = 2 * even_odd + d - 1
                    group, phase = (2, 3) if q < 0 else (even_odd, q)
                    for c in range(4):
                        column = 48 * a + 16 * b + 4 * phase + c
                        table[group, 4 * (9 * a + 3 * b + d) + c, column] = 1.0
    return table


def rows_lanes(shape):
    return lax.broadcasted_iota(jnp.int32, shape, 0), lax.broadcasted_iota(jnp.int32, shape, 1)


def turn_matrix():
    row, column = rows_lanes((256, 256))
    source = lax.shift_left(row & 15, 4) + lax.shift_right_logical(row, 4)
    return (source == column).astype(F32).astype(BF16)


def regroup_kernel(volume_in, weight_in, cotangent_in, own, slab_x, packed_out, volume, weight, cotangent, packed, sems):
    channels, planes, width, depth = volume.shape
    pairs = [(weight_in, weight), (cotangent_in, cotangent), (packed, packed_out)]
    pairs += [(volume_in.at[c], volume.at[c]) for c in range(channels)]
    copies = [pltpu.make_async_copy(*pair, sems.at[k]) for k, pair in enumerate(pairs)]
    for copy in copies[:2] + copies[3:]:
        copy.start()
    z, column = rows_lanes((depth, depth))
    source = lax.shift_left(column & (LANES - 1), 2) + lax.shift_right_logical(column, 7)
    select = (z == source).astype(F32).astype(BF16)
    turn = turn_matrix()

    blank = jnp.zeros((16, 32), BF16)
    copies[0].wait()
    taps = [weight[t] if t < 27 else blank for t in range(28)]
    for t in range(7):
        tile = jnp.concatenate(taps[4 * t : 4 * t + 4], axis=1)
        for f in range(packed.shape[0]):
            packed[f, t] = tile
    copies[1].wait()
    turned = nn(turn, cotangent[...].reshape(256, LANES)).astype(BF16)
    for f in range(packed.shape[0]):
        for j in range(4):
            row = 16 * (4 * f + j)
            packed[f, 7 + j] = turned[row : row + 16]
    copies[2].start()

    for copy in copies[3:]:
        copy.wait()
    picked = nn(volume[...].reshape(channels * planes * width, depth), select).astype(BF16)
    grouped = []
    for x in range(planes):
        parts = []
        for phase in range(4):
            for c in range(channels):
                start = (c * planes + x) * width
                parts.append(picked[start : start + width, phase * LANES : (phase + 1) * LANES])
        grouped.append(jnp.concatenate(parts, axis=0))
    turned = nn(turn, jnp.concatenate(grouped, axis=1)).astype(BF16)
    for x in range(planes):
        plane = turned[:, x * LANES : (x + 1) * LANES]
        own[x] = plane
        if x > 0:
            slab_x[x - 1] = plane
    copies[2].wait()


def border_kernel(slab_x, own, border):
    for x in range(3):
        border[x] = slab_x[x, -48:]
    for x in range(4):
        border[3 + x] = own[x, -48:]


def softplus_sigmoid(values):
    small = jnp.exp(-jnp.abs(values))
    inverse = 1.0 / (1.0 + small)
    soft = jnp.maximum(values, 0.0) + jnp.log(1.0 + small)
    return soft, jnp.where(values >= 0.0, inverse, small * inverse)


def roll_blocks(values, amount):
    blocks = []
    for start in range(0, values.shape[1], LANES):
        block = values[:, start : start + LANES]
        lane = lax.broadcasted_iota(jnp.int32, block.shape, 1)
        edge = 0 if amount == 1 else LANES - 1
        blocks.append(jnp.where(lane == edge, 0.0, pltpu.roll(block, amount % LANES, 1)))
    return jnp.concatenate(blocks, axis=1)


def fill_columns(cols, planes, count):
    for x, plane in enumerate(planes):
        for j in range(count):
            cols[x, :, pl.ds(j * LANES, LANES)] = plane[32 * j : 32 * j + 48]


def stem_forward(weights, cols, i, keep):
    pre = nn(weights, cols[2 * i : 2 * i + 3].reshape(STEM_ROWS, cols.shape[2]))
    pre = jnp.concatenate([pre[0:32] + roll_blocks(pre[64:96], 1), pre[32:64]], axis=0)
    soft, sig = softplus_sigmoid(pre)
    act = (0.3 * pre + 0.7 * soft) * keep
    taps = jnp.concatenate([roll_blocks(act[32:64], 1), act], axis=0).astype(BF16)
    return (0.3 + 0.7 * sig) * keep, taps


def keep_space():
    return jnp.where(lax.axis_index("space") > 0, 1.0, 0.0).astype(F32)


def inner_kernel(own, slab_x, stem_w, place, weights, cols, slope, taps):
    weights[...] = jnp.concatenate([nn(stem_w[...], place[g]) for g in range(3)], axis=0).astype(BF16)
    planes = [slab_x[x, 16:256] if x < 3 else own[x - 3, 16:256] for x in range(7)]
    fill_columns(cols, planes, 7)
    for i in range(3):
        slope[i], taps[i] = stem_forward(weights[...], cols, i, keep_space() if i == 0 else 1.0)


def fill_taps(mid_cols, part, i, j, first, count):
    for b in range(3):
        if (j - b) % 2 == 0 and first <= (j - b) // 2 < first + count:
            row = 96 * (3 * i + b)
            mid_cols[row : row + 96, pl.ds(((j - b) // 2 - first) * LANES, LANES)] = part


def middle_cells_step(mid_w, mid_cols, cotangent):
    pre = nn(mid_w[:, 0:864], mid_cols[...])
    soft, sig = softplus_sigmoid(pre)
    delta = cotangent.astype(F32) * (0.3 + 0.7 * sig)
    delta_low = delta.astype(BF16)
    mid_grad = nt(delta_low, mid_cols[...])
    both = jnp.concatenate([delta_low, roll_blocks(delta, -1).astype(BF16)], axis=0)
    return (0.3 * pre + 0.7 * soft).astype(BF16), mid_grad, both


def put_back(target, i, start, part):
    lanes = pl.ds(start, LANES)
    target[i, 0:64, lanes] = part.astype(BF16)
    target[i, 64:96, lanes] = roll_blocks(part[0:32], -1).astype(BF16)


def upper_kernel(
    gathered, cols, slope, taps, features, mid_grad, stem_grad, mid_w, odd_w, even_w, mid_cols, stem_back,
):
    blocks = gathered.shape[0]
    for f in range(blocks):
        for t in range(7):
            mid_w[16 * f : 16 * f + 16, t * LANES : (t + 1) * LANES] = gathered[f, t]
    for i in range(3):
        for j in range(2, 9):
            fill_taps(mid_cols, taps[i, :, pl.ds((j - 2) * LANES, LANES)], i, j, 1, 3)
    cotangent = jnp.concatenate(
        [jnp.concatenate([gathered[f, 7 + j] for j in range(1, 4)], axis=1) for f in range(blocks)], axis=0
    )
    features[...], mid_grad[...], both = middle_cells_step(mid_w, mid_cols, cotangent)

    turned = jnp.concatenate(
        [mid_w[:, t * LANES : (t + 1) * LANES].astype(F32).T for t in range(7)], axis=0
    ).astype(BF16)
    zero = jnp.zeros((32, blocks * 16), BF16)

    def block(a, b, d):
        row = 32 * (9 * a + 3 * b + d)
        return turned[row : row + 32]

    def wide(a, b):
        even = jnp.concatenate([block(a, b, 1), zero], axis=1)
        odd = jnp.concatenate([block(a, b, 2), block(a, b, 0)], axis=1)
        return jnp.concatenate([even, odd], axis=0)

    odd_w[...] = jnp.concatenate([wide(i, 1) for i in range(3)], axis=0)
    even_w[...] = jnp.concatenate(
        [jnp.concatenate([wide(i, 0), wide(i, 2)], axis=1) for i in range(3)], axis=0
    )
    nothing = jnp.zeros((2 * blocks * 16, LANES), BF16)
    pair = jnp.concatenate(
        [jnp.concatenate([both, nothing], axis=1), jnp.concatenate([nothing, both], axis=1)], axis=0
    )
    odd_back = nn(odd_w[...], both)
    even_back = nn(even_w[...], pair)
    total = jnp.zeros((96, STEM_ROWS), F32)
    for i in range(3):
        for j in range(7):
            source = even_back if j % 2 == 0 else odd_back
            part = source[64 * i : 64 * i + 64, (j // 2) * LANES : (j // 2 + 1) * LANES]
            put_back(stem_back, i, j * LANES, part * slope[i, :, pl.ds(j * LANES, LANES)])
        total += nt(stem_back[i], cols[2 * i : 2 * i + 3].reshape(STEM_ROWS, 7 * LANES))
    stem_grad[...] = total


def lower_kernel(
    own, slab_x, border, place, gathered, weights, cols, slope, taps, upper_features, upper_mid, upper_stem,
    mid_w, odd_w, even_w, parts, low_cols, mid_cols, low_back,
):
    blocks = gathered.shape[0]
    keep_y = jnp.where(lax.axis_index("filt") > 0, 1.0, 0.0).astype(F32)
    planes = [
        jnp.concatenate([border[x], slab_x[x, 0:32] if x < 3 else own[x - 3, 0:32]], axis=0)
        for x in range(7)
    ]
    fill_columns(low_cols, planes, 2)
    low_slope = []
    for i in range(3):
        keep = jnp.where(lax.broadcasted_iota(jnp.int32, (64, 2 * LANES), 1) < LANES, keep_y, 1.0)
        if i == 0:
            keep = keep * keep_space()
        one_slope, low_taps = stem_forward(weights[...], low_cols, i, keep)
        low_slope.append(one_slope)
        for j in range(2):
            fill_taps(mid_cols, low_taps[:, j * LANES : (j + 1) * LANES], i, j, 0, 1)
        fill_taps(mid_cols, taps[i, :, 0:LANES], i, 2, 0, 1)
    cotangent = jnp.concatenate([gathered[f, 7] for f in range(blocks)], axis=0)
    features, mid_grad, both = middle_cells_step(mid_w, mid_cols, cotangent)

    back = [nn(even_w[:, 0:LANES], both), nn(odd_w[...], both), nn(even_w[:, LANES:], both)]
    stem_grad = upper_stem[...]
    for i in range(3):
        for j in range(2):
            part = back[j][64 * i : 64 * i + 64] * low_slope[i][:, j * LANES : (j + 1) * LANES]
            put_back(low_back, i, j * LANES, part)
        put_back(low_back, i, 2 * LANES, back[2][64 * i : 64 * i + 64] * slope[i, :, 0:LANES])
        low = low_cols[2 * i : 2 * i + 3].reshape(STEM_ROWS, 2 * LANES)
        near = cols[2 * i : 2 * i + 3, :, 0:LANES].reshape(STEM_ROWS, LANES)
        stem_grad += nt(low_back[i], jnp.concatenate([low, near], axis=1))
    high = stem_grad.astype(BF16)
    both = jnp.concatenate([high, (stem_grad - high.astype(F32)).astype(BF16)], axis=0)
    stem = 0.0
    for g in range(3):
        rows = jnp.concatenate([both[32 * g : 32 * g + 32], both[96 + 32 * g : 128 + 32 * g]], axis=0)
        taken = nt(rows, place[g])
        stem += taken[0:32] + taken[32:64]
    stem = stem.astype(BF16)

    middle = (mid_grad + upper_mid[...]).astype(BF16)
    middle = jnp.concatenate([middle, jnp.zeros((blocks * 16, 32), BF16)], axis=1)
    for f in range(blocks):
        rows = slice(16 * f, 16 * f + 16)
        for t in range(7):
            parts[f, t] = middle[rows, t * LANES : (t + 1) * LANES]
        for half in range(2):
            parts[f, 7 + half] = stem[16 * half : 16 * half + 16]
        parts[f, 9] = features[rows]
        for j in range(3):
            parts[f, 10 + j] = upper_features[rows, j * LANES : (j + 1) * LANES]


def sum_kernel(parts, sums):
    total = jnp.sum(parts[:, 0:9].astype(F32), axis=0).astype(BF16)
    for s in range(sums.shape[0]):
        sums[s] = total


def unpack_kernel(
    middle_scale, stem_scale, sums, parts, features_out, middle_out, stem_out, features, middle, stem, sems,
):
    copies = [
        pltpu.make_async_copy(source, target, sems.at[k])
        for k, (source, target) in enumerate(
            [(middle, middle_out), (stem, stem_out), (features, features_out)]
        )
    ]
    total = jnp.sum(sums[...].astype(F32), axis=0)
    for t in range(27):
        start = 32 * (t % 4)
        middle[t] = total[t // 4, :, start : start + 32] * middle_scale
    copies[0].start()
    rows = [parts[f, 9 + j] for f in range(parts.shape[0]) for j in range(4)]
    features[...] = nn(turn_matrix(), jnp.concatenate(rows, axis=0)).astype(BF16).reshape(16, 16, LANES)
    copies[2].start()
    turned = jnp.concatenate([total[7], total[8]], axis=0).T * stem_scale
    for t in range(27):
        stem[t] = turned[4 * t : 4 * t + 4]
    copies[1].start()
    for copy in copies:
        copy.wait()


def whole(count):
    return [pl.BlockSpec(memory_space=pltpu.VMEM)] * count


def body(volume, stem_weight, middle_weight, cotangent):
    spaces, filts = lax.axis_size("space"), lax.axis_size("filt")
    channels, planes, width, depth = volume.shape
    stem_cells = (planes // 2) * spaces * (width // 2) * filts * (depth // 2)
    middle_cells = stem_cells // 8
    limit = pltpu.CompilerParams(vmem_limit_bytes=48 * 1024 * 1024)

    raw = (volume, middle_weight.transpose(0, 2, 1), cotangent.reshape(16, 16, LANES))
    own, slab_x, packed = pl.pallas_call(
        regroup_kernel,
        out_shape=[
            jax.ShapeDtypeStruct((planes, 16 * width, LANES), BF16),
            jax.ShapeDtypeStruct((planes - 1, 16 * width, LANES), BF16),
            jax.ShapeDtypeStruct((filts, 11, 16, LANES), BF16),
        ],
        in_specs=[pl.BlockSpec(memory_space=pltpu.HBM)] * 3,
        out_specs=whole(2) + [pl.BlockSpec(memory_space=pl.ANY)],
        scratch_shapes=[
            pltpu.VMEM(volume.shape, BF16),
            pltpu.VMEM((27, 16, 32), BF16),
            pltpu.VMEM((16, 16, LANES), BF16),
            pltpu.VMEM((filts, 11, 16, LANES), BF16),
            pltpu.SemaphoreType.DMA((3 + channels,)),
        ],
        compiler_params=limit,
        name="regroup",
    )(*[pltpu.with_memory_space_constraint(x, pltpu.HBM) for x in raw])
    slab_x = lax.ppermute(slab_x, "space", [(s - 1, s) for s in range(1, spaces)])
    gathered = lax.all_to_all(packed, "filt", 0, 0, tiled=True)
    border = pl.pallas_call(
        border_kernel,
        out_shape=jax.ShapeDtypeStruct((7, 48, LANES), BF16),
        in_specs=whole(2),
        out_specs=whole(1)[0],
        compiler_params=limit,
        name="border",
    )(slab_x, own)
    border = lax.ppermute(border, "filt", [(f - 1, f) for f in range(1, filts)])

    stem_w = jnp.pad(stem_weight.reshape(108, 32).T, ((0, 0), (0, 20)))
    place = jnp.asarray(place_table(), BF16)
    weights, cols, slope, taps = pl.pallas_call(
        inner_kernel,
        out_shape=[
            jax.ShapeDtypeStruct((96, STEM_ROWS), BF16),
            jax.ShapeDtypeStruct((7, 48, 7 * LANES), BF16),
            jax.ShapeDtypeStruct((3, 64, 7 * LANES), F32),
            jax.ShapeDtypeStruct((3, 96, 7 * LANES), BF16),
        ],
        in_specs=whole(4),
        out_specs=whole(4),
        compiler_params=limit,
        cost_estimate=pl.CostEstimate(flops=200_000_000, bytes_accessed=4_000_000, transcendentals=500_000),
        name="stem_inner",
    )(own, slab_x, stem_w, place)
    upper = pl.pallas_call(
        upper_kernel,
        out_shape=[
            jax.ShapeDtypeStruct((64, 3 * LANES), BF16),
            jax.ShapeDtypeStruct((64, 864), F32),
            jax.ShapeDtypeStruct((96, STEM_ROWS), F32),
            jax.ShapeDtypeStruct((64, 896), BF16),
            jax.ShapeDtypeStruct((192, LANES), BF16),
            jax.ShapeDtypeStruct((192, 2 * LANES), BF16),
        ],
        in_specs=whole(4),
        out_specs=whole(6),
        scratch_shapes=[
            pltpu.VMEM((864, 3 * LANES), BF16),
            pltpu.VMEM((3, 96, 7 * LANES), BF16),
        ],
        compiler_params=limit,
        name="upper_cells",
    )(gathered, cols, slope, taps)
    parts = pl.pallas_call(
        lower_kernel,
        out_shape=jax.ShapeDtypeStruct((filts, 13, 16, LANES), BF16),
        in_specs=whole(15),
        out_specs=whole(1)[0],
        scratch_shapes=[
            pltpu.VMEM((7, 48, 2 * LANES), BF16),
            pltpu.VMEM((864, LANES), BF16),
            pltpu.VMEM((3, 96, 3 * LANES), BF16),
        ],
        compiler_params=limit,
        cost_estimate=pl.CostEstimate(flops=600_000_000, bytes_accessed=8_000_000, transcendentals=500_000),
        name="lower_cells",
    )(own, slab_x, border, place, gathered, weights, cols, slope, taps, *upper)

    parts = lax.all_to_all(parts, "filt", 0, 0, tiled=True)
    sums = pl.pallas_call(
        sum_kernel,
        out_shape=jax.ShapeDtypeStruct((spaces, 9, 16, LANES), BF16),
        in_specs=whole(1),
        out_specs=whole(1)[0],
        compiler_params=limit,
        name="sums",
    )(parts)
    sums = lax.all_to_all(sums, "space", 0, 0, tiled=True)
    features, middle, stem = pl.pallas_call(
        functools.partial(unpack_kernel, middle_cells**-0.5, stem_cells**-0.5),
        out_shape=[
            jax.ShapeDtypeStruct((16, 16, LANES), BF16),
            jax.ShapeDtypeStruct((27, 16, 32), F32),
            jax.ShapeDtypeStruct((27, 4, 32), F32),
        ],
        in_specs=whole(2),
        out_specs=[pl.BlockSpec(memory_space=pl.ANY)] * 3,
        scratch_shapes=[
            pltpu.VMEM((16, 16, LANES), BF16),
            pltpu.VMEM((27, 16, 32), F32),
            pltpu.VMEM((27, 4, 32), F32),
            pltpu.SemaphoreType.DMA((3,)),
        ],
        compiler_params=limit,
        name="unpack",
    )(sums, parts)
    return features.reshape(16, 1, 16, LANES), middle.transpose(0, 2, 1), stem


def solution(mesh):
    in_specs = (
        P(None, "space", "filt", None),
        P(),
        P(None, None, "filt"),
        P("filt", "space", None, None),
    )
    out_specs = (P("filt", "space", None, None), P(None, None, "filt"), P())
    return jax.shard_map(body, mesh=mesh, in_specs=in_specs, out_specs=out_specs, check_vma=False)
```

```python
import functools

import jax
import jax.numpy as jnp
import numpy as np
from jax import lax
from jax.experimental import pallas as pl
from jax.experimental.pallas import tpu as pltpu
from jax.sharding import PartitionSpec as P

F32 = jnp.float32
BF16 = jnp.bfloat16
LANES = 128
STEM_ROWS = 144


def nn(a, b):
    return lax.dot_general(a, b, (((1,), (0,)), ((), ())), preferred_element_type=F32)


def nt(a, b):
    return lax.dot_general(a, b, (((1,), (1,)), ((), ())), preferred_element_type=F32)


def place_table():
    table = np.zeros((3, LANES, STEM_ROWS), np.float32)
    for even_odd in range(2):
        for a in range(3):
            for b in range(3):
                for d in range(3):
                    q = 2 * even_odd + d - 1
                    group, phase = (2, 3) if q < 0 else (even_odd, q)
                    for c in range(4):
                        column = 48 * a + 16 * b + 4 * phase + c
                        table[group, 4 * (9 * a + 3 * b + d) + c, column] = 1.0
    return table


def rows_lanes(shape):
    return lax.broadcasted_iota(jnp.int32, shape, 0), lax.broadcasted_iota(jnp.int32, shape, 1)


def turn_matrix():
    row, column = rows_lanes((256, 256))
    source = lax.shift_left(row & 15, 4) + lax.shift_right_logical(row, 4)
    return (source == column).astype(F32).astype(BF16)


def regroup_kernel(volume_in, weight_in, cotangent_in, own, slab_x, packed_out, volume, weight, cotangent, packed, sems):
    channels, planes, width, depth = volume.shape
    pairs = [(weight_in, weight), (cotangent_in, cotangent), (packed, packed_out)]
    pairs += [(volume_in.at[c], volume.at[c]) for c in range(channels)]
    copies = [pltpu.make_async_copy(*pair, sems.at[k]) for k, pair in enumerate(pairs)]
    for copy in copies[:2] + copies[3:]:
        copy.start()
    z, column = rows_lanes((depth, depth))
    source = lax.shift_left(column & (LANES - 1), 2) + lax.shift_right_logical(column, 7)
    select = (z == source).astype(F32).astype(BF16)
    turn = turn_matrix()

    blank = jnp.zeros((16, 32), BF16)
    copies[0].wait()
    taps = [weight[t] if t < 27 else blank for t in range(28)]
    for t in range(7):
        tile = jnp.concatenate(taps[4 * t : 4 * t + 4], axis=1)
        for f in range(packed.shape[0]):
            packed[f, t] = tile
    copies[1].wait()
    turned = nn(turn, cotangent[...].reshape(256, LANES)).astype(BF16)
    for f in range(packed.shape[0]):
        for j in range(4):
            row = 16 * (4 * f + j)
            packed[f, 7 + j] = turned[row : row + 16]
    copies[2].start()

    for copy in copies[3:]:
        copy.wait()
    picked = nn(volume[...].reshape(channels * planes * width, depth), select).astype(BF16)
    grouped = []
    for x in range(planes):
        parts = []
        for phase in range(4):
            for c in range(channels):
                start = (c * planes + x) * width
                parts.append(picked[start : start + width, phase * LANES : (phase + 1) * LANES])
        grouped.append(jnp.concatenate(parts, axis=0))
    turned = nn(turn, jnp.concatenate(grouped, axis=1)).astype(BF16)
    for x in range(planes):
        plane = turned[:, x * LANES : (x + 1) * LANES]
        own[x] = plane
        if x > 0:
            slab_x[x - 1] = plane
    copies[2].wait()


def border_kernel(slab_x, own, border):
    for x in range(3):
        border[x] = slab_x[x, -48:]
    for x in range(4):
        border[3 + x] = own[x, -48:]


def softplus_sigmoid(values):
    small = jnp.exp(-jnp.abs(values))
    inverse = 1.0 / (1.0 + small)
    soft = jnp.maximum(values, 0.0) + jnp.log(1.0 + small)
    return soft, jnp.where(values >= 0.0, inverse, small * inverse)


def roll_blocks(values, amount):
    blocks = []
    for start in range(0, values.shape[1], LANES):
        block = values[:, start : start + LANES]
        lane = lax.broadcasted_iota(jnp.int32, block.shape, 1)
        edge = 0 if amount == 1 else LANES - 1
        blocks.append(jnp.where(lane == edge, 0.0, pltpu.roll(block, amount % LANES, 1)))
    return jnp.concatenate(blocks, axis=1)


def fill_columns(cols, planes, count):
    for x, plane in enumerate(planes):
        for j in range(count):
            cols[x, :, pl.ds(j * LANES, LANES)] = plane[32 * j : 32 * j + 48]


def stem_forward(weights, cols, i, keep):
    pre = nn(weights, cols[2 * i : 2 * i + 3].reshape(STEM_ROWS, cols.shape[2]))
    pre = jnp.concatenate([pre[0:32] + roll_blocks(pre[64:96], 1), pre[32:64]], axis=0)
    soft, sig = softplus_sigmoid(pre)
    act = (0.3 * pre + 0.7 * soft) * keep
    taps = jnp.concatenate([roll_blocks(act[32:64], 1), act], axis=0).astype(BF16)
    return (0.3 + 0.7 * sig) * keep, taps


def keep_space():
    return jnp.where(lax.axis_index("space") > 0, 1.0, 0.0).astype(F32)


def inner_kernel(own, slab_x, stem_w, place, weights, cols, slope, taps):
    weights[...] = jnp.concatenate([nn(stem_w[...], place[g]) for g in range(3)], axis=0).astype(BF16)
    planes = [slab_x[x, 16:256] if x < 3 else own[x - 3, 16:256] for x in range(7)]
    fill_columns(cols, planes, 7)
    for i in range(3):
        slope[i], taps[i] = stem_forward(weights[...], cols, i, keep_space() if i == 0 else 1.0)


def fill_taps(mid_cols, part, i, j, first, count):
    for b in range(3):
        if (j - b) % 2 == 0 and first <= (j - b) // 2 < first + count:
            row = 96 * (3 * i + b)
            mid_cols[row : row + 96, pl.ds(((j - b) // 2 - first) * LANES, LANES)] = part


def middle_cells_step(mid_w, mid_cols, cotangent):
    pre = nn(mid_w[:, 0:864], mid_cols[...])
    soft, sig = softplus_sigmoid(pre)
    delta = cotangent.astype(F32) * (0.3 + 0.7 * sig)
    delta_low = delta.astype(BF16)
    mid_grad = nt(delta_low, mid_cols[...])
    both = jnp.concatenate([delta_low, roll_blocks(delta, -1).astype(BF16)], axis=0)
    return (0.3 * pre + 0.7 * soft).astype(BF16), mid_grad, both


def put_back(target, i, start, part):
    lanes = pl.ds(start, LANES)
    target[i, 0:64, lanes] = part.astype(BF16)
    target[i, 64:96, lanes] = roll_blocks(part[0:32], -1).astype(BF16)


def upper_kernel(
    gathered, cols, slope, taps, features, mid_grad, stem_grad, mid_w, odd_w, even_w, mid_cols, stem_back,
):
    blocks = gathered.shape[0]
    for f in range(blocks):
        for t in range(7):
            mid_w[16 * f : 16 * f + 16, t * LANES : (t + 1) * LANES] = gathered[f, t]
    for i in range(3):
        for j in range(2, 9):
            fill_taps(mid_cols, taps[i, :, pl.ds((j - 2) * LANES, LANES)], i, j, 1, 3)
    cotangent = jnp.concatenate(
        [jnp.concatenate([gathered[f, 7 + j] for j in range(1, 4)], axis=1) for f in range(blocks)], axis=0
    )
    features[...], mid_grad[...], both = middle_cells_step(mid_w, mid_cols, cotangent)

    turned = jnp.concatenate(
        [mid_w[:, t * LANES : (t + 1) * LANES].astype(F32).T for t in range(7)], axis=0
    ).astype(BF16)
    zero = jnp.zeros((32, blocks * 16), BF16)

    def block(a, b, d):
        row = 32 * (9 * a + 3 * b + d)
        return turned[row : row + 32]

    def wide(a, b):
        even = jnp.concatenate([block(a, b, 1), zero], axis=1)
        odd = jnp.concatenate([block(a, b, 2), block(a, b, 0)], axis=1)
        return jnp.concatenate([even, odd], axis=0)

    odd_w[...] = jnp.concatenate([wide(i, 1) for i in range(3)], axis=0)
    even_w[...] = jnp.concatenate(
        [jnp.concatenate([wide(i, 0), wide(i, 2)], axis=1) for i in range(3)], axis=0
    )
    nothing = jnp.zeros((2 * blocks * 16, LANES), BF16)
    pair = jnp.concatenate(
        [jnp.concatenate([both, nothing], axis=1), jnp.concatenate([nothing, both], axis=1)], axis=0
    )
    odd_back = nn(odd_w[...], both)
    even_back = nn(even_w[...], pair)
    total = jnp.zeros((96, STEM_ROWS), F32)
    for i in range(3):
        for j in range(7):
            source = even_back if j % 2 == 0 else odd_back
            part = source[64 * i : 64 * i + 64, (j // 2) * LANES : (j // 2 + 1) * LANES]
            put_back(stem_back, i, j * LANES, part * slope[i, :, pl.ds(j * LANES, LANES)])
        total += nt(stem_back[i], cols[2 * i : 2 * i + 3].reshape(STEM_ROWS, 7 * LANES))
    stem_grad[...] = total


def lower_kernel(
    own, slab_x, border, place, gathered, weights, cols, slope, taps, upper_features, upper_mid, upper_stem,
    mid_w, odd_w, even_w, parts, low_cols, mid_cols, low_back,
):
    blocks = gathered.shape[0]
    keep_y = jnp.where(lax.axis_index("filt") > 0, 1.0, 0.0).astype(F32)
    planes = [
        jnp.concatenate([border[x], slab_x[x, 0:32] if x < 3 else own[x - 3, 0:32]], axis=0)
        for x in range(7)
    ]
    fill_columns(low_cols, planes, 2)
    low_slope = []
    for i in range(3):
        keep = jnp.where(lax.broadcasted_iota(jnp.int32, (64, 2 * LANES), 1) < LANES, keep_y, 1.0)
        if i == 0:
            keep = keep * keep_space()
        one_slope, low_taps = stem_forward(weights[...], low_cols, i, keep)
        low_slope.append(one_slope)
        for j in range(2):
            fill_taps(mid_cols, low_taps[:, j * LANES : (j + 1) * LANES], i, j, 0, 1)
        fill_taps(mid_cols, taps[i, :, 0:LANES], i, 2, 0, 1)
    cotangent = jnp.concatenate([gathered[f, 7] for f in range(blocks)], axis=0)
    features, mid_grad, both = middle_cells_step(mid_w, mid_cols, cotangent)

    back = [nn(even_w[:, 0:LANES], both), nn(odd_w[...], both), nn(even_w[:, LANES:], both)]
    stem_grad = upper_stem[...]
    for i in range(3):
        for j in range(2):
            part = back[j][64 * i : 64 * i + 64] * low_slope[i][:, j * LANES : (j + 1) * LANES]
            put_back(low_back, i, j * LANES, part)
        put_back(low_back, i, 2 * LANES, back[2][64 * i : 64 * i + 64] * slope[i, :, 0:LANES])
        low = low_cols[2 * i : 2 * i + 3].reshape(STEM_ROWS, 2 * LANES)
        near = cols[2 * i : 2 * i + 3, :, 0:LANES].reshape(STEM_ROWS, LANES)
        stem_grad += nt(low_back[i], jnp.concatenate([low, near], axis=1))
    high = stem_grad.astype(BF16)
    both = jnp.concatenate([high, (stem_grad - high.astype(F32)).astype(BF16)], axis=0)
    stem = 0.0
    for g in range(3):
        rows = jnp.concatenate([both[32 * g : 32 * g + 32], both[96 + 32 * g : 128 + 32 * g]], axis=0)
        taken = nt(rows, place[g])
        stem += taken[0:32] + taken[32:64]
    stem = stem.astype(BF16)

    middle = (mid_grad + upper_mid[...]).astype(BF16)
    middle = jnp.concatenate([middle, jnp.zeros((blocks * 16, 32), BF16)], axis=1)
    for f in range(blocks):
        rows = slice(16 * f, 16 * f + 16)
        for t in range(7):
            parts[f, t] = middle[rows, t * LANES : (t + 1) * LANES]
        for half in range(2):
            parts[f, 7 + half] = stem[16 * half : 16 * half + 16]
        parts[f, 9] = features[rows]
        for j in range(3):
            parts[f, 10 + j] = upper_features[rows, j * LANES : (j + 1) * LANES]


def sum_kernel(parts, sums):
    sums[...] = jnp.sum(parts[:, 0:9].astype(F32), axis=0).astype(BF16)


def unpack_kernel(
    middle_scale, stem_scale, sums, parts, features_out, middle_out, stem_out, features, middle, stem, sems,
):
    copies = [
        pltpu.make_async_copy(source, target, sems.at[k])
        for k, (source, target) in enumerate(
            [(middle, middle_out), (stem, stem_out), (features, features_out)]
        )
    ]
    total = jnp.sum(sums[...].astype(F32), axis=0)
    for t in range(27):
        start = 32 * (t % 4)
        middle[t] = total[t // 4, :, start : start + 32] * middle_scale
    copies[0].start()
    rows = [parts[f, 9 + j] for f in range(parts.shape[0]) for j in range(4)]
    features[...] = nn(turn_matrix(), jnp.concatenate(rows, axis=0)).astype(BF16).reshape(16, 16, LANES)
    copies[2].start()
    turned = jnp.concatenate([total[7], total[8]], axis=0).T * stem_scale
    for t in range(27):
        stem[t] = turned[4 * t : 4 * t + 4]
    copies[1].start()
    for copy in copies:
        copy.wait()


def whole(count):
    return [pl.BlockSpec(memory_space=pltpu.VMEM)] * count


def body(volume, stem_weight, middle_weight, cotangent):
    spaces, filts = lax.axis_size("space"), lax.axis_size("filt")
    channels, planes, width, depth = volume.shape
    stem_cells = (planes // 2) * spaces * (width // 2) * filts * (depth // 2)
    middle_cells = stem_cells // 8
    limit = pltpu.CompilerParams(vmem_limit_bytes=48 * 1024 * 1024)

    raw = (volume, middle_weight.transpose(0, 2, 1), cotangent.reshape(16, 16, LANES))
    own, slab_x, packed = pl.pallas_call(
        regroup_kernel,
        out_shape=[
            jax.ShapeDtypeStruct((planes, 16 * width, LANES), BF16),
            jax.ShapeDtypeStruct((planes - 1, 16 * width, LANES), BF16),
            jax.ShapeDtypeStruct((filts, 11, 16, LANES), BF16),
        ],
        in_specs=[pl.BlockSpec(memory_space=pltpu.HBM)] * 3,
        out_specs=whole(2) + [pl.BlockSpec(memory_space=pl.ANY)],
        scratch_shapes=[
            pltpu.VMEM(volume.shape, BF16),
            pltpu.VMEM((27, 16, 32), BF16),
            pltpu.VMEM((16, 16, LANES), BF16),
            pltpu.VMEM((filts, 11, 16, LANES), BF16),
            pltpu.SemaphoreType.DMA((3 + channels,)),
        ],
        compiler_params=limit,
        name="regroup",
    )(*[pltpu.with_memory_space_constraint(x, pltpu.HBM) for x in raw])
    slab_x = lax.ppermute(slab_x, "space", [(s - 1, s) for s in range(1, spaces)])
    gathered = lax.all_to_all(packed, "filt", 0, 0, tiled=True)
    border = pl.pallas_call(
        border_kernel,
        out_shape=jax.ShapeDtypeStruct((7, 48, LANES), BF16),
        in_specs=whole(2),
        out_specs=whole(1)[0],
        compiler_params=limit,
        name="border",
    )(slab_x, own)
    border = lax.ppermute(border, "filt", [(f - 1, f) for f in range(1, filts)])

    stem_w = jnp.pad(stem_weight.reshape(108, 32).T, ((0, 0), (0, 20)))
    place = jnp.asarray(place_table(), BF16)
    weights, cols, slope, taps = pl.pallas_call(
        inner_kernel,
        out_shape=[
            jax.ShapeDtypeStruct((96, STEM_ROWS), BF16),
            jax.ShapeDtypeStruct((7, 48, 7 * LANES), BF16),
            jax.ShapeDtypeStruct((3, 64, 7 * LANES), F32),
            jax.ShapeDtypeStruct((3, 96, 7 * LANES), BF16),
        ],
        in_specs=whole(4),
        out_specs=whole(4),
        compiler_params=limit,
        cost_estimate=pl.CostEstimate(flops=200_000_000, bytes_accessed=4_000_000, transcendentals=500_000),
        name="stem_inner",
    )(own, slab_x, stem_w, place)
    upper = pl.pallas_call(
        upper_kernel,
        out_shape=[
            jax.ShapeDtypeStruct((64, 3 * LANES), BF16),
            jax.ShapeDtypeStruct((64, 864), F32),
            jax.ShapeDtypeStruct((96, STEM_ROWS), F32),
            jax.ShapeDtypeStruct((64, 896), BF16),
            jax.ShapeDtypeStruct((192, LANES), BF16),
            jax.ShapeDtypeStruct((192, 2 * LANES), BF16),
        ],
        in_specs=whole(4),
        out_specs=whole(6),
        scratch_shapes=[
            pltpu.VMEM((864, 3 * LANES), BF16),
            pltpu.VMEM((3, 96, 7 * LANES), BF16),
        ],
        compiler_params=limit,
        name="upper_cells",
    )(gathered, cols, slope, taps)
    parts = pl.pallas_call(
        lower_kernel,
        out_shape=jax.ShapeDtypeStruct((filts, 13, 16, LANES), BF16),
        in_specs=whole(15),
        out_specs=whole(1)[0],
        scratch_shapes=[
            pltpu.VMEM((7, 48, 2 * LANES), BF16),
            pltpu.VMEM((864, LANES), BF16),
            pltpu.VMEM((3, 96, 3 * LANES), BF16),
        ],
        compiler_params=limit,
        cost_estimate=pl.CostEstimate(flops=600_000_000, bytes_accessed=8_000_000, transcendentals=500_000),
        name="lower_cells",
    )(own, slab_x, border, place, gathered, weights, cols, slope, taps, *upper)

    parts = lax.all_to_all(parts, "filt", 0, 0, tiled=True)
    sums = pl.pallas_call(
        sum_kernel,
        out_shape=jax.ShapeDtypeStruct((9, 16, LANES), BF16),
        in_specs=whole(1),
        out_specs=whole(1)[0],
        compiler_params=limit,
        name="sums",
    )(parts)
    sums = lax.all_gather(sums, "space")
    features, middle, stem = pl.pallas_call(
        functools.partial(unpack_kernel, middle_cells**-0.5, stem_cells**-0.5),
        out_shape=[
            jax.ShapeDtypeStruct((16, 16, LANES), BF16),
            jax.ShapeDtypeStruct((27, 16, 32), F32),
            jax.ShapeDtypeStruct((27, 4, 32), F32),
        ],
        in_specs=whole(2),
        out_specs=[pl.BlockSpec(memory_space=pl.ANY)] * 3,
        scratch_shapes=[
            pltpu.VMEM((16, 16, LANES), BF16),
            pltpu.VMEM((27, 16, 32), F32),
            pltpu.VMEM((27, 4, 32), F32),
            pltpu.SemaphoreType.DMA((3,)),
        ],
        compiler_params=limit,
        name="unpack",
    )(sums, parts)
    return features.reshape(16, 1, 16, LANES), middle.transpose(0, 2, 1), stem


def solution(mesh):
    in_specs = (
        P(None, "space", "filt", None),
        P(),
        P(None, None, "filt"),
        P("filt", "space", None, None),
    )
    out_specs = (P("filt", "space", None, None), P(None, None, "filt"), P())
    return jax.shard_map(body, mesh=mesh, in_specs=in_specs, out_specs=out_specs, check_vma=False)
```

```python
import functools

import jax
import jax.numpy as jnp
import numpy as np
from jax import lax
from jax.experimental import pallas as pl
from jax.experimental.pallas import tpu as pltpu
from jax.sharding import PartitionSpec as P

F32 = jnp.float32
BF16 = jnp.bfloat16
LANES = 128
STEM_ROWS = 144


def nn(a, b):
    return lax.dot_general(a, b, (((1,), (0,)), ((), ())), preferred_element_type=F32)


def nt(a, b):
    return lax.dot_general(a, b, (((1,), (1,)), ((), ())), preferred_element_type=F32)


def place_table():
    table = np.zeros((3, LANES, STEM_ROWS), np.float32)
    for even_odd in range(2):
        for a in range(3):
            for b in range(3):
                for d in range(3):
                    q = 2 * even_odd + d - 1
                    group, phase = (2, 3) if q < 0 else (even_odd, q)
                    for c in range(4):
                        column = 48 * a + 16 * b + 4 * phase + c
                        table[group, 4 * (9 * a + 3 * b + d) + c, column] = 1.0
    return table


def rows_lanes(shape):
    return lax.broadcasted_iota(jnp.int32, shape, 0), lax.broadcasted_iota(jnp.int32, shape, 1)


def turn_matrix():
    row, column = rows_lanes((256, 256))
    source = lax.shift_left(row & 15, 4) + lax.shift_right_logical(row, 4)
    return (source == column).astype(F32).astype(BF16)


def regroup_kernel(volume_in, weight_in, cotangent_in, own, slab_x, packed_out, volume, weight, cotangent, packed, sems):
    channels, planes, width, depth = volume.shape
    pairs = [(weight_in, weight), (cotangent_in, cotangent), (packed, packed_out)]
    pairs += [(volume_in.at[c], volume.at[c]) for c in range(channels)]
    copies = [pltpu.make_async_copy(*pair, sems.at[k]) for k, pair in enumerate(pairs)]
    for copy in copies[:2] + copies[3:]:
        copy.start()
    z, column = rows_lanes((depth, depth))
    source = lax.shift_left(column & (LANES - 1), 2) + lax.shift_right_logical(column, 7)
    select = (z == source).astype(F32).astype(BF16)
    turn = turn_matrix()

    blank = jnp.zeros((16, 32), BF16)
    copies[0].wait()
    taps = [weight[t] if t < 27 else blank for t in range(28)]
    for t in range(7):
        tile = jnp.concatenate(taps[4 * t : 4 * t + 4], axis=1)
        for f in range(packed.shape[0]):
            packed[f, t] = tile
    copies[1].wait()
    turned = nn(turn, cotangent[...].reshape(256, LANES)).astype(BF16)
    for k, f in enumerate(exchange_order(packed.shape[0])):
        for j in range(4):
            row = 16 * (4 * f + j)
            packed[k, 7 + j] = turned[row : row + 16]
    copies[2].start()

    for copy in copies[3:]:
        copy.wait()
    picked = nn(volume[...].reshape(channels * planes * width, depth), select).astype(BF16)
    grouped = []
    for x in range(planes):
        parts = []
        for phase in range(4):
            for c in range(channels):
                start = (c * planes + x) * width
                parts.append(picked[start : start + width, phase * LANES : (phase + 1) * LANES])
        grouped.append(jnp.concatenate(parts, axis=0))
    turned = nn(turn, jnp.concatenate(grouped, axis=1)).astype(BF16)
    for x in range(planes):
        plane = turned[:, x * LANES : (x + 1) * LANES]
        own[x] = plane
        if x > 0:
            slab_x[x - 1] = plane
    copies[2].wait()


def border_kernel(slab_x, own, border):
    for x in range(3):
        border[x] = slab_x[x, -48:]
    for x in range(4):
        border[3 + x] = own[x, -48:]


def softplus_sigmoid(values):
    small = jnp.exp(-jnp.abs(values))
    inverse = 1.0 / (1.0 + small)
    soft = jnp.maximum(values, 0.0) + jnp.log(1.0 + small)
    return soft, jnp.where(values >= 0.0, inverse, small * inverse)


def roll_blocks(values, amount):
    blocks = []
    for start in range(0, values.shape[1], LANES):
        block = values[:, start : start + LANES]
        lane = lax.broadcasted_iota(jnp.int32, block.shape, 1)
        edge = 0 if amount == 1 else LANES - 1
        blocks.append(jnp.where(lane == edge, 0.0, pltpu.roll(block, amount % LANES, 1)))
    return jnp.concatenate(blocks, axis=1)


def fill_columns(cols, planes, count):
    for x, plane in enumerate(planes):
        for j in range(count):
            cols[x, :, pl.ds(j * LANES, LANES)] = plane[32 * j : 32 * j + 48]


def stem_forward(weights, cols, i, keep):
    pre = nn(weights, cols[2 * i : 2 * i + 3].reshape(STEM_ROWS, cols.shape[2]))
    pre = jnp.concatenate([pre[0:32] + roll_blocks(pre[64:96], 1), pre[32:64]], axis=0)
    soft, sig = softplus_sigmoid(pre)
    act = (0.3 * pre + 0.7 * soft) * keep
    taps = jnp.concatenate([roll_blocks(act[32:64], 1), act], axis=0).astype(BF16)
    return (0.3 + 0.7 * sig) * keep, taps


def keep_space():
    return jnp.where(lax.axis_index("space") > 0, 1.0, 0.0).astype(F32)


def inner_kernel(own, slab_x, stem_w, place, weights, cols, slope, taps):
    weights[...] = jnp.concatenate([nn(stem_w[...], place[g]) for g in range(3)], axis=0).astype(BF16)
    planes = [slab_x[x, 16:256] if x < 3 else own[x - 3, 16:256] for x in range(7)]
    fill_columns(cols, planes, 7)
    for i in range(3):
        slope[i], taps[i] = stem_forward(weights[...], cols, i, keep_space() if i == 0 else 1.0)


def fill_taps(mid_cols, part, i, j, first, count):
    for b in range(3):
        if (j - b) % 2 == 0 and first <= (j - b) // 2 < first + count:
            row = 96 * (3 * i + b)
            mid_cols[row : row + 96, pl.ds(((j - b) // 2 - first) * LANES, LANES)] = part


def middle_cells_step(mid_w, mid_cols, cotangent):
    pre = nn(mid_w[:, 0:864], mid_cols[...])
    soft, sig = softplus_sigmoid(pre)
    delta = cotangent.astype(F32) * (0.3 + 0.7 * sig)
    delta_low = delta.astype(BF16)
    mid_grad = nt(delta_low, mid_cols[...])
    both = jnp.concatenate([delta_low, roll_blocks(delta, -1).astype(BF16)], axis=0)
    return (0.3 * pre + 0.7 * soft).astype(BF16), mid_grad, both


def put_back(target, i, start, part):
    lanes = pl.ds(start, LANES)
    target[i, 0:64, lanes] = part.astype(BF16)
    target[i, 64:96, lanes] = roll_blocks(part[0:32], -1).astype(BF16)


def upper_kernel(
    gathered, cols, slope, taps, features, mid_grad, stem_grad, mid_w, odd_w, even_w, mid_cols, stem_back,
):
    blocks = gathered.shape[0]
    order = exchange_order(blocks)
    for k, f in enumerate(order):
        for t in range(7):
            mid_w[16 * f : 16 * f + 16, t * LANES : (t + 1) * LANES] = gathered[k, t]
    for i in range(3):
        for j in range(2, 9):
            fill_taps(mid_cols, taps[i, :, pl.ds((j - 2) * LANES, LANES)], i, j, 1, 3)
    cotangent = jnp.concatenate(
        [jnp.concatenate([gathered[order.index(f), 7 + j] for j in range(1, 4)], axis=1) for f in range(blocks)],
        axis=0,
    )
    features[...], mid_grad[...], both = middle_cells_step(mid_w, mid_cols, cotangent)

    turned = jnp.concatenate(
        [mid_w[:, t * LANES : (t + 1) * LANES].astype(F32).T for t in range(7)], axis=0
    ).astype(BF16)
    zero = jnp.zeros((32, blocks * 16), BF16)

    def block(a, b, d):
        row = 32 * (9 * a + 3 * b + d)
        return turned[row : row + 32]

    def wide(a, b):
        even = jnp.concatenate([block(a, b, 1), zero], axis=1)
        odd = jnp.concatenate([block(a, b, 2), block(a, b, 0)], axis=1)
        return jnp.concatenate([even, odd], axis=0)

    odd_w[...] = jnp.concatenate([wide(i, 1) for i in range(3)], axis=0)
    even_w[...] = jnp.concatenate(
        [jnp.concatenate([wide(i, 0), wide(i, 2)], axis=1) for i in range(3)], axis=0
    )
    nothing = jnp.zeros((2 * blocks * 16, LANES), BF16)
    pair = jnp.concatenate(
        [jnp.concatenate([both, nothing], axis=1), jnp.concatenate([nothing, both], axis=1)], axis=0
    )
    odd_back = nn(odd_w[...], both)
    even_back = nn(even_w[...], pair)
    total = jnp.zeros((96, STEM_ROWS), F32)
    for i in range(3):
        for j in range(7):
            source = even_back if j % 2 == 0 else odd_back
            part = source[64 * i : 64 * i + 64, (j // 2) * LANES : (j // 2 + 1) * LANES]
            put_back(stem_back, i, j * LANES, part * slope[i, :, pl.ds(j * LANES, LANES)])
        total += nt(stem_back[i], cols[2 * i : 2 * i + 3].reshape(STEM_ROWS, 7 * LANES))
    stem_grad[...] = total


def lower_kernel(
    own, slab_x, border, place, gathered, weights, cols, slope, taps, upper_features, upper_mid, upper_stem,
    mid_w, odd_w, even_w, parts, low_cols, mid_cols, low_back,
):
    blocks = gathered.shape[0]
    keep_y = jnp.where(lax.axis_index("filt") > 0, 1.0, 0.0).astype(F32)
    planes = [
        jnp.concatenate([border[x], slab_x[x, 0:32] if x < 3 else own[x - 3, 0:32]], axis=0)
        for x in range(7)
    ]
    fill_columns(low_cols, planes, 2)
    low_slope = []
    for i in range(3):
        keep = jnp.where(lax.broadcasted_iota(jnp.int32, (64, 2 * LANES), 1) < LANES, keep_y, 1.0)
        if i == 0:
            keep = keep * keep_space()
        one_slope, low_taps = stem_forward(weights[...], low_cols, i, keep)
        low_slope.append(one_slope)
        for j in range(2):
            fill_taps(mid_cols, low_taps[:, j * LANES : (j + 1) * LANES], i, j, 0, 1)
        fill_taps(mid_cols, taps[i, :, 0:LANES], i, 2, 0, 1)
    order = exchange_order(blocks)
    cotangent = jnp.concatenate([gathered[order.index(f), 7] for f in range(blocks)], axis=0)
    features, mid_grad, both = middle_cells_step(mid_w, mid_cols, cotangent)

    back = [nn(even_w[:, 0:LANES], both), nn(odd_w[...], both), nn(even_w[:, LANES:], both)]
    stem_grad = upper_stem[...]
    for i in range(3):
        for j in range(2):
            part = back[j][64 * i : 64 * i + 64] * low_slope[i][:, j * LANES : (j + 1) * LANES]
            put_back(low_back, i, j * LANES, part)
        put_back(low_back, i, 2 * LANES, back[2][64 * i : 64 * i + 64] * slope[i, :, 0:LANES])
        low = low_cols[2 * i : 2 * i + 3].reshape(STEM_ROWS, 2 * LANES)
        near = cols[2 * i : 2 * i + 3, :, 0:LANES].reshape(STEM_ROWS, LANES)
        stem_grad += nt(low_back[i], jnp.concatenate([low, near], axis=1))
    high = stem_grad.astype(BF16)
    both = jnp.concatenate([high, (stem_grad - high.astype(F32)).astype(BF16)], axis=0)
    stem = 0.0
    for g in range(3):
        rows = jnp.concatenate([both[32 * g : 32 * g + 32], both[96 + 32 * g : 128 + 32 * g]], axis=0)
        taken = nt(rows, place[g])
        stem += taken[0:32] + taken[32:64]
    stem = stem.astype(BF16)

    middle = (mid_grad + upper_mid[...]).astype(BF16)
    middle = jnp.concatenate([middle, jnp.zeros((blocks * 16, 32), BF16)], axis=1)
    for k, f in enumerate(order):
        rows = slice(16 * f, 16 * f + 16)
        for t in range(7):
            parts[k, t] = middle[rows, t * LANES : (t + 1) * LANES]
        for half in range(2):
            parts[k, 7 + half] = stem[16 * half : 16 * half + 16]
        parts[k, 9] = features[rows]
        for j in range(3):
            parts[k, 10 + j] = upper_features[rows, j * LANES : (j + 1) * LANES]


def sum_kernel(parts, sums):
    sums[...] = jnp.sum(parts[:, 0:9].astype(F32), axis=0).astype(BF16)


def unpack_kernel(
    middle_scale, stem_scale, sums, parts, features_out, middle_out, stem_out, features, middle, stem, sems,
):
    copies = [
        pltpu.make_async_copy(source, target, sems.at[k])
        for k, (source, target) in enumerate(
            [(middle, middle_out), (stem, stem_out), (features, features_out)]
        )
    ]
    total = jnp.sum(sums[...].astype(F32), axis=0)
    for t in range(27):
        start = 32 * (t % 4)
        middle[t] = total[t // 4, :, start : start + 32] * middle_scale
    copies[0].start()
    order = exchange_order(parts.shape[0])
    rows = [parts[order.index(f), 9 + j] for f in range(parts.shape[0]) for j in range(4)]
    features[...] = nn(turn_matrix(), jnp.concatenate(rows, axis=0)).astype(BF16).reshape(16, 16, LANES)
    copies[2].start()
    turned = jnp.concatenate([total[7], total[8]], axis=0).T * stem_scale
    for t in range(27):
        stem[t] = turned[4 * t : 4 * t + 4]
    copies[1].start()
    for copy in copies:
        copy.wait()


def exchange_order(filts):
    return sorted(range(filts), key=lambda f: (abs(f - filts // 2), f))


def exchange(chunks):
    groups = [exchange_order(lax.axis_size("filt"))]
    return lax.all_to_all(chunks, "filt", 0, 0, axis_index_groups=groups, tiled=True)


def whole(count):
    return [pl.BlockSpec(memory_space=pltpu.VMEM)] * count


def body(volume, stem_weight, middle_weight, cotangent):
    spaces, filts = lax.axis_size("space"), lax.axis_size("filt")
    channels, planes, width, depth = volume.shape
    stem_cells = (planes // 2) * spaces * (width // 2) * filts * (depth // 2)
    middle_cells = stem_cells // 8
    limit = pltpu.CompilerParams(vmem_limit_bytes=48 * 1024 * 1024)

    raw = (volume, middle_weight.transpose(0, 2, 1), cotangent.reshape(16, 16, LANES))
    own, slab_x, packed = pl.pallas_call(
        regroup_kernel,
        out_shape=[
            jax.ShapeDtypeStruct((planes, 16 * width, LANES), BF16),
            jax.ShapeDtypeStruct((planes - 1, 16 * width, LANES), BF16),
            jax.ShapeDtypeStruct((filts, 11, 16, LANES), BF16),
        ],
        in_specs=[pl.BlockSpec(memory_space=pltpu.HBM)] * 3,
        out_specs=whole(2) + [pl.BlockSpec(memory_space=pl.ANY)],
        scratch_shapes=[
            pltpu.VMEM(volume.shape, BF16),
            pltpu.VMEM((27, 16, 32), BF16),
            pltpu.VMEM((16, 16, LANES), BF16),
            pltpu.VMEM((filts, 11, 16, LANES), BF16),
            pltpu.SemaphoreType.DMA((3 + channels,)),
        ],
        compiler_params=limit,
        name="regroup",
    )(*[pltpu.with_memory_space_constraint(x, pltpu.HBM) for x in raw])
    slab_x = lax.ppermute(slab_x, "space", [(s - 1, s) for s in range(1, spaces)])
    gathered = exchange(packed)
    border = pl.pallas_call(
        border_kernel,
        out_shape=jax.ShapeDtypeStruct((7, 48, LANES), BF16),
        in_specs=whole(2),
        out_specs=whole(1)[0],
        compiler_params=limit,
        name="border",
    )(slab_x, own)
    border = lax.ppermute(border, "filt", [(f - 1, f) for f in range(1, filts)])

    stem_w = jnp.pad(stem_weight.reshape(108, 32).T, ((0, 0), (0, 20)))
    place = jnp.asarray(place_table(), BF16)
    weights, cols, slope, taps = pl.pallas_call(
        inner_kernel,
        out_shape=[
            jax.ShapeDtypeStruct((96, STEM_ROWS), BF16),
            jax.ShapeDtypeStruct((7, 48, 7 * LANES), BF16),
            jax.ShapeDtypeStruct((3, 64, 7 * LANES), F32),
            jax.ShapeDtypeStruct((3, 96, 7 * LANES), BF16),
        ],
        in_specs=whole(4),
        out_specs=whole(4),
        compiler_params=limit,
        cost_estimate=pl.CostEstimate(flops=200_000_000, bytes_accessed=4_000_000, transcendentals=500_000),
        name="stem_inner",
    )(own, slab_x, stem_w, place)
    upper = pl.pallas_call(
        upper_kernel,
        out_shape=[
            jax.ShapeDtypeStruct((64, 3 * LANES), BF16),
            jax.ShapeDtypeStruct((64, 864), F32),
            jax.ShapeDtypeStruct((96, STEM_ROWS), F32),
            jax.ShapeDtypeStruct((64, 896), BF16),
            jax.ShapeDtypeStruct((192, LANES), BF16),
            jax.ShapeDtypeStruct((192, 2 * LANES), BF16),
        ],
        in_specs=whole(4),
        out_specs=whole(6),
        scratch_shapes=[
            pltpu.VMEM((864, 3 * LANES), BF16),
            pltpu.VMEM((3, 96, 7 * LANES), BF16),
        ],
        compiler_params=limit,
        name="upper_cells",
    )(gathered, cols, slope, taps)
    parts = pl.pallas_call(
        lower_kernel,
        out_shape=jax.ShapeDtypeStruct((filts, 13, 16, LANES), BF16),
        in_specs=whole(15),
        out_specs=whole(1)[0],
        scratch_shapes=[
            pltpu.VMEM((7, 48, 2 * LANES), BF16),
            pltpu.VMEM((864, LANES), BF16),
            pltpu.VMEM((3, 96, 3 * LANES), BF16),
        ],
        compiler_params=limit,
        cost_estimate=pl.CostEstimate(flops=600_000_000, bytes_accessed=8_000_000, transcendentals=500_000),
        name="lower_cells",
    )(own, slab_x, border, place, gathered, weights, cols, slope, taps, *upper)

    parts = exchange(parts)
    sums = pl.pallas_call(
        sum_kernel,
        out_shape=jax.ShapeDtypeStruct((9, 16, LANES), BF16),
        in_specs=whole(1),
        out_specs=whole(1)[0],
        compiler_params=limit,
        name="sums",
    )(parts)
    sums = lax.all_gather(sums, "space")
    features, middle, stem = pl.pallas_call(
        functools.partial(unpack_kernel, middle_cells**-0.5, stem_cells**-0.5),
        out_shape=[
            jax.ShapeDtypeStruct((16, 16, LANES), BF16),
            jax.ShapeDtypeStruct((27, 16, 32), F32),
            jax.ShapeDtypeStruct((27, 4, 32), F32),
        ],
        in_specs=whole(2),
        out_specs=[pl.BlockSpec(memory_space=pl.ANY)] * 3,
        scratch_shapes=[
            pltpu.VMEM((16, 16, LANES), BF16),
            pltpu.VMEM((27, 16, 32), F32),
            pltpu.VMEM((27, 4, 32), F32),
            pltpu.SemaphoreType.DMA((3,)),
        ],
        compiler_params=limit,
        name="unpack",
    )(sums, parts)
    return features.reshape(16, 1, 16, LANES), middle.transpose(0, 2, 1), stem


def solution(mesh):
    in_specs = (
        P(None, "space", "filt", None),
        P(),
        P(None, None, "filt"),
        P("filt", "space", None, None),
    )
    out_specs = (P("filt", "space", None, None), P(None, None, "filt"), P())
    return jax.shard_map(body, mesh=mesh, in_specs=in_specs, out_specs=out_specs, check_vma=False)
```

```python
import functools

import jax
import jax.numpy as jnp
import numpy as np
from jax import lax
from jax.experimental import pallas as pl
from jax.experimental.pallas import tpu as pltpu
from jax.sharding import PartitionSpec as P

F32 = jnp.float32
BF16 = jnp.bfloat16
LANES = 128
STEM_ROWS = 144


def nn(a, b):
    return lax.dot_general(a, b, (((1,), (0,)), ((), ())), preferred_element_type=F32)


def nt(a, b):
    return lax.dot_general(a, b, (((1,), (1,)), ((), ())), preferred_element_type=F32)


def place_table():
    table = np.zeros((3, LANES, STEM_ROWS), np.float32)
    for even_odd in range(2):
        for a in range(3):
            for b in range(3):
                for d in range(3):
                    q = 2 * even_odd + d - 1
                    group, phase = (2, 3) if q < 0 else (even_odd, q)
                    for c in range(4):
                        column = 48 * a + 16 * b + 4 * phase + c
                        table[group, 4 * (9 * a + 3 * b + d) + c, column] = 1.0
    return table


def rows_lanes(shape):
    return lax.broadcasted_iota(jnp.int32, shape, 0), lax.broadcasted_iota(jnp.int32, shape, 1)


def turn_matrix():
    row, column = rows_lanes((256, 256))
    source = lax.shift_left(row & 15, 4) + lax.shift_right_logical(row, 4)
    return (source == column).astype(F32).astype(BF16)


def regroup_kernel(volume_in, weight_in, cotangent_in, own, slab_x, packed_out, volume, weight, cotangent, packed, sems):
    channels, planes, width, depth = volume.shape
    pairs = [(weight_in, weight), (cotangent_in, cotangent), (packed, packed_out)]
    pairs += [(volume_in.at[c], volume.at[c]) for c in range(channels)]
    copies = [pltpu.make_async_copy(*pair, sems.at[k]) for k, pair in enumerate(pairs)]
    for copy in copies[:2] + copies[3:]:
        copy.start()
    z, column = rows_lanes((depth, depth))
    source = lax.shift_left(column & (LANES - 1), 2) + lax.shift_right_logical(column, 7)
    select = (z == source).astype(F32).astype(BF16)
    turn = turn_matrix()

    blank = jnp.zeros((16, 32), BF16)
    copies[0].wait()
    taps = [weight[t] if t < 27 else blank for t in range(28)]
    for t in range(7):
        tile = jnp.concatenate(taps[4 * t : 4 * t + 4], axis=1)
        for f in range(packed.shape[0]):
            packed[f, t] = tile
    copies[1].wait()
    turned = nn(turn, cotangent[...].reshape(256, LANES)).astype(BF16)
    for k, f in enumerate(exchange_order(packed.shape[0])):
        for j in range(4):
            row = 16 * (4 * f + j)
            packed[k, 7 + j] = turned[row : row + 16]
    copies[2].start()

    for copy in copies[3:]:
        copy.wait()
    picked = nn(volume[...].reshape(channels * planes * width, depth), select).astype(BF16)
    grouped = []
    for x in range(planes):
        parts = []
        for phase in range(4):
            for c in range(channels):
                start = (c * planes + x) * width
                parts.append(picked[start : start + width, phase * LANES : (phase + 1) * LANES])
        grouped.append(jnp.concatenate(parts, axis=0))
    turned = nn(turn, jnp.concatenate(grouped, axis=1)).astype(BF16)
    for x in range(planes):
        plane = turned[:, x * LANES : (x + 1) * LANES]
        own[x] = plane
        if x > 0:
            slab_x[x - 1] = plane
    copies[2].wait()


def border_kernel(slab_x, own, border):
    for x in range(3):
        border[x] = slab_x[x, -48:]
    for x in range(4):
        border[3 + x] = own[x, -48:]


def softplus_sigmoid(values):
    small = jnp.exp(-jnp.abs(values))
    inverse = 1.0 / (1.0 + small)
    soft = jnp.maximum(values, 0.0) + jnp.log(1.0 + small)
    return soft, jnp.where(values >= 0.0, inverse, small * inverse)


def roll_blocks(values, amount):
    blocks = []
    for start in range(0, values.shape[1], LANES):
        block = values[:, start : start + LANES]
        lane = lax.broadcasted_iota(jnp.int32, block.shape, 1)
        edge = 0 if amount == 1 else LANES - 1
        blocks.append(jnp.where(lane == edge, 0.0, pltpu.roll(block, amount % LANES, 1)))
    return jnp.concatenate(blocks, axis=1)


def fill_columns(cols, planes, count):
    for x, plane in enumerate(planes):
        for j in range(count):
            cols[x, :, pl.ds(j * LANES, LANES)] = plane[32 * j : 32 * j + 48]


def stem_forward(weights, cols, i, keep):
    pre = nn(weights, cols[2 * i : 2 * i + 3].reshape(STEM_ROWS, cols.shape[2]))
    pre = jnp.concatenate([pre[0:32] + roll_blocks(pre[64:96], 1), pre[32:64]], axis=0)
    soft, sig = softplus_sigmoid(pre)
    act = (0.3 * pre + 0.7 * soft) * keep
    taps = jnp.concatenate([roll_blocks(act[32:64], 1), act], axis=0).astype(BF16)
    return (0.3 + 0.7 * sig) * keep, taps


def keep_space():
    return jnp.where(lax.axis_index("space") > 0, 1.0, 0.0).astype(F32)


def inner_kernel(own, slab_x, stem_w, place, weights, cols, slope, taps):
    weights[...] = jnp.concatenate([nn(stem_w[...], place[g]) for g in range(3)], axis=0).astype(BF16)
    planes = [slab_x[x, 16:256] if x < 3 else own[x - 3, 16:256] for x in range(7)]
    fill_columns(cols, planes, 7)
    for i in range(3):
        slope[i], taps[i] = stem_forward(weights[...], cols, i, keep_space() if i == 0 else 1.0)


def fill_taps(mid_cols, part, i, j, first, count):
    for b in range(3):
        if (j - b) % 2 == 0 and first <= (j - b) // 2 < first + count:
            row = 96 * (3 * i + b)
            mid_cols[row : row + 96, pl.ds(((j - b) // 2 - first) * LANES, LANES)] = part


def middle_cells_step(mid_w, mid_cols, cotangent):
    pre = nn(mid_w[:, 0:864], mid_cols[...])
    soft, sig = softplus_sigmoid(pre)
    delta = cotangent.astype(F32) * (0.3 + 0.7 * sig)
    delta_low = delta.astype(BF16)
    mid_grad = nt(delta_low, mid_cols[...])
    both = jnp.concatenate([delta_low, roll_blocks(delta, -1).astype(BF16)], axis=0)
    return (0.3 * pre + 0.7 * soft).astype(BF16), mid_grad, both


def put_back(target, i, start, part):
    lanes = pl.ds(start, LANES)
    target[i, 0:64, lanes] = part.astype(BF16)
    target[i, 64:96, lanes] = roll_blocks(part[0:32], -1).astype(BF16)


def upper_kernel(
    gathered, cols, slope, taps, features, mid_grad, stem_grad, mid_w, odd_w, even_w, mid_cols, stem_back,
):
    blocks = gathered.shape[0]
    order = exchange_order(blocks)
    for k, f in enumerate(order):
        for t in range(7):
            mid_w[16 * f : 16 * f + 16, t * LANES : (t + 1) * LANES] = gathered[k, t]
    for i in range(3):
        for j in range(2, 9):
            fill_taps(mid_cols, taps[i, :, pl.ds((j - 2) * LANES, LANES)], i, j, 1, 3)
    cotangent = jnp.concatenate(
        [jnp.concatenate([gathered[order.index(f), 7 + j] for j in range(1, 4)], axis=1) for f in range(blocks)],
        axis=0,
    )
    features[...], mid_grad[...], both = middle_cells_step(mid_w, mid_cols, cotangent)

    turned = jnp.concatenate(
        [mid_w[:, t * LANES : (t + 1) * LANES].astype(F32).T for t in range(7)], axis=0
    ).astype(BF16)
    zero = jnp.zeros((32, blocks * 16), BF16)

    def block(a, b, d):
        row = 32 * (9 * a + 3 * b + d)
        return turned[row : row + 32]

    def wide(a, b):
        even = jnp.concatenate([block(a, b, 1), zero], axis=1)
        odd = jnp.concatenate([block(a, b, 2), block(a, b, 0)], axis=1)
        return jnp.concatenate([even, odd], axis=0)

    odd_w[...] = jnp.concatenate([wide(i, 1) for i in range(3)], axis=0)
    even_w[...] = jnp.concatenate(
        [jnp.concatenate([wide(i, 0), wide(i, 2)], axis=1) for i in range(3)], axis=0
    )
    nothing = jnp.zeros((2 * blocks * 16, LANES), BF16)
    pair = jnp.concatenate(
        [jnp.concatenate([both, nothing], axis=1), jnp.concatenate([nothing, both], axis=1)], axis=0
    )
    odd_back = nn(odd_w[...], both)
    even_back = nn(even_w[...], pair)
    total = jnp.zeros((96, STEM_ROWS), F32)
    for i in range(3):
        for j in range(7):
            source = even_back if j % 2 == 0 else odd_back
            part = source[64 * i : 64 * i + 64, (j // 2) * LANES : (j // 2 + 1) * LANES]
            put_back(stem_back, i, j * LANES, part * slope[i, :, pl.ds(j * LANES, LANES)])
        total += nt(stem_back[i], cols[2 * i : 2 * i + 3].reshape(STEM_ROWS, 7 * LANES))
    stem_grad[...] = total


def lower_kernel(
    own, slab_x, border, place, gathered, weights, cols, slope, taps, upper_features, upper_mid, upper_stem,
    mid_w, odd_w, even_w, parts, low_cols, mid_cols, low_back,
):
    blocks = gathered.shape[0]
    keep_y = jnp.where(lax.axis_index("filt") > 0, 1.0, 0.0).astype(F32)
    planes = [
        jnp.concatenate([border[x], slab_x[x, 0:32] if x < 3 else own[x - 3, 0:32]], axis=0)
        for x in range(7)
    ]
    fill_columns(low_cols, planes, 2)
    low_slope = []
    for i in range(3):
        keep = jnp.where(lax.broadcasted_iota(jnp.int32, (64, 2 * LANES), 1) < LANES, keep_y, 1.0)
        if i == 0:
            keep = keep * keep_space()
        one_slope, low_taps = stem_forward(weights[...], low_cols, i, keep)
        low_slope.append(one_slope)
        for j in range(2):
            fill_taps(mid_cols, low_taps[:, j * LANES : (j + 1) * LANES], i, j, 0, 1)
        fill_taps(mid_cols, taps[i, :, 0:LANES], i, 2, 0, 1)
    order = exchange_order(blocks)
    cotangent = jnp.concatenate([gathered[order.index(f), 7] for f in range(blocks)], axis=0)
    features, mid_grad, both = middle_cells_step(mid_w, mid_cols, cotangent)

    back = [nn(even_w[:, 0:LANES], both), nn(odd_w[...], both), nn(even_w[:, LANES:], both)]
    stem_grad = upper_stem[...]
    for i in range(3):
        for j in range(2):
            part = back[j][64 * i : 64 * i + 64] * low_slope[i][:, j * LANES : (j + 1) * LANES]
            put_back(low_back, i, j * LANES, part)
        put_back(low_back, i, 2 * LANES, back[2][64 * i : 64 * i + 64] * slope[i, :, 0:LANES])
        low = low_cols[2 * i : 2 * i + 3].reshape(STEM_ROWS, 2 * LANES)
        near = cols[2 * i : 2 * i + 3, :, 0:LANES].reshape(STEM_ROWS, LANES)
        stem_grad += nt(low_back[i], jnp.concatenate([low, near], axis=1))
    high = stem_grad.astype(BF16)
    both = jnp.concatenate([high, (stem_grad - high.astype(F32)).astype(BF16)], axis=0)
    stem = 0.0
    for g in range(3):
        rows = jnp.concatenate([both[32 * g : 32 * g + 32], both[96 + 32 * g : 128 + 32 * g]], axis=0)
        taken = nt(rows, place[g])
        stem += taken[0:32] + taken[32:64]
    stem = stem.astype(BF16)

    middle = (mid_grad + upper_mid[...]).astype(BF16)
    middle = jnp.concatenate([middle, jnp.zeros((blocks * 16, 32), BF16)], axis=1)
    for k, f in enumerate(order):
        rows = slice(16 * f, 16 * f + 16)
        for t in range(7):
            parts[k, t] = middle[rows, t * LANES : (t + 1) * LANES]
        for half in range(2):
            parts[k, 7 + half] = stem[16 * half : 16 * half + 16]
        parts[k, 9] = features[rows]
        for j in range(3):
            parts[k, 10 + j] = upper_features[rows, j * LANES : (j + 1) * LANES]


def sum_kernel(parts, sums):
    sums[...] = jnp.sum(parts[:, 0:9].astype(F32), axis=0).astype(BF16)


def unpack_kernel(
    middle_scale, stem_scale, sums, parts, features_out, middle_out, stem_out, features, middle, stem, sems,
):
    copies = [
        pltpu.make_async_copy(source, target, sems.at[k])
        for k, (source, target) in enumerate(
            [(middle, middle_out), (stem, stem_out), (features, features_out)]
        )
    ]
    total = jnp.sum(sums[...].astype(F32), axis=0)
    for t in range(27):
        start = 32 * (t % 4)
        middle[t] = total[t // 4, :, start : start + 32] * middle_scale
    copies[0].start()
    order = exchange_order(parts.shape[0])
    rows = [parts[order.index(f), 9 + j] for f in range(parts.shape[0]) for j in range(4)]
    features[...] = nn(turn_matrix(), jnp.concatenate(rows, axis=0)).astype(BF16).reshape(16, 16, LANES)
    copies[2].start()
    turned = jnp.concatenate([total[7], total[8]], axis=0).T * stem_scale
    for t in range(27):
        stem[t] = turned[4 * t : 4 * t + 4]
    copies[1].start()
    for copy in copies:
        copy.wait()


def exchange_order(filts):
    return list(range(filts))[::-1]


def exchange(chunks):
    groups = [exchange_order(lax.axis_size("filt"))]
    return lax.all_to_all(chunks, "filt", 0, 0, axis_index_groups=groups, tiled=True)


def whole(count):
    return [pl.BlockSpec(memory_space=pltpu.VMEM)] * count


def body(volume, stem_weight, middle_weight, cotangent):
    spaces, filts = lax.axis_size("space"), lax.axis_size("filt")
    channels, planes, width, depth = volume.shape
    stem_cells = (planes // 2) * spaces * (width // 2) * filts * (depth // 2)
    middle_cells = stem_cells // 8
    limit = pltpu.CompilerParams(vmem_limit_bytes=48 * 1024 * 1024)

    raw = (volume, middle_weight.transpose(0, 2, 1), cotangent.reshape(16, 16, LANES))
    own, slab_x, packed = pl.pallas_call(
        regroup_kernel,
        out_shape=[
            jax.ShapeDtypeStruct((planes, 16 * width, LANES), BF16),
            jax.ShapeDtypeStruct((planes - 1, 16 * width, LANES), BF16),
            jax.ShapeDtypeStruct((filts, 11, 16, LANES), BF16),
        ],
        in_specs=[pl.BlockSpec(memory_space=pltpu.HBM)] * 3,
        out_specs=whole(2) + [pl.BlockSpec(memory_space=pl.ANY)],
        scratch_shapes=[
            pltpu.VMEM(volume.shape, BF16),
            pltpu.VMEM((27, 16, 32), BF16),
            pltpu.VMEM((16, 16, LANES), BF16),
            pltpu.VMEM((filts, 11, 16, LANES), BF16),
            pltpu.SemaphoreType.DMA((3 + channels,)),
        ],
        compiler_params=limit,
        name="regroup",
    )(*[pltpu.with_memory_space_constraint(x, pltpu.HBM) for x in raw])
    slab_x = lax.ppermute(slab_x, "space", [(s - 1, s) for s in range(1, spaces)])
    gathered = exchange(packed)
    border = pl.pallas_call(
        border_kernel,
        out_shape=jax.ShapeDtypeStruct((7, 48, LANES), BF16),
        in_specs=whole(2),
        out_specs=whole(1)[0],
        compiler_params=limit,
        name="border",
    )(slab_x, own)
    border = lax.ppermute(border, "filt", [(f - 1, f) for f in range(1, filts)])

    stem_w = jnp.pad(stem_weight.reshape(108, 32).T, ((0, 0), (0, 20)))
    place = jnp.asarray(place_table(), BF16)
    weights, cols, slope, taps = pl.pallas_call(
        inner_kernel,
        out_shape=[
            jax.ShapeDtypeStruct((96, STEM_ROWS), BF16),
            jax.ShapeDtypeStruct((7, 48, 7 * LANES), BF16),
            jax.ShapeDtypeStruct((3, 64, 7 * LANES), F32),
            jax.ShapeDtypeStruct((3, 96, 7 * LANES), BF16),
        ],
        in_specs=whole(4),
        out_specs=whole(4),
        compiler_params=limit,
        cost_estimate=pl.CostEstimate(flops=200_000_000, bytes_accessed=4_000_000, transcendentals=500_000),
        name="stem_inner",
    )(own, slab_x, stem_w, place)
    upper = pl.pallas_call(
        upper_kernel,
        out_shape=[
            jax.ShapeDtypeStruct((64, 3 * LANES), BF16),
            jax.ShapeDtypeStruct((64, 864), F32),
            jax.ShapeDtypeStruct((96, STEM_ROWS), F32),
            jax.ShapeDtypeStruct((64, 896), BF16),
            jax.ShapeDtypeStruct((192, LANES), BF16),
            jax.ShapeDtypeStruct((192, 2 * LANES), BF16),
        ],
        in_specs=whole(4),
        out_specs=whole(6),
        scratch_shapes=[
            pltpu.VMEM((864, 3 * LANES), BF16),
            pltpu.VMEM((3, 96, 7 * LANES), BF16),
        ],
        compiler_params=limit,
        name="upper_cells",
    )(gathered, cols, slope, taps)
    parts = pl.pallas_call(
        lower_kernel,
        out_shape=jax.ShapeDtypeStruct((filts, 13, 16, LANES), BF16),
        in_specs=whole(15),
        out_specs=whole(1)[0],
        scratch_shapes=[
            pltpu.VMEM((7, 48, 2 * LANES), BF16),
            pltpu.VMEM((864, LANES), BF16),
            pltpu.VMEM((3, 96, 3 * LANES), BF16),
        ],
        compiler_params=limit,
        cost_estimate=pl.CostEstimate(flops=600_000_000, bytes_accessed=8_000_000, transcendentals=500_000),
        name="lower_cells",
    )(own, slab_x, border, place, gathered, weights, cols, slope, taps, *upper)

    parts = exchange(parts)
    sums = pl.pallas_call(
        sum_kernel,
        out_shape=jax.ShapeDtypeStruct((9, 16, LANES), BF16),
        in_specs=whole(1),
        out_specs=whole(1)[0],
        compiler_params=limit,
        name="sums",
    )(parts)
    sums = lax.all_gather(sums, "space")
    features, middle, stem = pl.pallas_call(
        functools.partial(unpack_kernel, middle_cells**-0.5, stem_cells**-0.5),
        out_shape=[
            jax.ShapeDtypeStruct((16, 16, LANES), BF16),
            jax.ShapeDtypeStruct((27, 16, 32), F32),
            jax.ShapeDtypeStruct((27, 4, 32), F32),
        ],
        in_specs=whole(2),
        out_specs=[pl.BlockSpec(memory_space=pl.ANY)] * 3,
        scratch_shapes=[
            pltpu.VMEM((16, 16, LANES), BF16),
            pltpu.VMEM((27, 16, 32), F32),
            pltpu.VMEM((27, 4, 32), F32),
            pltpu.SemaphoreType.DMA((3,)),
        ],
        compiler_params=limit,
        name="unpack",
    )(sums, parts)
    return features.reshape(16, 1, 16, LANES), middle.transpose(0, 2, 1), stem


def solution(mesh):
    in_specs = (
        P(None, "space", "filt", None),
        P(),
        P(None, None, "filt"),
        P("filt", "space", None, None),
    )
    out_specs = (P("filt", "space", None, None), P(None, None, "filt"), P())
    return jax.shard_map(body, mesh=mesh, in_specs=in_specs, out_specs=out_specs, check_vma=False)
```

```python
import functools

import jax
import jax.numpy as jnp
import numpy as np
from jax import lax
from jax.experimental import pallas as pl
from jax.experimental.pallas import tpu as pltpu
from jax.sharding import PartitionSpec as P

F32 = jnp.float32
BF16 = jnp.bfloat16
LANES = 128
STEM_ROWS = 144


def nn(a, b):
    return lax.dot_general(a, b, (((1,), (0,)), ((), ())), preferred_element_type=F32)


def nt(a, b):
    return lax.dot_general(a, b, (((1,), (1,)), ((), ())), preferred_element_type=F32)


def place_table():
    table = np.zeros((3, LANES, STEM_ROWS), np.float32)
    for even_odd in range(2):
        for a in range(3):
            for b in range(3):
                for d in range(3):
                    q = 2 * even_odd + d - 1
                    group, phase = (2, 3) if q < 0 else (even_odd, q)
                    for c in range(4):
                        column = 48 * a + 16 * b + 4 * phase + c
                        table[group, 4 * (9 * a + 3 * b + d) + c, column] = 1.0
    return table


def rows_lanes(shape):
    return lax.broadcasted_iota(jnp.int32, shape, 0), lax.broadcasted_iota(jnp.int32, shape, 1)


def turn_matrix():
    row, column = rows_lanes((256, 256))
    source = lax.shift_left(row & 15, 4) + lax.shift_right_logical(row, 4)
    return (source == column).astype(F32).astype(BF16)


def depth_phases(rows):
    count = rows.shape[0]
    z, column = rows_lanes((256, 256))
    source = lax.shift_left(column & 63, 2) + lax.shift_right_logical(column, 6)
    select = (z == source).astype(F32).astype(BF16)
    halves = jnp.concatenate([rows[:, 0:256], rows[:, 256:512]], axis=0)
    picked = nn(halves, select)
    return [
        jnp.concatenate([picked[h * count : (h + 1) * count, 64 * p : 64 * p + 64] for h in range(2)], axis=1)
        for p in range(4)
    ]


def grouped_planes(volume, chosen):
    channels, planes, width, depth = volume.shape
    phases = [part.astype(BF16) for part in depth_phases(volume[...].reshape(channels * planes * width, depth))]
    grouped = []
    for x in chosen:
        starts = [(c * planes + x) * width for c in range(channels)]
        grouped.append(
            jnp.concatenate([part[start : start + width] for part in phases for start in starts], axis=0)
        )
    return grouped


def regroup_kernel(volume_in, weight_in, cotangent_in, own, packed_out, volume, weight, cotangent, packed, sems):
    pairs = [(weight_in, weight), (cotangent_in, cotangent), (volume_in, volume), (packed, packed_out)]
    copies = [pltpu.make_async_copy(*pair, sems.at[k]) for k, pair in enumerate(pairs)]
    for copy in copies[:3]:
        copy.start()
    turn = turn_matrix()
    blank = jnp.zeros((16, 32), BF16)
    copies[0].wait()
    taps = [weight[t] if t < 27 else blank for t in range(28)]
    for t in range(7):
        tile = jnp.concatenate(taps[4 * t : 4 * t + 4], axis=1)
        for f in range(packed.shape[0]):
            packed[f, t] = tile
    copies[1].wait()
    turned = nn(turn, cotangent[...].reshape(256, LANES)).astype(BF16)
    for k, f in enumerate(exchange_order(packed.shape[0])):
        for j in range(4):
            row = 16 * (4 * f + j)
            packed[k, 7 + j] = turned[row : row + 16]
    copies[3].start()
    copies[2].wait()
    turned = nn(turn, jnp.concatenate(grouped_planes(volume, range(4)), axis=1)).astype(BF16)
    for x in range(4):
        own[x] = turned[:, x * LANES : (x + 1) * LANES]
    copies[3].wait()


def border_kernel(raw, own, border):
    channels, planes, width, depth = raw.shape
    rows = [raw[c, x, 8:16].astype(F32) for c in range(channels) for x in range(1, planes)]
    phases = depth_phases(jnp.concatenate(rows, axis=0).astype(BF16))
    grouped = []
    for x in range(3):
        starts = [8 * (3 * c + x) for c in range(channels)]
        grouped.append(
            jnp.concatenate([part[start : start + 8] for part in phases for start in starts], axis=0)
        )
    row, column = rows_lanes((64, LANES))
    source = lax.shift_left(row & 15, 3) + 4 + lax.shift_right_logical(row, 4)
    turned = nn(
        (source == column).astype(F32).astype(BF16), jnp.concatenate(grouped, axis=1).astype(BF16)
    ).astype(BF16)
    for x in range(3):
        border[x] = turned[16:64, x * LANES : (x + 1) * LANES]
    for x in range(4):
        border[3 + x] = own[x, -48:]


def softplus_sigmoid(values):
    small = jnp.exp(-jnp.abs(values))
    inverse = 1.0 / (1.0 + small)
    soft = jnp.maximum(values, 0.0) + jnp.log(1.0 + small)
    return soft, jnp.where(values >= 0.0, inverse, small * inverse)


def roll_blocks(values, amount):
    blocks = []
    for start in range(0, values.shape[1], LANES):
        block = values[:, start : start + LANES]
        lane = lax.broadcasted_iota(jnp.int32, block.shape, 1)
        edge = 0 if amount == 1 else LANES - 1
        blocks.append(jnp.where(lane == edge, 0.0, pltpu.roll(block, amount % LANES, 1)))
    return jnp.concatenate(blocks, axis=1)


def fill_columns(cols, planes, count):
    for x, plane in enumerate(planes):
        for j in range(count):
            cols[x, :, pl.ds(j * LANES, LANES)] = plane[32 * j : 32 * j + 48]


def stem_forward(weights, cols, i, keep):
    pre = nn(weights, cols[2 * i : 2 * i + 3].reshape(STEM_ROWS, cols.shape[2]))
    pre = jnp.concatenate([pre[0:32] + roll_blocks(pre[64:96], 1), pre[32:64]], axis=0)
    soft, sig = softplus_sigmoid(pre)
    act = (0.3 * pre + 0.7 * soft) * keep
    taps = jnp.concatenate([roll_blocks(act[32:64], 1), act], axis=0).astype(BF16)
    return (0.3 + 0.7 * sig) * keep, taps


def keep_space():
    return jnp.where(lax.axis_index("space") > 0, 1.0, 0.0).astype(F32)


def inner_kernel(own, raw, stem_w, place, slab, weights, cols, slope, taps):
    turned = nn(turn_matrix(), jnp.concatenate(grouped_planes(raw, range(1, 4)), axis=1)).astype(BF16)
    for x in range(3):
        slab[x] = turned[:, x * LANES : (x + 1) * LANES]
    weights[...] = jnp.concatenate([nn(stem_w[...], place[g]) for g in range(3)], axis=0).astype(BF16)
    planes = [turned[16:256, x * LANES : (x + 1) * LANES] if x < 3 else own[x - 3, 16:256] for x in range(7)]
    fill_columns(cols, planes, 7)
    for i in range(3):
        slope[i], taps[i] = stem_forward(weights[...], cols, i, keep_space() if i == 0 else 1.0)


def fill_taps(mid_cols, part, i, j, first, count):
    for b in range(3):
        if (j - b) % 2 == 0 and first <= (j - b) // 2 < first + count:
            row = 96 * (3 * i + b)
            mid_cols[row : row + 96, pl.ds(((j - b) // 2 - first) * LANES, LANES)] = part


def middle_cells_step(mid_w, mid_cols, cotangent):
    pre = nn(mid_w[:, 0:864], mid_cols[...])
    soft, sig = softplus_sigmoid(pre)
    delta = cotangent.astype(F32) * (0.3 + 0.7 * sig)
    delta_low = delta.astype(BF16)
    mid_grad = nt(delta_low, mid_cols[...])
    both = jnp.concatenate([delta_low, roll_blocks(delta, -1).astype(BF16)], axis=0)
    return (0.3 * pre + 0.7 * soft).astype(BF16), mid_grad, both


def put_back(target, i, start, part):
    lanes = pl.ds(start, LANES)
    target[i, 0:64, lanes] = part.astype(BF16)
    target[i, 64:96, lanes] = roll_blocks(part[0:32], -1).astype(BF16)


def upper_kernel(
    gathered, cols, slope, taps, features, mid_grad, stem_grad, mid_w, odd_w, even_w, mid_cols, stem_back,
):
    blocks = gathered.shape[0]
    order = exchange_order(blocks)
    for k, f in enumerate(order):
        for t in range(7):
            mid_w[16 * f : 16 * f + 16, t * LANES : (t + 1) * LANES] = gathered[k, t]
    for i in range(3):
        for j in range(2, 9):
            fill_taps(mid_cols, taps[i, :, pl.ds((j - 2) * LANES, LANES)], i, j, 1, 3)
    cotangent = jnp.concatenate(
        [jnp.concatenate([gathered[order.index(f), 7 + j] for j in range(1, 4)], axis=1) for f in range(blocks)],
        axis=0,
    )
    features[...], mid_grad[...], both = middle_cells_step(mid_w, mid_cols, cotangent)

    turned = jnp.concatenate(
        [mid_w[:, t * LANES : (t + 1) * LANES].astype(F32).T for t in range(7)], axis=0
    ).astype(BF16)
    zero = jnp.zeros((32, blocks * 16), BF16)

    def block(a, b, d):
        row = 32 * (9 * a + 3 * b + d)
        return turned[row : row + 32]

    def wide(a, b):
        even = jnp.concatenate([block(a, b, 1), zero], axis=1)
        odd = jnp.concatenate([block(a, b, 2), block(a, b, 0)], axis=1)
        return jnp.concatenate([even, odd], axis=0)

    odd_w[...] = jnp.concatenate([wide(i, 1) for i in range(3)], axis=0)
    even_w[...] = jnp.concatenate(
        [jnp.concatenate([wide(i, 0), wide(i, 2)], axis=1) for i in range(3)], axis=0
    )
    nothing = jnp.zeros((2 * blocks * 16, LANES), BF16)
    pair = jnp.concatenate(
        [jnp.concatenate([both, nothing], axis=1), jnp.concatenate([nothing, both], axis=1)], axis=0
    )
    odd_back = nn(odd_w[...], both)
    even_back = nn(even_w[...], pair)
    total = jnp.zeros((96, STEM_ROWS), F32)
    for i in range(3):
        for j in range(7):
            source = even_back if j % 2 == 0 else odd_back
            part = source[64 * i : 64 * i + 64, (j // 2) * LANES : (j // 2 + 1) * LANES]
            put_back(stem_back, i, j * LANES, part * slope[i, :, pl.ds(j * LANES, LANES)])
        total += nt(stem_back[i], cols[2 * i : 2 * i + 3].reshape(STEM_ROWS, 7 * LANES))
    stem_grad[...] = total


def lower_kernel(
    own, slab_x, border, place, gathered, weights, cols, slope, taps, upper_features, upper_mid, upper_stem,
    mid_w, odd_w, even_w, parts, low_cols, mid_cols, low_back,
):
    blocks = gathered.shape[0]
    keep_y = jnp.where(lax.axis_index("filt") > 0, 1.0, 0.0).astype(F32)
    planes = [
        jnp.concatenate([border[x], slab_x[x, 0:32] if x < 3 else own[x - 3, 0:32]], axis=0)
        for x in range(7)
    ]
    fill_columns(low_cols, planes, 2)
    low_slope = []
    for i in range(3):
        keep = jnp.where(lax.broadcasted_iota(jnp.int32, (64, 2 * LANES), 1) < LANES, keep_y, 1.0)
        if i == 0:
            keep = keep * keep_space()
        one_slope, low_taps = stem_forward(weights[...], low_cols, i, keep)
        low_slope.append(one_slope)
        for j in range(2):
            fill_taps(mid_cols, low_taps[:, j * LANES : (j + 1) * LANES], i, j, 0, 1)
        fill_taps(mid_cols, taps[i, :, 0:LANES], i, 2, 0, 1)
    order = exchange_order(blocks)
    cotangent = jnp.concatenate([gathered[order.index(f), 7] for f in range(blocks)], axis=0)
    features, mid_grad, both = middle_cells_step(mid_w, mid_cols, cotangent)

    back = [nn(even_w[:, 0:LANES], both), nn(odd_w[...], both), nn(even_w[:, LANES:], both)]
    stem_grad = upper_stem[...]
    for i in range(3):
        for j in range(2):
            part = back[j][64 * i : 64 * i + 64] * low_slope[i][:, j * LANES : (j + 1) * LANES]
            put_back(low_back, i, j * LANES, part)
        put_back(low_back, i, 2 * LANES, back[2][64 * i : 64 * i + 64] * slope[i, :, 0:LANES])
        low = low_cols[2 * i : 2 * i + 3].reshape(STEM_ROWS, 2 * LANES)
        near = cols[2 * i : 2 * i + 3, :, 0:LANES].reshape(STEM_ROWS, LANES)
        stem_grad += nt(low_back[i], jnp.concatenate([low, near], axis=1))
    high = stem_grad.astype(BF16)
    both = jnp.concatenate([high, (stem_grad - high.astype(F32)).astype(BF16)], axis=0)
    stem = 0.0
    for g in range(3):
        rows = jnp.concatenate([both[32 * g : 32 * g + 32], both[96 + 32 * g : 128 + 32 * g]], axis=0)
        taken = nt(rows, place[g])
        stem += taken[0:32] + taken[32:64]
    stem = stem.astype(BF16)

    middle = (mid_grad + upper_mid[...]).astype(BF16)
    middle = jnp.concatenate([middle, jnp.zeros((blocks * 16, 32), BF16)], axis=1)
    for k, f in enumerate(order):
        rows = slice(16 * f, 16 * f + 16)
        for t in range(7):
            parts[k, t] = middle[rows, t * LANES : (t + 1) * LANES]
        for half in range(2):
            parts[k, 7 + half] = stem[16 * half : 16 * half + 16]
        parts[k, 9] = features[rows]
        for j in range(3):
            parts[k, 10 + j] = upper_features[rows, j * LANES : (j + 1) * LANES]


def sum_kernel(parts, sums):
    sums[...] = jnp.sum(parts[:, 0:9].astype(F32), axis=0).astype(BF16)


def unpack_kernel(
    middle_scale, stem_scale, sums, parts, features_out, middle_out, stem_out, features, middle, stem, sems,
):
    copies = [
        pltpu.make_async_copy(source, target, sems.at[k])
        for k, (source, target) in enumerate(
            [(middle, middle_out), (stem, stem_out), (features, features_out)]
        )
    ]
    total = jnp.sum(sums[...].astype(F32), axis=0)
    for t in range(27):
        start = 32 * (t % 4)
        middle[t] = total[t // 4, :, start : start + 32] * middle_scale
    copies[0].start()
    order = exchange_order(parts.shape[0])
    rows = [parts[order.index(f), 9 + j] for f in range(parts.shape[0]) for j in range(4)]
    features[...] = nn(turn_matrix(), jnp.concatenate(rows, axis=0)).astype(BF16).reshape(16, 16, LANES)
    copies[2].start()
    turned = jnp.concatenate([total[7], total[8]], axis=0).T * stem_scale
    for t in range(27):
        stem[t] = turned[4 * t : 4 * t + 4]
    copies[1].start()
    for copy in copies:
        copy.wait()


def exchange_order(filts):
    return sorted(range(filts), key=lambda f: (abs(f - filts // 2), f))


def exchange(chunks):
    groups = [exchange_order(lax.axis_size("filt"))]
    return lax.all_to_all(chunks, "filt", 0, 0, axis_index_groups=groups, tiled=True)


def whole(count):
    return [pl.BlockSpec(memory_space=pltpu.VMEM)] * count


def body(volume, stem_weight, middle_weight, cotangent):
    spaces, filts = lax.axis_size("space"), lax.axis_size("filt")
    channels, planes, width, depth = volume.shape
    stem_cells = (planes // 2) * spaces * (width // 2) * filts * (depth // 2)
    middle_cells = stem_cells // 8
    limit = pltpu.CompilerParams(vmem_limit_bytes=48 * 1024 * 1024)

    raw = lax.ppermute(volume, "space", [(s - 1, s) for s in range(1, spaces)])
    inputs = (volume, middle_weight.transpose(0, 2, 1), cotangent.reshape(16, 16, LANES))
    own, packed = pl.pallas_call(
        regroup_kernel,
        out_shape=[
            jax.ShapeDtypeStruct((planes, 16 * width, LANES), BF16),
            jax.ShapeDtypeStruct((filts, 11, 16, LANES), BF16),
        ],
        in_specs=[pl.BlockSpec(memory_space=pltpu.HBM)] * 3,
        out_specs=whole(1) + [pl.BlockSpec(memory_space=pl.ANY)],
        scratch_shapes=[
            pltpu.VMEM(volume.shape, BF16),
            pltpu.VMEM((27, 16, 32), BF16),
            pltpu.VMEM((16, 16, LANES), BF16),
            pltpu.VMEM((filts, 11, 16, LANES), BF16),
            pltpu.SemaphoreType.DMA((4,)),
        ],
        compiler_params=limit,
        name="regroup",
    )(*[pltpu.with_memory_space_constraint(x, pltpu.HBM) for x in inputs])
    gathered = exchange(packed)
    border = pl.pallas_call(
        border_kernel,
        out_shape=jax.ShapeDtypeStruct((7, 48, LANES), BF16),
        in_specs=whole(2),
        out_specs=whole(1)[0],
        compiler_params=limit,
        name="border",
    )(raw, own)
    border = lax.ppermute(border, "filt", [(f - 1, f) for f in range(1, filts)])

    stem_w = jnp.pad(stem_weight.reshape(108, 32).T, ((0, 0), (0, 20)))
    place = jnp.asarray(place_table(), BF16)
    slab, weights, cols, slope, taps = pl.pallas_call(
        inner_kernel,
        out_shape=[
            jax.ShapeDtypeStruct((planes - 1, 16 * width, LANES), BF16),
            jax.ShapeDtypeStruct((96, STEM_ROWS), BF16),
            jax.ShapeDtypeStruct((7, 48, 7 * LANES), BF16),
            jax.ShapeDtypeStruct((3, 64, 7 * LANES), F32),
            jax.ShapeDtypeStruct((3, 96, 7 * LANES), BF16),
        ],
        in_specs=whole(4),
        out_specs=whole(5),
        compiler_params=limit,
        cost_estimate=pl.CostEstimate(flops=200_000_000, bytes_accessed=4_000_000, transcendentals=500_000),
        name="stem_inner",
    )(own, raw, stem_w, place)
    upper = pl.pallas_call(
        upper_kernel,
        out_shape=[
            jax.ShapeDtypeStruct((64, 3 * LANES), BF16),
            jax.ShapeDtypeStruct((64, 864), F32),
            jax.ShapeDtypeStruct((96, STEM_ROWS), F32),
            jax.ShapeDtypeStruct((64, 896), BF16),
            jax.ShapeDtypeStruct((192, LANES), BF16),
            jax.ShapeDtypeStruct((192, 2 * LANES), BF16),
        ],
        in_specs=whole(4),
        out_specs=whole(6),
        scratch_shapes=[
            pltpu.VMEM((864, 3 * LANES), BF16),
            pltpu.VMEM((3, 96, 7 * LANES), BF16),
        ],
        compiler_params=limit,
        name="upper_cells",
    )(gathered, cols, slope, taps)
    parts = pl.pallas_call(
        lower_kernel,
        out_shape=jax.ShapeDtypeStruct((filts, 13, 16, LANES), BF16),
        in_specs=whole(15),
        out_specs=whole(1)[0],
        scratch_shapes=[
            pltpu.VMEM((7, 48, 2 * LANES), BF16),
            pltpu.VMEM((864, LANES), BF16),
            pltpu.VMEM((3, 96, 3 * LANES), BF16),
        ],
        compiler_params=limit,
        cost_estimate=pl.CostEstimate(flops=600_000_000, bytes_accessed=8_000_000, transcendentals=500_000),
        name="lower_cells",
    )(own, slab, border, place, gathered, weights, cols, slope, taps, *upper)

    parts = exchange(parts)
    sums = pl.pallas_call(
        sum_kernel,
        out_shape=jax.ShapeDtypeStruct((9, 16, LANES), BF16),
        in_specs=whole(1),
        out_specs=whole(1)[0],
        compiler_params=limit,
        name="sums",
    )(parts)
    sums = lax.all_gather(sums, "space")
    features, middle, stem = pl.pallas_call(
        functools.partial(unpack_kernel, middle_cells**-0.5, stem_cells**-0.5),
        out_shape=[
            jax.ShapeDtypeStruct((16, 16, LANES), BF16),
            jax.ShapeDtypeStruct((27, 16, 32), F32),
            jax.ShapeDtypeStruct((27, 4, 32), F32),
        ],
        in_specs=whole(2),
        out_specs=[pl.BlockSpec(memory_space=pl.ANY)] * 3,
        scratch_shapes=[
            pltpu.VMEM((16, 16, LANES), BF16),
            pltpu.VMEM((27, 16, 32), F32),
            pltpu.VMEM((27, 4, 32), F32),
            pltpu.SemaphoreType.DMA((3,)),
        ],
        compiler_params=limit,
        name="unpack",
    )(sums, parts)
    return features.reshape(16, 1, 16, LANES), middle.transpose(0, 2, 1), stem


def solution(mesh):
    in_specs = (
        P(None, "space", "filt", None),
        P(),
        P(None, None, "filt"),
        P("filt", "space", None, None),
    )
    out_specs = (P("filt", "space", None, None), P(None, None, "filt"), P())
    return jax.shard_map(body, mesh=mesh, in_specs=in_specs, out_specs=out_specs, check_vma=False)
```

```python
import functools

import jax
import jax.numpy as jnp
import numpy as np
from jax import lax
from jax.experimental import pallas as pl
from jax.experimental.pallas import tpu as pltpu
from jax.sharding import PartitionSpec as P

F32 = jnp.float32
BF16 = jnp.bfloat16
LANES = 128
STEM_ROWS = 144


def nn(a, b):
    return lax.dot_general(a, b, (((1,), (0,)), ((), ())), preferred_element_type=F32)


def nt(a, b):
    return lax.dot_general(a, b, (((1,), (1,)), ((), ())), preferred_element_type=F32)


def place_table():
    table = np.zeros((3, LANES, STEM_ROWS), np.float32)
    for even_odd in range(2):
        for a in range(3):
            for b in range(3):
                for d in range(3):
                    q = 2 * even_odd + d - 1
                    group, phase = (2, 3) if q < 0 else (even_odd, q)
                    for c in range(4):
                        column = 48 * a + 16 * b + 4 * phase + c
                        table[group, 4 * (9 * a + 3 * b + d) + c, column] = 1.0
    return table


def rows_lanes(shape):
    return lax.broadcasted_iota(jnp.int32, shape, 0), lax.broadcasted_iota(jnp.int32, shape, 1)


def turn_matrix():
    row, column = rows_lanes((256, 256))
    source = lax.shift_left(row & 15, 4) + lax.shift_right_logical(row, 4)
    return (source == column).astype(F32).astype(BF16)


def regroup_kernel(volume_in, weight_in, cotangent_in, own, slab_x, packed_out, volume, weight, cotangent, packed, sems):
    channels, planes, width, depth = volume.shape
    pairs = [(weight_in, weight), (cotangent_in, cotangent), (packed, packed_out)]
    pairs += [(volume_in.at[c], volume.at[c]) for c in range(channels)]
    copies = [pltpu.make_async_copy(*pair, sems.at[k]) for k, pair in enumerate(pairs)]
    for copy in copies[:2] + copies[3:]:
        copy.start()
    z, column = rows_lanes((depth, depth))
    source = lax.shift_left(column & (LANES - 1), 2) + lax.shift_right_logical(column, 7)
    select = (z == source).astype(F32).astype(BF16)
    turn = turn_matrix()

    blank = jnp.zeros((16, 32), BF16)
    copies[0].wait()
    taps = [weight[t] if t < 27 else blank for t in range(28)]
    for t in range(7):
        tile = jnp.concatenate(taps[4 * t : 4 * t + 4], axis=1)
        for f in range(packed.shape[0]):
            packed[f, t] = tile
    copies[1].wait()
    turned = nn(turn, cotangent[...].reshape(256, LANES)).astype(BF16)
    for k, f in enumerate(exchange_order(packed.shape[0])):
        for j in range(4):
            row = 16 * (4 * f + j)
            packed[k, 7 + j] = turned[row : row + 16]
    copies[2].start()

    for copy in copies[3:]:
        copy.wait()
    picked = nn(volume[...].reshape(channels * planes * width, depth), select).astype(BF16)
    grouped = []
    for x in range(planes):
        parts = []
        for phase in range(4):
            for c in range(channels):
                start = (c * planes + x) * width
                parts.append(picked[start : start + width, phase * LANES : (phase + 1) * LANES])
        grouped.append(jnp.concatenate(parts, axis=0))
    turned = nn(turn, jnp.concatenate(grouped, axis=1)).astype(BF16)
    for x in range(planes):
        plane = turned[:, x * LANES : (x + 1) * LANES]
        own[x] = plane
        if x > 0:
            slab_x[x - 1] = plane
    copies[2].wait()


def border_kernel(slab_x, own, border):
    for x in range(3):
        border[x] = slab_x[x, -48:]
    for x in range(4):
        border[3 + x] = own[x, -48:]


def softplus_sigmoid(values):
    small = jnp.exp(-jnp.abs(values))
    inverse = 1.0 / (1.0 + small)
    soft = jnp.maximum(values, 0.0) + jnp.log(1.0 + small)
    return soft, jnp.where(values >= 0.0, inverse, small * inverse)


def roll_blocks(values, amount):
    blocks = []
    for start in range(0, values.shape[1], LANES):
        block = values[:, start : start + LANES]
        lane = lax.broadcasted_iota(jnp.int32, block.shape, 1)
        edge = 0 if amount == 1 else LANES - 1
        blocks.append(jnp.where(lane == edge, 0.0, pltpu.roll(block, amount % LANES, 1)))
    return jnp.concatenate(blocks, axis=1)


def fill_columns(cols, planes, count):
    for x, plane in enumerate(planes):
        for j in range(count):
            cols[x, :, pl.ds(j * LANES, LANES)] = plane[32 * j : 32 * j + 48]


def stem_forward(weights, cols, i, keep):
    pre = nn(weights, cols[2 * i : 2 * i + 3].reshape(STEM_ROWS, cols.shape[2]))
    pre = jnp.concatenate([pre[0:32] + roll_blocks(pre[64:96], 1), pre[32:64]], axis=0)
    soft, sig = softplus_sigmoid(pre)
    act = (0.3 * pre + 0.7 * soft) * keep
    taps = jnp.concatenate([roll_blocks(act[32:64], 1), act], axis=0).astype(BF16)
    return (0.3 + 0.7 * sig) * keep, taps


def keep_space():
    return jnp.where(lax.axis_index("space") > 0, 1.0, 0.0).astype(F32)


def fill_taps(mid_cols, part, i, j, first, count):
    for b in range(3):
        if (j - b) % 2 == 0 and first <= (j - b) // 2 < first + count:
            row = 96 * (3 * i + b)
            mid_cols[row : row + 96, pl.ds(((j - b) // 2 - first) * LANES, LANES)] = part


def inner_kernel(own, slab_x, stem_w, place, weights, cols, slope, mid_cols, near_taps):
    weights[...] = jnp.concatenate([nn(stem_w[...], place[g]) for g in range(3)], axis=0).astype(BF16)
    planes = [slab_x[x, 16:256] if x < 3 else own[x - 3, 16:256] for x in range(7)]
    fill_columns(cols, planes, 7)
    for i in range(3):
        slope[i], taps = stem_forward(weights[...], cols, i, keep_space() if i == 0 else 1.0)
        for j in range(2, 9):
            fill_taps(mid_cols, taps[:, (j - 2) * LANES : (j - 1) * LANES], i, j, 1, 3)
        near_taps[i] = taps[:, 0:LANES]


def middle_cells_step(mid_w, mid_cols, cotangent):
    pre = nn(mid_w[:, 0:864], mid_cols[...])
    soft, sig = softplus_sigmoid(pre)
    delta = cotangent.astype(F32) * (0.3 + 0.7 * sig)
    delta_low = delta.astype(BF16)
    mid_grad = nt(delta_low, mid_cols[...])
    both = jnp.concatenate([delta_low, roll_blocks(delta, -1).astype(BF16)], axis=0)
    return (0.3 * pre + 0.7 * soft).astype(BF16), mid_grad, both


def put_back(target, i, start, part):
    lanes = pl.ds(start, LANES)
    target[i, 0:64, lanes] = part.astype(BF16)
    target[i, 64:96, lanes] = roll_blocks(part[0:32], -1).astype(BF16)


def upper_kernel(
    gathered, cols, slope, mid_cols, features, mid_grad, stem_grad, mid_w, odd_w, even_w, stem_back,
):
    blocks = gathered.shape[0]
    order = exchange_order(blocks)
    for k, f in enumerate(order):
        for t in range(7):
            mid_w[16 * f : 16 * f + 16, t * LANES : (t + 1) * LANES] = gathered[k, t]
    cotangent = jnp.concatenate(
        [jnp.concatenate([gathered[order.index(f), 7 + j] for j in range(1, 4)], axis=1) for f in range(blocks)],
        axis=0,
    )
    features[...], mid_grad[...], both = middle_cells_step(mid_w, mid_cols, cotangent)

    turned = jnp.concatenate(
        [mid_w[:, t * LANES : (t + 1) * LANES].astype(F32).T for t in range(7)], axis=0
    ).astype(BF16)
    zero = jnp.zeros((32, blocks * 16), BF16)

    def block(a, b, d):
        row = 32 * (9 * a + 3 * b + d)
        return turned[row : row + 32]

    def wide(a, b):
        even = jnp.concatenate([block(a, b, 1), zero], axis=1)
        odd = jnp.concatenate([block(a, b, 2), block(a, b, 0)], axis=1)
        return jnp.concatenate([even, odd], axis=0)

    odd_w[...] = jnp.concatenate([wide(i, 1) for i in range(3)], axis=0)
    even_w[...] = jnp.concatenate(
        [jnp.concatenate([wide(i, 0), wide(i, 2)], axis=1) for i in range(3)], axis=0
    )
    nothing = jnp.zeros((2 * blocks * 16, LANES), BF16)
    pair = jnp.concatenate(
        [jnp.concatenate([both, nothing], axis=1), jnp.concatenate([nothing, both], axis=1)], axis=0
    )
    odd_back = nn(odd_w[...], both)
    even_back = nn(even_w[...], pair)
    total = jnp.zeros((96, STEM_ROWS), F32)
    for i in range(3):
        for j in range(7):
            source = even_back if j % 2 == 0 else odd_back
            part = source[64 * i : 64 * i + 64, (j // 2) * LANES : (j // 2 + 1) * LANES]
            put_back(stem_back, i, j * LANES, part * slope[i, :, pl.ds(j * LANES, LANES)])
        total += nt(stem_back[i], cols[2 * i : 2 * i + 3].reshape(STEM_ROWS, 7 * LANES))
    stem_grad[...] = total


def lower_kernel(
    own, slab_x, border, place, gathered, weights, cols, slope, near_taps, upper_features, upper_mid, upper_stem,
    mid_w, odd_w, even_w, parts, low_cols, mid_cols, low_back,
):
    blocks = gathered.shape[0]
    keep_y = jnp.where(lax.axis_index("filt") > 0, 1.0, 0.0).astype(F32)
    planes = [
        jnp.concatenate([border[x], slab_x[x, 0:32] if x < 3 else own[x - 3, 0:32]], axis=0)
        for x in range(7)
    ]
    fill_columns(low_cols, planes, 2)
    low_slope = []
    for i in range(3):
        keep = jnp.where(lax.broadcasted_iota(jnp.int32, (64, 2 * LANES), 1) < LANES, keep_y, 1.0)
        if i == 0:
            keep = keep * keep_space()
        one_slope, low_taps = stem_forward(weights[...], low_cols, i, keep)
        low_slope.append(one_slope)
        for j in range(2):
            fill_taps(mid_cols, low_taps[:, j * LANES : (j + 1) * LANES], i, j, 0, 1)
        fill_taps(mid_cols, near_taps[i], i, 2, 0, 1)
    order = exchange_order(blocks)
    cotangent = jnp.concatenate([gathered[order.index(f), 7] for f in range(blocks)], axis=0)
    features, mid_grad, both = middle_cells_step(mid_w, mid_cols, cotangent)

    back = [nn(even_w[:, 0:LANES], both), nn(odd_w[...], both), nn(even_w[:, LANES:], both)]
    stem_grad = upper_stem[...]
    for i in range(3):
        for j in range(2):
            part = back[j][64 * i : 64 * i + 64] * low_slope[i][:, j * LANES : (j + 1) * LANES]
            put_back(low_back, i, j * LANES, part)
        put_back(low_back, i, 2 * LANES, back[2][64 * i : 64 * i + 64] * slope[i, :, 0:LANES])
        low = low_cols[2 * i : 2 * i + 3].reshape(STEM_ROWS, 2 * LANES)
        near = cols[2 * i : 2 * i + 3, :, 0:LANES].reshape(STEM_ROWS, LANES)
        stem_grad += nt(low_back[i], jnp.concatenate([low, near], axis=1))
    high = stem_grad.astype(BF16)
    both = jnp.concatenate([high, (stem_grad - high.astype(F32)).astype(BF16)], axis=0)
    stem = 0.0
    for g in range(3):
        rows = jnp.concatenate([both[32 * g : 32 * g + 32], both[96 + 32 * g : 128 + 32 * g]], axis=0)
        taken = nt(rows, place[g])
        stem += taken[0:32] + taken[32:64]
    stem = stem.astype(BF16)

    middle = (mid_grad + upper_mid[...]).astype(BF16)
    middle = jnp.concatenate([middle, jnp.zeros((blocks * 16, 32), BF16)], axis=1)
    for k, f in enumerate(order):
        rows = slice(16 * f, 16 * f + 16)
        for t in range(7):
            parts[k, t] = middle[rows, t * LANES : (t + 1) * LANES]
        for half in range(2):
            parts[k, 7 + half] = stem[16 * half : 16 * half + 16]
        parts[k, 9] = features[rows]
        for j in range(3):
            parts[k, 10 + j] = upper_features[rows, j * LANES : (j + 1) * LANES]


def sum_kernel(parts, sums):
    sums[...] = jnp.sum(parts[:, 0:9].astype(F32), axis=0).astype(BF16)


def unpack_kernel(
    middle_scale, stem_scale, sums, parts, features_out, middle_out, stem_out, features, middle, stem, sems,
):
    copies = [
        pltpu.make_async_copy(source, target, sems.at[k])
        for k, (source, target) in enumerate(
            [(middle, middle_out), (stem, stem_out), (features, features_out)]
        )
    ]
    total = jnp.sum(sums[...].astype(F32), axis=0)
    for t in range(27):
        start = 32 * (t % 4)
        middle[t] = total[t // 4, :, start : start + 32] * middle_scale
    copies[0].start()
    order = exchange_order(parts.shape[0])
    rows = [parts[order.index(f), 9 + j] for f in range(parts.shape[0]) for j in range(4)]
    features[...] = nn(turn_matrix(), jnp.concatenate(rows, axis=0)).astype(BF16).reshape(16, 16, LANES)
    copies[2].start()
    turned = jnp.concatenate([total[7], total[8]], axis=0).T * stem_scale
    for t in range(27):
        stem[t] = turned[4 * t : 4 * t + 4]
    copies[1].start()
    for copy in copies:
        copy.wait()


def exchange_order(filts):
    return sorted(range(filts), key=lambda f: (abs(f - filts // 2), f))


def exchange(chunks):
    groups = [exchange_order(lax.axis_size("filt"))]
    return lax.all_to_all(chunks, "filt", 0, 0, axis_index_groups=groups, tiled=True)


def whole(count):
    return [pl.BlockSpec(memory_space=pltpu.VMEM)] * count


def body(volume, stem_weight, middle_weight, cotangent):
    spaces, filts = lax.axis_size("space"), lax.axis_size("filt")
    channels, planes, width, depth = volume.shape
    stem_cells = (planes // 2) * spaces * (width // 2) * filts * (depth // 2)
    middle_cells = stem_cells // 8
    limit = pltpu.CompilerParams(vmem_limit_bytes=48 * 1024 * 1024)

    raw = (volume, middle_weight.transpose(0, 2, 1), cotangent.reshape(16, 16, LANES))
    own, slab_x, packed = pl.pallas_call(
        regroup_kernel,
        out_shape=[
            jax.ShapeDtypeStruct((planes, 16 * width, LANES), BF16),
            jax.ShapeDtypeStruct((planes - 1, 16 * width, LANES), BF16),
            jax.ShapeDtypeStruct((filts, 11, 16, LANES), BF16),
        ],
        in_specs=[pl.BlockSpec(memory_space=pltpu.HBM)] * 3,
        out_specs=whole(2) + [pl.BlockSpec(memory_space=pl.ANY)],
        scratch_shapes=[
            pltpu.VMEM(volume.shape, BF16),
            pltpu.VMEM((27, 16, 32), BF16),
            pltpu.VMEM((16, 16, LANES), BF16),
            pltpu.VMEM((filts, 11, 16, LANES), BF16),
            pltpu.SemaphoreType.DMA((3 + channels,)),
        ],
        compiler_params=limit,
        name="regroup",
    )(*[pltpu.with_memory_space_constraint(x, pltpu.HBM) for x in raw])
    slab_x = lax.ppermute(slab_x, "space", [(s - 1, s) for s in range(1, spaces)])
    gathered = exchange(packed)
    border = pl.pallas_call(
        border_kernel,
        out_shape=jax.ShapeDtypeStruct((7, 48, LANES), BF16),
        in_specs=whole(2),
        out_specs=whole(1)[0],
        compiler_params=limit,
        name="border",
    )(slab_x, own)
    border = lax.ppermute(border, "filt", [(f - 1, f) for f in range(1, filts)])

    stem_w = jnp.pad(stem_weight.reshape(108, 32).T, ((0, 0), (0, 20)))
    place = jnp.asarray(place_table(), BF16)
    weights, cols, slope, mid_cols, near_taps = pl.pallas_call(
        inner_kernel,
        out_shape=[
            jax.ShapeDtypeStruct((96, STEM_ROWS), BF16),
            jax.ShapeDtypeStruct((7, 48, 7 * LANES), BF16),
            jax.ShapeDtypeStruct((3, 64, 7 * LANES), F32),
            jax.ShapeDtypeStruct((864, 3 * LANES), BF16),
            jax.ShapeDtypeStruct((3, 96, LANES), BF16),
        ],
        in_specs=whole(4),
        out_specs=whole(5),
        compiler_params=limit,
        cost_estimate=pl.CostEstimate(flops=200_000_000, bytes_accessed=4_000_000, transcendentals=500_000),
        name="stem_inner",
    )(own, slab_x, stem_w, place)
    upper = pl.pallas_call(
        upper_kernel,
        out_shape=[
            jax.ShapeDtypeStruct((64, 3 * LANES), BF16),
            jax.ShapeDtypeStruct((64, 864), F32),
            jax.ShapeDtypeStruct((96, STEM_ROWS), F32),
            jax.ShapeDtypeStruct((64, 896), BF16),
            jax.ShapeDtypeStruct((192, LANES), BF16),
            jax.ShapeDtypeStruct((192, 2 * LANES), BF16),
        ],
        in_specs=whole(4),
        out_specs=whole(6),
        scratch_shapes=[pltpu.VMEM((3, 96, 7 * LANES), BF16)],
        compiler_params=limit,
        name="upper_cells",
    )(gathered, cols, slope, mid_cols)
    parts = pl.pallas_call(
        lower_kernel,
        out_shape=jax.ShapeDtypeStruct((filts, 13, 16, LANES), BF16),
        in_specs=whole(15),
        out_specs=whole(1)[0],
        scratch_shapes=[
            pltpu.VMEM((7, 48, 2 * LANES), BF16),
            pltpu.VMEM((864, LANES), BF16),
            pltpu.VMEM((3, 96, 3 * LANES), BF16),
        ],
        compiler_params=limit,
        cost_estimate=pl.CostEstimate(flops=600_000_000, bytes_accessed=8_000_000, transcendentals=500_000),
        name="lower_cells",
    )(own, slab_x, border, place, gathered, weights, cols, slope, near_taps, *upper)

    parts = exchange(parts)
    sums = pl.pallas_call(
        sum_kernel,
        out_shape=jax.ShapeDtypeStruct((9, 16, LANES), BF16),
        in_specs=whole(1),
        out_specs=whole(1)[0],
        compiler_params=limit,
        name="sums",
    )(parts)
    around = [(s + 2) % spaces for s in range(spaces)]
    sums = lax.all_gather(sums, "space", axis_index_groups=[around])
    features, middle, stem = pl.pallas_call(
        functools.partial(unpack_kernel, middle_cells**-0.5, stem_cells**-0.5),
        out_shape=[
            jax.ShapeDtypeStruct((16, 16, LANES), BF16),
            jax.ShapeDtypeStruct((27, 16, 32), F32),
            jax.ShapeDtypeStruct((27, 4, 32), F32),
        ],
        in_specs=whole(2),
        out_specs=[pl.BlockSpec(memory_space=pl.ANY)] * 3,
        scratch_shapes=[
            pltpu.VMEM((16, 16, LANES), BF16),
            pltpu.VMEM((27, 16, 32), F32),
            pltpu.VMEM((27, 4, 32), F32),
            pltpu.SemaphoreType.DMA((3,)),
        ],
        compiler_params=limit,
        name="unpack",
    )(sums, parts)
    return features.reshape(16, 1, 16, LANES), middle.transpose(0, 2, 1), stem


def solution(mesh):
    in_specs = (
        P(None, "space", "filt", None),
        P(),
        P(None, None, "filt"),
        P("filt", "space", None, None),
    )
    out_specs = (P("filt", "space", None, None), P(None, None, "filt"), P())
    return jax.shard_map(body, mesh=mesh, in_specs=in_specs, out_specs=out_specs, check_vma=False)
```

```python
import functools

import jax
import jax.numpy as jnp
import numpy as np
from jax import lax
from jax.experimental import pallas as pl
from jax.experimental.pallas import tpu as pltpu
from jax.sharding import PartitionSpec as P

F32 = jnp.float32
BF16 = jnp.bfloat16
LANES = 128
STEM_ROWS = 144


def nn(a, b):
    return lax.dot_general(a, b, (((1,), (0,)), ((), ())), preferred_element_type=F32)


def nt(a, b):
    return lax.dot_general(a, b, (((1,), (1,)), ((), ())), preferred_element_type=F32)


def place_table():
    table = np.zeros((3, LANES, STEM_ROWS), np.float32)
    for even_odd in range(2):
        for a in range(3):
            for b in range(3):
                for d in range(3):
                    q = 2 * even_odd + d - 1
                    group, phase = (2, 3) if q < 0 else (even_odd, q)
                    for c in range(4):
                        column = 48 * a + 16 * b + 4 * phase + c
                        table[group, 4 * (9 * a + 3 * b + d) + c, column] = 1.0
    return table


def rows_lanes(shape):
    return lax.broadcasted_iota(jnp.int32, shape, 0), lax.broadcasted_iota(jnp.int32, shape, 1)


def turn_matrix():
    row, column = rows_lanes((256, 256))
    source = lax.shift_left(row & 15, 4) + lax.shift_right_logical(row, 4)
    return (source == column).astype(F32).astype(BF16)


def regroup_kernel(volume_in, weight_in, cotangent_in, own, slab_x, packed_out, volume, weight, cotangent, packed, sems):
    channels, planes, width, depth = volume.shape
    pairs = [(weight_in, weight), (cotangent_in, cotangent), (packed, packed_out)]
    pairs += [(volume_in.at[c], volume.at[c]) for c in range(channels)]
    copies = [pltpu.make_async_copy(*pair, sems.at[k]) for k, pair in enumerate(pairs)]
    for copy in copies[:2] + copies[3:]:
        copy.start()
    z, column = rows_lanes((depth, depth))
    source = lax.shift_left(column & (LANES - 1), 2) + lax.shift_right_logical(column, 7)
    select = (z == source).astype(F32).astype(BF16)
    turn = turn_matrix()

    blank = jnp.zeros((16, 32), BF16)
    copies[0].wait()
    taps = [weight[t] if t < 27 else blank for t in range(28)]
    for t in range(7):
        tile = jnp.concatenate(taps[4 * t : 4 * t + 4], axis=1)
        for f in range(packed.shape[0]):
            packed[f, t] = tile
    copies[1].wait()
    turned = nn(turn, cotangent[...].reshape(256, LANES)).astype(BF16)
    for k, f in enumerate(exchange_order(packed.shape[0])):
        for j in range(4):
            row = 16 * (4 * f + j)
            packed[k, 7 + j] = turned[row : row + 16]
    copies[2].start()

    for copy in copies[3:]:
        copy.wait()
    picked = nn(volume[...].reshape(channels * planes * width, depth), select).astype(BF16)
    grouped = []
    for x in range(planes):
        parts = []
        for phase in range(4):
            for c in range(channels):
                start = (c * planes + x) * width
                parts.append(picked[start : start + width, phase * LANES : (phase + 1) * LANES])
        grouped.append(jnp.concatenate(parts, axis=0))
    turned = nn(turn, jnp.concatenate(grouped, axis=1)).astype(BF16)
    for x in range(planes):
        plane = turned[:, x * LANES : (x + 1) * LANES]
        own[x] = plane
        if x > 0:
            slab_x[x - 1] = plane
    copies[2].wait()


def border_kernel(slab_x, own, border):
    for x in range(3):
        border[x] = slab_x[x, -48:]
    for x in range(4):
        border[3 + x] = own[x, -48:]


def softplus_sigmoid(values):
    small = jnp.exp(-jnp.abs(values))
    inverse = 1.0 / (1.0 + small)
    soft = jnp.maximum(values, 0.0) + jnp.log(1.0 + small)
    return soft, jnp.where(values >= 0.0, inverse, small * inverse)


def roll_blocks(values, amount):
    blocks = []
    for start in range(0, values.shape[1], LANES):
        block = values[:, start : start + LANES]
        lane = lax.broadcasted_iota(jnp.int32, block.shape, 1)
        edge = 0 if amount == 1 else LANES - 1
        blocks.append(jnp.where(lane == edge, 0.0, pltpu.roll(block, amount % LANES, 1)))
    return jnp.concatenate(blocks, axis=1)


def fill_columns(cols, planes, count):
    for x, plane in enumerate(planes):
        for j in range(count):
            cols[x, :, pl.ds(j * LANES, LANES)] = plane[32 * j : 32 * j + 48]


def stem_forward(weights, cols, i, keep):
    pre = nn(weights, cols[2 * i : 2 * i + 3].reshape(STEM_ROWS, cols.shape[2]))
    pre = jnp.concatenate([pre[0:32] + roll_blocks(pre[64:96], 1), pre[32:64]], axis=0)
    soft, sig = softplus_sigmoid(pre)
    act = (0.3 * pre + 0.7 * soft) * keep
    taps = jnp.concatenate([roll_blocks(act[32:64], 1), act], axis=0).astype(BF16)
    return (0.3 + 0.7 * sig) * keep, taps


def keep_space():
    return jnp.where(lax.axis_index("space") > 0, 1.0, 0.0).astype(F32)


def fill_taps(mid_cols, part, i, j, first, count):
    for b in range(3):
        if (j - b) % 2 == 0 and first <= (j - b) // 2 < first + count:
            row = 96 * (3 * i + b)
            mid_cols[row : row + 96, pl.ds(((j - b) // 2 - first) * LANES, LANES)] = part


def inner_kernel(own, slab_x, stem_w, place, weights, cols, slope, mid_cols, near_taps):
    weights[...] = jnp.concatenate([nn(stem_w[...], place[g]) for g in range(3)], axis=0).astype(BF16)
    planes = [slab_x[x, 16:256] if x < 3 else own[x - 3, 16:256] for x in range(7)]
    fill_columns(cols, planes, 7)
    for i in range(3):
        slope[i], taps = stem_forward(weights[...], cols, i, keep_space() if i == 0 else 1.0)
        for j in range(2, 9):
            fill_taps(mid_cols, taps[:, (j - 2) * LANES : (j - 1) * LANES], i, j, 1, 3)
        near_taps[i] = taps[:, 0:LANES]


def middle_cells_step(mid_w, mid_cols, cotangent):
    pre = nn(mid_w[:, 0:864], mid_cols[...])
    soft, sig = softplus_sigmoid(pre)
    delta = cotangent.astype(F32) * (0.3 + 0.7 * sig)
    delta_low = delta.astype(BF16)
    mid_grad = nt(delta_low, mid_cols[...])
    both = jnp.concatenate([delta_low, roll_blocks(delta, -1).astype(BF16)], axis=0)
    return (0.3 * pre + 0.7 * soft).astype(BF16), mid_grad, both


def put_back(target, i, start, part):
    lanes = pl.ds(start, LANES)
    target[i, 0:64, lanes] = part.astype(BF16)
    target[i, 64:96, lanes] = roll_blocks(part[0:32], -1).astype(BF16)


def upper_kernel(
    gathered, cols, slope, mid_cols, features, mid_grad, stem_grad, mid_w, odd_w, even_w, stem_back,
):
    blocks = gathered.shape[0]
    order = exchange_order(blocks)
    for k, f in enumerate(order):
        for t in range(7):
            mid_w[16 * f : 16 * f + 16, t * LANES : (t + 1) * LANES] = gathered[k, t]
    cotangent = jnp.concatenate(
        [jnp.concatenate([gathered[order.index(f), 7 + j] for j in range(1, 4)], axis=1) for f in range(blocks)],
        axis=0,
    )
    features[...], mid_grad[...], both = middle_cells_step(mid_w, mid_cols, cotangent)

    turned = jnp.concatenate(
        [mid_w[:, t * LANES : (t + 1) * LANES].astype(F32).T for t in range(7)], axis=0
    ).astype(BF16)
    zero = jnp.zeros((32, blocks * 16), BF16)

    def block(a, b, d):
        row = 32 * (9 * a + 3 * b + d)
        return turned[row : row + 32]

    def wide(a, b):
        even = jnp.concatenate([block(a, b, 1), zero], axis=1)
        odd = jnp.concatenate([block(a, b, 2), block(a, b, 0)], axis=1)
        return jnp.concatenate([even, odd], axis=0)

    odd_w[...] = jnp.concatenate([wide(i, 1) for i in range(3)], axis=0)
    even_w[...] = jnp.concatenate(
        [jnp.concatenate([wide(i, 0), wide(i, 2)], axis=1) for i in range(3)], axis=0
    )
    nothing = jnp.zeros((2 * blocks * 16, LANES), BF16)
    pair = jnp.concatenate(
        [jnp.concatenate([both, nothing], axis=1), jnp.concatenate([nothing, both], axis=1)], axis=0
    )
    odd_back = nn(odd_w[...], both)
    even_back = nn(even_w[...], pair)
    total = jnp.zeros((96, STEM_ROWS), F32)
    for i in range(3):
        for j in range(7):
            source = even_back if j % 2 == 0 else odd_back
            part = source[64 * i : 64 * i + 64, (j // 2) * LANES : (j // 2 + 1) * LANES]
            put_back(stem_back, i, j * LANES, part * slope[i, :, pl.ds(j * LANES, LANES)])
        total += nt(stem_back[i], cols[2 * i : 2 * i + 3].reshape(STEM_ROWS, 7 * LANES))
    stem_grad[...] = total


def lower_kernel(
    own, slab_x, border, place, gathered, weights, cols, slope, near_taps, upper_features, upper_mid, upper_stem,
    mid_w, odd_w, even_w, parts, low_cols, mid_cols, low_back,
):
    blocks = gathered.shape[0]
    keep_y = jnp.where(lax.axis_index("filt") > 0, 1.0, 0.0).astype(F32)
    planes = [
        jnp.concatenate([border[x], slab_x[x, 0:32] if x < 3 else own[x - 3, 0:32]], axis=0)
        for x in range(7)
    ]
    fill_columns(low_cols, planes, 2)
    low_slope = []
    for i in range(3):
        keep = jnp.where(lax.broadcasted_iota(jnp.int32, (64, 2 * LANES), 1) < LANES, keep_y, 1.0)
        if i == 0:
            keep = keep * keep_space()
        one_slope, low_taps = stem_forward(weights[...], low_cols, i, keep)
        low_slope.append(one_slope)
        for j in range(2):
            fill_taps(mid_cols, low_taps[:, j * LANES : (j + 1) * LANES], i, j, 0, 1)
        fill_taps(mid_cols, near_taps[i], i, 2, 0, 1)
    order = exchange_order(blocks)
    cotangent = jnp.concatenate([gathered[order.index(f), 7] for f in range(blocks)], axis=0)
    features, mid_grad, both = middle_cells_step(mid_w, mid_cols, cotangent)

    back = [nn(even_w[:, 0:LANES], both), nn(odd_w[...], both), nn(even_w[:, LANES:], both)]
    stem_grad = upper_stem[...]
    for i in range(3):
        for j in range(2):
            part = back[j][64 * i : 64 * i + 64] * low_slope[i][:, j * LANES : (j + 1) * LANES]
            put_back(low_back, i, j * LANES, part)
        put_back(low_back, i, 2 * LANES, back[2][64 * i : 64 * i + 64] * slope[i, :, 0:LANES])
        low = low_cols[2 * i : 2 * i + 3].reshape(STEM_ROWS, 2 * LANES)
        near = cols[2 * i : 2 * i + 3, :, 0:LANES].reshape(STEM_ROWS, LANES)
        stem_grad += nt(low_back[i], jnp.concatenate([low, near], axis=1))
    high = stem_grad.astype(BF16)
    both = jnp.concatenate([high, (stem_grad - high.astype(F32)).astype(BF16)], axis=0)
    stem = 0.0
    for g in range(3):
        rows = jnp.concatenate([both[32 * g : 32 * g + 32], both[96 + 32 * g : 128 + 32 * g]], axis=0)
        taken = nt(rows, place[g])
        stem += taken[0:32] + taken[32:64]
    stem = stem.astype(BF16)

    middle = (mid_grad + upper_mid[...]).astype(BF16)
    middle = jnp.concatenate([middle, jnp.zeros((blocks * 16, 32), BF16)], axis=1)
    for k, f in enumerate(order):
        rows = slice(16 * f, 16 * f + 16)
        for t in range(7):
            parts[k, t] = middle[rows, t * LANES : (t + 1) * LANES]
        for half in range(2):
            parts[k, 7 + half] = stem[16 * half : 16 * half + 16]
        parts[k, 9] = features[rows]
        for j in range(3):
            parts[k, 10 + j] = upper_features[rows, j * LANES : (j + 1) * LANES]


def sum_kernel(parts, sums):
    sums[...] = jnp.sum(parts[:, 0:9].astype(F32), axis=0).astype(BF16)


def unpack_kernel(
    middle_scale, stem_scale, sums, parts, features_out, middle_out, stem_out, features, middle, stem, sems,
):
    copies = [
        pltpu.make_async_copy(source, target, sems.at[k])
        for k, (source, target) in enumerate(
            [(middle, middle_out), (stem, stem_out), (features, features_out)]
        )
    ]
    total = jnp.sum(sums[...].astype(F32), axis=0)
    for t in range(27):
        start = 32 * (t % 4)
        middle[t] = total[t // 4, :, start : start + 32] * middle_scale
    copies[0].start()
    order = exchange_order(parts.shape[0])
    rows = [parts[order.index(f), 9 + j] for f in range(parts.shape[0]) for j in range(4)]
    features[...] = nn(turn_matrix(), jnp.concatenate(rows, axis=0)).astype(BF16).reshape(16, 16, LANES)
    copies[2].start()
    turned = jnp.concatenate([total[7], total[8]], axis=0).T * stem_scale
    for t in range(27):
        stem[t] = turned[4 * t : 4 * t + 4]
    copies[1].start()
    for copy in copies:
        copy.wait()


def exchange_order(filts):
    return sorted(range(filts), key=lambda f: (abs(f - filts // 2), f))


def exchange(chunks):
    groups = [exchange_order(lax.axis_size("filt"))]
    return lax.all_to_all(chunks, "filt", 0, 0, axis_index_groups=groups, tiled=True)


def whole(count):
    return [pl.BlockSpec(memory_space=pltpu.VMEM)] * count


def body(volume, stem_weight, middle_weight, cotangent):
    spaces, filts = lax.axis_size("space"), lax.axis_size("filt")
    channels, planes, width, depth = volume.shape
    stem_cells = (planes // 2) * spaces * (width // 2) * filts * (depth // 2)
    middle_cells = stem_cells // 8
    limit = pltpu.CompilerParams(vmem_limit_bytes=48 * 1024 * 1024)

    raw = (volume, middle_weight.transpose(0, 2, 1), cotangent.reshape(16, 16, LANES))
    own, slab_x, packed = pl.pallas_call(
        regroup_kernel,
        out_shape=[
            jax.ShapeDtypeStruct((planes, 16 * width, LANES), BF16),
            jax.ShapeDtypeStruct((planes - 1, 16 * width, LANES), BF16),
            jax.ShapeDtypeStruct((filts, 11, 16, LANES), BF16),
        ],
        in_specs=[pl.BlockSpec(memory_space=pltpu.HBM)] * 3,
        out_specs=whole(2) + [pl.BlockSpec(memory_space=pl.ANY)],
        scratch_shapes=[
            pltpu.VMEM(volume.shape, BF16),
            pltpu.VMEM((27, 16, 32), BF16),
            pltpu.VMEM((16, 16, LANES), BF16),
            pltpu.VMEM((filts, 11, 16, LANES), BF16),
            pltpu.SemaphoreType.DMA((3 + channels,)),
        ],
        compiler_params=limit,
        name="regroup",
    )(*[pltpu.with_memory_space_constraint(x, pltpu.HBM) for x in raw])
    slab_x = lax.ppermute(slab_x, "space", [(s - 1, s) for s in range(1, spaces)])
    gathered = exchange(packed)
    border = pl.pallas_call(
        border_kernel,
        out_shape=jax.ShapeDtypeStruct((7, 48, LANES), BF16),
        in_specs=whole(2),
        out_specs=whole(1)[0],
        compiler_params=limit,
        name="border",
    )(slab_x, own)
    border = lax.ppermute(border, "filt", [(f - 1, f) for f in range(1, filts)])

    stem_w = jnp.pad(stem_weight.reshape(108, 32).T, ((0, 0), (0, 20)))
    place = jnp.asarray(place_table(), BF16)
    weights, cols, slope, mid_cols, near_taps = pl.pallas_call(
        inner_kernel,
        out_shape=[
            jax.ShapeDtypeStruct((96, STEM_ROWS), BF16),
            jax.ShapeDtypeStruct((7, 48, 7 * LANES), BF16),
            jax.ShapeDtypeStruct((3, 64, 7 * LANES), F32),
            jax.ShapeDtypeStruct((864, 3 * LANES), BF16),
            jax.ShapeDtypeStruct((3, 96, LANES), BF16),
        ],
        in_specs=whole(4),
        out_specs=whole(5),
        compiler_params=limit,
        cost_estimate=pl.CostEstimate(flops=200_000_000, bytes_accessed=4_000_000, transcendentals=500_000),
        name="stem_inner",
    )(own, slab_x, stem_w, place)
    upper = pl.pallas_call(
        upper_kernel,
        out_shape=[
            jax.ShapeDtypeStruct((64, 3 * LANES), BF16),
            jax.ShapeDtypeStruct((64, 864), F32),
            jax.ShapeDtypeStruct((96, STEM_ROWS), F32),
            jax.ShapeDtypeStruct((64, 896), BF16),
            jax.ShapeDtypeStruct((192, LANES), BF16),
            jax.ShapeDtypeStruct((192, 2 * LANES), BF16),
        ],
        in_specs=whole(4),
        out_specs=whole(6),
        scratch_shapes=[pltpu.VMEM((3, 96, 7 * LANES), BF16)],
        compiler_params=limit,
        name="upper_cells",
    )(gathered, cols, slope, mid_cols)
    parts = pl.pallas_call(
        lower_kernel,
        out_shape=jax.ShapeDtypeStruct((filts, 13, 16, LANES), BF16),
        in_specs=whole(15),
        out_specs=whole(1)[0],
        scratch_shapes=[
            pltpu.VMEM((7, 48, 2 * LANES), BF16),
            pltpu.VMEM((864, LANES), BF16),
            pltpu.VMEM((3, 96, 3 * LANES), BF16),
        ],
        compiler_params=limit,
        cost_estimate=pl.CostEstimate(flops=600_000_000, bytes_accessed=8_000_000, transcendentals=500_000),
        name="lower_cells",
    )(own, slab_x, border, place, gathered, weights, cols, slope, near_taps, *upper)

    parts = exchange(parts)
    sums = pl.pallas_call(
        sum_kernel,
        out_shape=jax.ShapeDtypeStruct((9, 16, LANES), BF16),
        in_specs=whole(1),
        out_specs=whole(1)[0],
        compiler_params=limit,
        name="sums",
    )(parts)
    sums = lax.all_gather(sums, "space")
    features, middle, stem = pl.pallas_call(
        functools.partial(unpack_kernel, middle_cells**-0.5, stem_cells**-0.5),
        out_shape=[
            jax.ShapeDtypeStruct((16, 16, LANES), BF16),
            jax.ShapeDtypeStruct((27, 16, 32), F32),
            jax.ShapeDtypeStruct((27, 4, 32), F32),
        ],
        in_specs=whole(2),
        out_specs=[pl.BlockSpec(memory_space=pl.ANY)] * 3,
        scratch_shapes=[
            pltpu.VMEM((16, 16, LANES), BF16),
            pltpu.VMEM((27, 16, 32), F32),
            pltpu.VMEM((27, 4, 32), F32),
            pltpu.SemaphoreType.DMA((3,)),
        ],
        compiler_params=limit,
        name="unpack",
    )(sums, parts)
    return features.reshape(16, 1, 16, LANES), middle.transpose(0, 2, 1), stem


def solution(mesh):
    in_specs = (
        P(None, "space", "filt", None),
        P(),
        P(None, None, "filt"),
        P("filt", "space", None, None),
    )
    out_specs = (P("filt", "space", None, None), P(None, None, "filt"), P())
    return jax.shard_map(body, mesh=mesh, in_specs=in_specs, out_specs=out_specs, check_vma=False)
```

```python
import functools

import jax
import jax.numpy as jnp
import numpy as np
from jax import lax
from jax.experimental import pallas as pl
from jax.experimental.pallas import tpu as pltpu
from jax.sharding import PartitionSpec as P

F32 = jnp.float32
BF16 = jnp.bfloat16
LANES = 128
STEM_ROWS = 144


def nn(a, b):
    return lax.dot_general(a, b, (((1,), (0,)), ((), ())), preferred_element_type=F32)


def nt(a, b):
    return lax.dot_general(a, b, (((1,), (1,)), ((), ())), preferred_element_type=F32)


def place_table():
    table = np.zeros((3, LANES, STEM_ROWS), np.float32)
    for even_odd in range(2):
        for a in range(3):
            for b in range(3):
                for d in range(3):
                    q = 2 * even_odd + d - 1
                    group, phase = (2, 3) if q < 0 else (even_odd, q)
                    for c in range(4):
                        column = 48 * a + 16 * b + 4 * phase + c
                        table[group, 4 * (9 * a + 3 * b + d) + c, column] = 1.0
    return table


def rows_lanes(shape):
    return lax.broadcasted_iota(jnp.int32, shape, 0), lax.broadcasted_iota(jnp.int32, shape, 1)


def turn_matrix():
    row, column = rows_lanes((256, 256))
    source = lax.shift_left(row & 15, 4) + lax.shift_right_logical(row, 4)
    return (source == column).astype(F32).astype(BF16)


def regroup_kernel(volume_in, weight_in, cotangent_in, own, slab_x, packed, volume, weight, cotangent, sems):
    channels, planes, width, depth = volume.shape
    pairs = [(weight_in, weight), (cotangent_in, cotangent)]
    pairs += [(volume_in.at[c], volume.at[c]) for c in range(channels)]
    copies = [pltpu.make_async_copy(*pair, sems.at[k]) for k, pair in enumerate(pairs)]
    for copy in copies:
        copy.start()
    z, column = rows_lanes((depth, depth))
    source = lax.shift_left(column & (LANES - 1), 2) + lax.shift_right_logical(column, 7)
    select = (z == source).astype(F32).astype(BF16)
    turn = turn_matrix()

    blank = jnp.zeros((16, 32), BF16)
    copies[0].wait()
    taps = [weight[t] if t < 27 else blank for t in range(28)]
    for t in range(7):
        tile = jnp.concatenate(taps[4 * t : 4 * t + 4], axis=1)
        for f in range(packed.shape[0]):
            packed[f, t] = tile
    copies[1].wait()
    turned = nn(turn, cotangent[...].reshape(256, LANES)).astype(BF16)
    for k, f in enumerate(exchange_order(packed.shape[0])):
        for j in range(4):
            row = 16 * (4 * f + j)
            packed[k, 7 + j] = turned[row : row + 16]

    for copy in copies[2:]:
        copy.wait()
    picked = nn(volume[...].reshape(channels * planes * width, depth), select).astype(BF16)
    grouped = []
    for x in range(planes):
        parts = []
        for phase in range(4):
            for c in range(channels):
                start = (c * planes + x) * width
                parts.append(picked[start : start + width, phase * LANES : (phase + 1) * LANES])
        grouped.append(jnp.concatenate(parts, axis=0))
    turned = nn(turn, jnp.concatenate(grouped, axis=1)).astype(BF16)
    for x in range(planes):
        plane = turned[:, x * LANES : (x + 1) * LANES]
        own[x] = plane
        if x > 0:
            slab_x[x - 1] = plane


def border_kernel(slab_x, own, border):
    for x in range(3):
        border[x] = slab_x[x, -48:]
    for x in range(4):
        border[3 + x] = own[x, -48:]


def softplus_sigmoid(values):
    small = jnp.exp(-jnp.abs(values))
    inverse = 1.0 / (1.0 + small)
    soft = jnp.maximum(values, 0.0) + jnp.log(1.0 + small)
    return soft, jnp.where(values >= 0.0, inverse, small * inverse)


def roll_blocks(values, amount):
    blocks = []
    for start in range(0, values.shape[1], LANES):
        block = values[:, start : start + LANES]
        lane = lax.broadcasted_iota(jnp.int32, block.shape, 1)
        edge = 0 if amount == 1 else LANES - 1
        blocks.append(jnp.where(lane == edge, 0.0, pltpu.roll(block, amount % LANES, 1)))
    return jnp.concatenate(blocks, axis=1)


def fill_columns(cols, planes, count):
    for x, plane in enumerate(planes):
        for j in range(count):
            cols[x, :, pl.ds(j * LANES, LANES)] = plane[32 * j : 32 * j + 48]


def stem_forward(weights, cols, i, keep):
    pre = nn(weights, cols[2 * i : 2 * i + 3].reshape(STEM_ROWS, cols.shape[2]))
    pre = jnp.concatenate([pre[0:32] + roll_blocks(pre[64:96], 1), pre[32:64]], axis=0)
    soft, sig = softplus_sigmoid(pre)
    act = (0.3 * pre + 0.7 * soft) * keep
    taps = jnp.concatenate([roll_blocks(act[32:64], 1), act], axis=0).astype(BF16)
    return (0.3 + 0.7 * sig) * keep, taps


def keep_space():
    return jnp.where(lax.axis_index("space") > 0, 1.0, 0.0).astype(F32)


def fill_taps(mid_cols, part, i, j, first, count):
    for b in range(3):
        if (j - b) % 2 == 0 and first <= (j - b) // 2 < first + count:
            row = 96 * (3 * i + b)
            mid_cols[row : row + 96, pl.ds(((j - b) // 2 - first) * LANES, LANES)] = part


def inner_kernel(own, slab_x, stem_w, place, weights, cols, slope, mid_cols, near_taps):
    weights[...] = jnp.concatenate([nn(stem_w[...], place[g]) for g in range(3)], axis=0).astype(BF16)
    planes = [slab_x[x, 16:256] if x < 3 else own[x - 3, 16:256] for x in range(7)]
    fill_columns(cols, planes, 7)
    for i in range(3):
        slope[i], taps = stem_forward(weights[...], cols, i, keep_space() if i == 0 else 1.0)
        for j in range(2, 9):
            fill_taps(mid_cols, taps[:, (j - 2) * LANES : (j - 1) * LANES], i, j, 1, 3)
        near_taps[i] = taps[:, 0:LANES]


def middle_cells_step(mid_w, mid_cols, cotangent):
    pre = nn(mid_w[:, 0:864], mid_cols[...])
    soft, sig = softplus_sigmoid(pre)
    delta = cotangent.astype(F32) * (0.3 + 0.7 * sig)
    delta_low = delta.astype(BF16)
    mid_grad = nt(delta_low, mid_cols[...])
    both = jnp.concatenate([delta_low, roll_blocks(delta, -1).astype(BF16)], axis=0)
    return (0.3 * pre + 0.7 * soft).astype(BF16), mid_grad, both


def put_back(target, i, start, part):
    lanes = pl.ds(start, LANES)
    target[i, 0:64, lanes] = part.astype(BF16)
    target[i, 64:96, lanes] = roll_blocks(part[0:32], -1).astype(BF16)


def upper_kernel(
    gathered, cols, slope, mid_cols, features, mid_grad, stem_grad, mid_w, odd_w, even_w, stem_back,
):
    blocks = gathered.shape[0]
    order = exchange_order(blocks)
    for k, f in enumerate(order):
        for t in range(7):
            mid_w[16 * f : 16 * f + 16, t * LANES : (t + 1) * LANES] = gathered[k, t]
    cotangent = jnp.concatenate(
        [jnp.concatenate([gathered[order.index(f), 7 + j] for j in range(1, 4)], axis=1) for f in range(blocks)],
        axis=0,
    )
    features[...], mid_grad[...], both = middle_cells_step(mid_w, mid_cols, cotangent)

    turned = jnp.concatenate(
        [mid_w[:, t * LANES : (t + 1) * LANES].astype(F32).T for t in range(7)], axis=0
    ).astype(BF16)
    zero = jnp.zeros((32, blocks * 16), BF16)

    def block(a, b, d):
        row = 32 * (9 * a + 3 * b + d)
        return turned[row : row + 32]

    def wide(a, b):
        even = jnp.concatenate([block(a, b, 1), zero], axis=1)
        odd = jnp.concatenate([block(a, b, 2), block(a, b, 0)], axis=1)
        return jnp.concatenate([even, odd], axis=0)

    odd_w[...] = jnp.concatenate([wide(i, 1) for i in range(3)], axis=0)
    even_w[...] = jnp.concatenate(
        [jnp.concatenate([wide(i, 0), wide(i, 2)], axis=1) for i in range(3)], axis=0
    )
    nothing = jnp.zeros((2 * blocks * 16, LANES), BF16)
    pair = jnp.concatenate(
        [jnp.concatenate([both, nothing], axis=1), jnp.concatenate([nothing, both], axis=1)], axis=0
    )
    odd_back = nn(odd_w[...], both)
    even_back = nn(even_w[...], pair)
    total = jnp.zeros((96, STEM_ROWS), F32)
    for i in range(3):
        for j in range(7):
            source = even_back if j % 2 == 0 else odd_back
            part = source[64 * i : 64 * i + 64, (j // 2) * LANES : (j // 2 + 1) * LANES]
            put_back(stem_back, i, j * LANES, part * slope[i, :, pl.ds(j * LANES, LANES)])
        total += nt(stem_back[i], cols[2 * i : 2 * i + 3].reshape(STEM_ROWS, 7 * LANES))
    stem_grad[...] = total


def lower_kernel(
    own, slab_x, border, place, gathered, weights, cols, slope, near_taps, upper_features, upper_mid, upper_stem,
    mid_w, odd_w, even_w, parts, low_cols, mid_cols, low_back,
):
    blocks = gathered.shape[0]
    keep_y = jnp.where(lax.axis_index("filt") > 0, 1.0, 0.0).astype(F32)
    planes = [
        jnp.concatenate([border[x], slab_x[x, 0:32] if x < 3 else own[x - 3, 0:32]], axis=0)
        for x in range(7)
    ]
    fill_columns(low_cols, planes, 2)
    low_slope = []
    for i in range(3):
        keep = jnp.where(lax.broadcasted_iota(jnp.int32, (64, 2 * LANES), 1) < LANES, keep_y, 1.0)
        if i == 0:
            keep = keep * keep_space()
        one_slope, low_taps = stem_forward(weights[...], low_cols, i, keep)
        low_slope.append(one_slope)
        for j in range(2):
            fill_taps(mid_cols, low_taps[:, j * LANES : (j + 1) * LANES], i, j, 0, 1)
        fill_taps(mid_cols, near_taps[i], i, 2, 0, 1)
    order = exchange_order(blocks)
    cotangent = jnp.concatenate([gathered[order.index(f), 7] for f in range(blocks)], axis=0)
    features, mid_grad, both = middle_cells_step(mid_w, mid_cols, cotangent)

    back = [nn(even_w[:, 0:LANES], both), nn(odd_w[...], both), nn(even_w[:, LANES:], both)]
    stem_grad = upper_stem[...]
    for i in range(3):
        for j in range(2):
            part = back[j][64 * i : 64 * i + 64] * low_slope[i][:, j * LANES : (j + 1) * LANES]
            put_back(low_back, i, j * LANES, part)
        put_back(low_back, i, 2 * LANES, back[2][64 * i : 64 * i + 64] * slope[i, :, 0:LANES])
        low = low_cols[2 * i : 2 * i + 3].reshape(STEM_ROWS, 2 * LANES)
        near = cols[2 * i : 2 * i + 3, :, 0:LANES].reshape(STEM_ROWS, LANES)
        stem_grad += nt(low_back[i], jnp.concatenate([low, near], axis=1))
    high = stem_grad.astype(BF16)
    both = jnp.concatenate([high, (stem_grad - high.astype(F32)).astype(BF16)], axis=0)
    stem = 0.0
    for g in range(3):
        rows = jnp.concatenate([both[32 * g : 32 * g + 32], both[96 + 32 * g : 128 + 32 * g]], axis=0)
        taken = nt(rows, place[g])
        stem += taken[0:32] + taken[32:64]
    stem = stem.astype(BF16)

    middle = (mid_grad + upper_mid[...]).astype(BF16)
    middle = jnp.concatenate([middle, jnp.zeros((blocks * 16, 32), BF16)], axis=1)
    for k, f in enumerate(order):
        rows = slice(16 * f, 16 * f + 16)
        for t in range(7):
            parts[k, t] = middle[rows, t * LANES : (t + 1) * LANES]
        for half in range(2):
            parts[k, 7 + half] = stem[16 * half : 16 * half + 16]
        parts[k, 9] = features[rows]
        for j in range(3):
            parts[k, 10 + j] = upper_features[rows, j * LANES : (j + 1) * LANES]


def sum_kernel(parts, sums):
    sums[...] = jnp.sum(parts[:, 0:9].astype(F32), axis=0).astype(BF16)


def unpack_kernel(
    middle_scale, stem_scale, sums, parts, features_out, middle_out, stem_out, features, middle, stem, sems,
):
    copies = [
        pltpu.make_async_copy(source, target, sems.at[k])
        for k, (source, target) in enumerate(
            [(middle, middle_out), (stem, stem_out), (features, features_out)]
        )
    ]
    total = jnp.sum(sums[...].astype(F32), axis=0)
    for t in range(27):
        start = 32 * (t % 4)
        middle[t] = total[t // 4, :, start : start + 32] * middle_scale
    copies[0].start()
    order = exchange_order(parts.shape[0])
    rows = [parts[order.index(f), 9 + j] for f in range(parts.shape[0]) for j in range(4)]
    features[...] = nn(turn_matrix(), jnp.concatenate(rows, axis=0)).astype(BF16).reshape(16, 16, LANES)
    copies[2].start()
    turned = jnp.concatenate([total[7], total[8]], axis=0).T * stem_scale
    for t in range(27):
        stem[t] = turned[4 * t : 4 * t + 4]
    copies[1].start()
    for copy in copies:
        copy.wait()


def exchange_order(filts):
    return sorted(range(filts), key=lambda f: (abs(f - filts // 2), f))


def exchange(chunks):
    groups = [exchange_order(lax.axis_size("filt"))]
    return lax.all_to_all(chunks, "filt", 0, 0, axis_index_groups=groups, tiled=True)


def whole(count):
    return [pl.BlockSpec(memory_space=pltpu.VMEM)] * count


def body(volume, stem_weight, middle_weight, cotangent):
    spaces, filts = lax.axis_size("space"), lax.axis_size("filt")
    channels, planes, width, depth = volume.shape
    stem_cells = (planes // 2) * spaces * (width // 2) * filts * (depth // 2)
    middle_cells = stem_cells // 8
    limit = pltpu.CompilerParams(vmem_limit_bytes=48 * 1024 * 1024)

    raw = (volume, middle_weight.transpose(0, 2, 1), cotangent.reshape(16, 16, LANES))
    own, slab_x, packed = pl.pallas_call(
        regroup_kernel,
        out_shape=[
            jax.ShapeDtypeStruct((planes, 16 * width, LANES), BF16),
            jax.ShapeDtypeStruct((planes - 1, 16 * width, LANES), BF16),
            pltpu.VMEM((filts, 11, 16, LANES), BF16),
        ],
        in_specs=[pl.BlockSpec(memory_space=pltpu.HBM)] * 3,
        out_specs=whole(3),
        scratch_shapes=[
            pltpu.VMEM(volume.shape, BF16),
            pltpu.VMEM((27, 16, 32), BF16),
            pltpu.VMEM((16, 16, LANES), BF16),
            pltpu.SemaphoreType.DMA((2 + channels,)),
        ],
        compiler_params=limit,
        name="regroup",
    )(*[pltpu.with_memory_space_constraint(x, pltpu.HBM) for x in raw])
    slab_x = lax.ppermute(slab_x, "space", [(s - 1, s) for s in range(1, spaces)])
    gathered = exchange(packed)
    border = pl.pallas_call(
        border_kernel,
        out_shape=jax.ShapeDtypeStruct((7, 48, LANES), BF16),
        in_specs=whole(2),
        out_specs=whole(1)[0],
        compiler_params=limit,
        name="border",
    )(slab_x, own)
    border = lax.ppermute(border, "filt", [(f - 1, f) for f in range(1, filts)])

    stem_w = jnp.pad(stem_weight.reshape(108, 32).T, ((0, 0), (0, 20)))
    place = jnp.asarray(place_table(), BF16)
    weights, cols, slope, mid_cols, near_taps = pl.pallas_call(
        inner_kernel,
        out_shape=[
            jax.ShapeDtypeStruct((96, STEM_ROWS), BF16),
            jax.ShapeDtypeStruct((7, 48, 7 * LANES), BF16),
            jax.ShapeDtypeStruct((3, 64, 7 * LANES), F32),
            jax.ShapeDtypeStruct((864, 3 * LANES), BF16),
            jax.ShapeDtypeStruct((3, 96, LANES), BF16),
        ],
        in_specs=whole(4),
        out_specs=whole(5),
        compiler_params=limit,
        cost_estimate=pl.CostEstimate(flops=200_000_000, bytes_accessed=4_000_000, transcendentals=500_000),
        name="stem_inner",
    )(own, slab_x, stem_w, place)
    upper = pl.pallas_call(
        upper_kernel,
        out_shape=[
            jax.ShapeDtypeStruct((64, 3 * LANES), BF16),
            jax.ShapeDtypeStruct((64, 864), F32),
            jax.ShapeDtypeStruct((96, STEM_ROWS), F32),
            jax.ShapeDtypeStruct((64, 896), BF16),
            jax.ShapeDtypeStruct((192, LANES), BF16),
            jax.ShapeDtypeStruct((192, 2 * LANES), BF16),
        ],
        in_specs=whole(4),
        out_specs=whole(6),
        scratch_shapes=[pltpu.VMEM((3, 96, 7 * LANES), BF16)],
        compiler_params=limit,
        name="upper_cells",
    )(gathered, cols, slope, mid_cols)
    parts = pl.pallas_call(
        lower_kernel,
        out_shape=jax.ShapeDtypeStruct((filts, 13, 16, LANES), BF16),
        in_specs=whole(15),
        out_specs=whole(1)[0],
        scratch_shapes=[
            pltpu.VMEM((7, 48, 2 * LANES), BF16),
            pltpu.VMEM((864, LANES), BF16),
            pltpu.VMEM((3, 96, 3 * LANES), BF16),
        ],
        compiler_params=limit,
        cost_estimate=pl.CostEstimate(flops=600_000_000, bytes_accessed=8_000_000, transcendentals=500_000),
        name="lower_cells",
    )(own, slab_x, border, place, gathered, weights, cols, slope, near_taps, *upper)

    parts = exchange(parts)
    sums = pl.pallas_call(
        sum_kernel,
        out_shape=jax.ShapeDtypeStruct((9, 16, LANES), BF16),
        in_specs=whole(1),
        out_specs=whole(1)[0],
        compiler_params=limit,
        name="sums",
    )(parts)
    sums = lax.all_gather(sums, "space")
    features, middle, stem = pl.pallas_call(
        functools.partial(unpack_kernel, middle_cells**-0.5, stem_cells**-0.5),
        out_shape=[
            jax.ShapeDtypeStruct((16, 16, LANES), BF16),
            jax.ShapeDtypeStruct((27, 16, 32), F32),
            jax.ShapeDtypeStruct((27, 4, 32), F32),
        ],
        in_specs=whole(2),
        out_specs=[pl.BlockSpec(memory_space=pl.ANY)] * 3,
        scratch_shapes=[
            pltpu.VMEM((16, 16, LANES), BF16),
            pltpu.VMEM((27, 16, 32), F32),
            pltpu.VMEM((27, 4, 32), F32),
            pltpu.SemaphoreType.DMA((3,)),
        ],
        compiler_params=limit,
        name="unpack",
    )(sums, parts)
    return features.reshape(16, 1, 16, LANES), middle.transpose(0, 2, 1), stem


def solution(mesh):
    in_specs = (
        P(None, "space", "filt", None),
        P(),
        P(None, None, "filt"),
        P("filt", "space", None, None),
    )
    out_specs = (P("filt", "space", None, None), P(None, None, "filt"), P())
    return jax.shard_map(body, mesh=mesh, in_specs=in_specs, out_specs=out_specs, check_vma=False)
```

```python
import functools

import jax
import jax.numpy as jnp
import numpy as np
from jax import lax
from jax.experimental import pallas as pl
from jax.experimental.pallas import tpu as pltpu
from jax.sharding import PartitionSpec as P

F32 = jnp.float32
BF16 = jnp.bfloat16
LANES = 128
STEM_ROWS = 144


def nn(a, b):
    return lax.dot_general(a, b, (((1,), (0,)), ((), ())), preferred_element_type=F32)


def nt(a, b):
    return lax.dot_general(a, b, (((1,), (1,)), ((), ())), preferred_element_type=F32)


def place_table():
    table = np.zeros((3, LANES, STEM_ROWS), np.float32)
    for even_odd in range(2):
        for a in range(3):
            for b in range(3):
                for d in range(3):
                    q = 2 * even_odd + d - 1
                    group, phase = (2, 3) if q < 0 else (even_odd, q)
                    for c in range(4):
                        column = 48 * a + 16 * b + 4 * phase + c
                        table[group, 4 * (9 * a + 3 * b + d) + c, column] = 1.0
    return table


def rows_lanes(shape):
    return lax.broadcasted_iota(jnp.int32, shape, 0), lax.broadcasted_iota(jnp.int32, shape, 1)


def turn_matrix():
    row, column = rows_lanes((256, 256))
    source = lax.shift_left(row & 15, 4) + lax.shift_right_logical(row, 4)
    return (source == column).astype(F32).astype(BF16)


def regroup_kernel(volume_in, weight_in, cotangent_in, own, slab_x, packed, volume, weight, cotangent, sems):
    channels, planes, width, depth = volume.shape
    pairs = [(weight_in, weight), (cotangent_in, cotangent)]
    pairs += [(volume_in.at[c], volume.at[c]) for c in range(channels)]
    copies = [pltpu.make_async_copy(*pair, sems.at[k]) for k, pair in enumerate(pairs)]
    for copy in copies:
        copy.start()
    z, column = rows_lanes((depth, depth))
    source = lax.shift_left(column & (LANES - 1), 2) + lax.shift_right_logical(column, 7)
    select = (z == source).astype(F32).astype(BF16)
    turn = turn_matrix()

    blank = jnp.zeros((16, 32), BF16)
    copies[0].wait()
    taps = [weight[t] if t < 27 else blank for t in range(28)]
    for t in range(7):
        tile = jnp.concatenate(taps[4 * t : 4 * t + 4], axis=1)
        for f in range(packed.shape[0]):
            packed[f, t] = tile
    copies[1].wait()
    turned = nn(turn, cotangent[...].reshape(256, LANES)).astype(BF16)
    for k, f in enumerate(exchange_order(packed.shape[0])):
        for j in range(4):
            row = 16 * (4 * f + j)
            packed[k, 7 + j] = turned[row : row + 16]

    for copy in copies[2:]:
        copy.wait()
    picked = nn(volume[...].reshape(channels * planes * width, depth), select).astype(BF16)
    grouped = []
    for x in range(planes):
        parts = []
        for phase in range(4):
            for c in range(channels):
                start = (c * planes + x) * width
                parts.append(picked[start : start + width, phase * LANES : (phase + 1) * LANES])
        grouped.append(jnp.concatenate(parts, axis=0))
    turned = nn(turn, jnp.concatenate(grouped, axis=1)).astype(BF16)
    for x in range(planes):
        plane = turned[:, x * LANES : (x + 1) * LANES]
        own[x] = plane
        if x > 0:
            slab_x[x - 1] = plane


def border_kernel(slab_x, own, border):
    for x in range(3):
        border[x] = slab_x[x, -48:]
    for x in range(4):
        border[3 + x] = own[x, -48:]


def softplus_sigmoid(values):
    small = jnp.exp(-jnp.abs(values))
    inverse = 1.0 / (1.0 + small)
    soft = jnp.maximum(values, 0.0) + jnp.log(1.0 + small)
    return soft, jnp.where(values >= 0.0, inverse, small * inverse)


def roll_blocks(values, amount):
    blocks = []
    for start in range(0, values.shape[1], LANES):
        block = values[:, start : start + LANES]
        lane = lax.broadcasted_iota(jnp.int32, block.shape, 1)
        edge = 0 if amount == 1 else LANES - 1
        blocks.append(jnp.where(lane == edge, 0.0, pltpu.roll(block, amount % LANES, 1)))
    return jnp.concatenate(blocks, axis=1)


def fill_columns(cols, planes, count):
    for x, plane in enumerate(planes):
        for j in range(count):
            cols[x, :, pl.ds(j * LANES, LANES)] = plane[32 * j : 32 * j + 48]


def stem_forward(weights, cols, i, keep):
    pre = nn(weights, cols[2 * i : 2 * i + 3].reshape(STEM_ROWS, cols.shape[2]))
    pre = jnp.concatenate([pre[0:32] + roll_blocks(pre[64:96], 1), pre[32:64]], axis=0)
    soft, sig = softplus_sigmoid(pre)
    act = (0.3 * pre + 0.7 * soft) * keep
    taps = jnp.concatenate([roll_blocks(act[32:64], 1), act], axis=0).astype(BF16)
    return (0.3 + 0.7 * sig) * keep, taps


def keep_space():
    return jnp.where(lax.axis_index("space") > 0, 1.0, 0.0).astype(F32)


def fill_taps(mid_cols, part, i, j, first, count):
    for b in range(3):
        if (j - b) % 2 == 0 and first <= (j - b) // 2 < first + count:
            row = 96 * (3 * i + b)
            mid_cols[row : row + 96, pl.ds(((j - b) // 2 - first) * LANES, LANES)] = part


def inner_kernel(own, slab_x, stem_w, place, weights, cols, slope, mid_cols, near_taps):
    weights[...] = jnp.concatenate([nn(stem_w[...], place[g]) for g in range(3)], axis=0).astype(BF16)
    planes = [slab_x[x, 16:256] if x < 3 else own[x - 3, 16:256] for x in range(7)]
    fill_columns(cols, planes, 7)
    for i in range(3):
        slope[i], taps = stem_forward(weights[...], cols, i, keep_space() if i == 0 else 1.0)
        for j in range(2, 9):
            fill_taps(mid_cols, taps[:, (j - 2) * LANES : (j - 1) * LANES], i, j, 1, 3)
        near_taps[i] = taps[:, 0:LANES]


def middle_cells_step(mid_w, mid_cols, cotangent):
    pre = nn(mid_w[:, 0:864], mid_cols[...])
    soft, sig = softplus_sigmoid(pre)
    delta = cotangent.astype(F32) * (0.3 + 0.7 * sig)
    delta_low = delta.astype(BF16)
    mid_grad = nt(delta_low, mid_cols[...])
    both = jnp.concatenate([delta_low, roll_blocks(delta, -1).astype(BF16)], axis=0)
    return (0.3 * pre + 0.7 * soft).astype(BF16), mid_grad, both


def put_back(target, i, start, part):
    lanes = pl.ds(start, LANES)
    target[i, 0:64, lanes] = part.astype(BF16)
    target[i, 64:96, lanes] = roll_blocks(part[0:32], -1).astype(BF16)


def upper_kernel(
    gathered, cols, slope, mid_cols, features, mid_grad, stem_grad, mid_w, odd_w, even_w, stem_back,
):
    blocks = gathered.shape[0]
    order = exchange_order(blocks)
    for k, f in enumerate(order):
        for t in range(7):
            mid_w[16 * f : 16 * f + 16, t * LANES : (t + 1) * LANES] = gathered[k, t]
    cotangent = jnp.concatenate(
        [jnp.concatenate([gathered[order.index(f), 7 + j] for j in range(1, 4)], axis=1) for f in range(blocks)],
        axis=0,
    )
    features[...], mid_grad[...], both = middle_cells_step(mid_w, mid_cols, cotangent)

    turned = jnp.concatenate(
        [mid_w[:, t * LANES : (t + 1) * LANES].astype(F32).T for t in range(7)], axis=0
    ).astype(BF16)
    zero = jnp.zeros((32, blocks * 16), BF16)

    def block(a, b, d):
        row = 32 * (9 * a + 3 * b + d)
        return turned[row : row + 32]

    def wide(a, b):
        even = jnp.concatenate([block(a, b, 1), zero], axis=1)
        odd = jnp.concatenate([block(a, b, 2), block(a, b, 0)], axis=1)
        return jnp.concatenate([even, odd], axis=0)

    odd_w[...] = jnp.concatenate([wide(i, 1) for i in range(3)], axis=0)
    even_w[...] = jnp.concatenate(
        [jnp.concatenate([wide(i, 0), wide(i, 2)], axis=1) for i in range(3)], axis=0
    )
    nothing = jnp.zeros((2 * blocks * 16, LANES), BF16)
    pair = jnp.concatenate(
        [jnp.concatenate([both, nothing], axis=1), jnp.concatenate([nothing, both], axis=1)], axis=0
    )
    odd_back = nn(odd_w[...], both)
    even_back = nn(even_w[...], pair)
    total = jnp.zeros((96, STEM_ROWS), F32)
    for i in range(3):
        for j in range(7):
            source = even_back if j % 2 == 0 else odd_back
            part = source[64 * i : 64 * i + 64, (j // 2) * LANES : (j // 2 + 1) * LANES]
            put_back(stem_back, i, j * LANES, part * slope[i, :, pl.ds(j * LANES, LANES)])
        total += nt(stem_back[i], cols[2 * i : 2 * i + 3].reshape(STEM_ROWS, 7 * LANES))
    stem_grad[...] = total


def lower_kernel(
    own, slab_x, border, place, gathered, weights, cols, slope, near_taps, upper_features, upper_mid, upper_stem,
    mid_w, odd_w, even_w, parts, low_cols, mid_cols, low_back,
):
    blocks = gathered.shape[0]
    keep_y = jnp.where(lax.axis_index("filt") > 0, 1.0, 0.0).astype(F32)
    planes = [
        jnp.concatenate([border[x], slab_x[x, 0:32] if x < 3 else own[x - 3, 0:32]], axis=0)
        for x in range(7)
    ]
    fill_columns(low_cols, planes, 2)
    low_slope = []
    for i in range(3):
        keep = jnp.where(lax.broadcasted_iota(jnp.int32, (64, 2 * LANES), 1) < LANES, keep_y, 1.0)
        if i == 0:
            keep = keep * keep_space()
        one_slope, low_taps = stem_forward(weights[...], low_cols, i, keep)
        low_slope.append(one_slope)
        for j in range(2):
            fill_taps(mid_cols, low_taps[:, j * LANES : (j + 1) * LANES], i, j, 0, 1)
        fill_taps(mid_cols, near_taps[i], i, 2, 0, 1)
    order = exchange_order(blocks)
    cotangent = jnp.concatenate([gathered[order.index(f), 7] for f in range(blocks)], axis=0)
    features, mid_grad, both = middle_cells_step(mid_w, mid_cols, cotangent)

    back = [nn(even_w[:, 0:LANES], both), nn(odd_w[...], both), nn(even_w[:, LANES:], both)]
    stem_grad = upper_stem[...]
    for i in range(3):
        for j in range(2):
            part = back[j][64 * i : 64 * i + 64] * low_slope[i][:, j * LANES : (j + 1) * LANES]
            put_back(low_back, i, j * LANES, part)
        put_back(low_back, i, 2 * LANES, back[2][64 * i : 64 * i + 64] * slope[i, :, 0:LANES])
        low = low_cols[2 * i : 2 * i + 3].reshape(STEM_ROWS, 2 * LANES)
        near = cols[2 * i : 2 * i + 3, :, 0:LANES].reshape(STEM_ROWS, LANES)
        stem_grad += nt(low_back[i], jnp.concatenate([low, near], axis=1))
    high = stem_grad.astype(BF16)
    both = jnp.concatenate([high, (stem_grad - high.astype(F32)).astype(BF16)], axis=0)
    stem = 0.0
    for g in range(3):
        rows = jnp.concatenate([both[32 * g : 32 * g + 32], both[96 + 32 * g : 128 + 32 * g]], axis=0)
        taken = nt(rows, place[g])
        stem += taken[0:32] + taken[32:64]
    stem = stem.astype(BF16)

    middle = (mid_grad + upper_mid[...]).astype(BF16)
    middle = jnp.concatenate([middle, jnp.zeros((blocks * 16, 32), BF16)], axis=1)
    for k, f in enumerate(order):
        rows = slice(16 * f, 16 * f + 16)
        for t in range(7):
            parts[k, t] = middle[rows, t * LANES : (t + 1) * LANES]
        for half in range(2):
            parts[k, 7 + half] = stem[16 * half : 16 * half + 16]
        parts[k, 9] = features[rows]
        for j in range(3):
            parts[k, 10 + j] = upper_features[rows, j * LANES : (j + 1) * LANES]


def sum_kernel(parts, sums):
    total = jnp.sum(parts[:, 0:9].astype(F32), axis=0).astype(BF16)
    for s in range(sums.shape[0]):
        sums[s] = total


def unpack_kernel(
    middle_scale, stem_scale, sums, parts, features_out, middle_out, stem_out, features, middle, stem, sems,
):
    copies = [
        pltpu.make_async_copy(source, target, sems.at[k])
        for k, (source, target) in enumerate(
            [(middle, middle_out), (stem, stem_out), (features, features_out)]
        )
    ]
    total = jnp.sum(sums[...].astype(F32), axis=0)
    for t in range(27):
        start = 32 * (t % 4)
        middle[t] = total[t // 4, :, start : start + 32] * middle_scale
    copies[0].start()
    order = exchange_order(parts.shape[0])
    rows = [parts[order.index(f), 9 + j] for f in range(parts.shape[0]) for j in range(4)]
    features[...] = nn(turn_matrix(), jnp.concatenate(rows, axis=0)).astype(BF16).reshape(16, 16, LANES)
    copies[2].start()
    turned = jnp.concatenate([total[7], total[8]], axis=0).T * stem_scale
    for t in range(27):
        stem[t] = turned[4 * t : 4 * t + 4]
    copies[1].start()
    for copy in copies:
        copy.wait()


def exchange_order(filts):
    return sorted(range(filts), key=lambda f: (abs(f - filts // 2), f))


def exchange(chunks):
    groups = [exchange_order(lax.axis_size("filt"))]
    return lax.all_to_all(chunks, "filt", 0, 0, axis_index_groups=groups, tiled=True)


def whole(count):
    return [pl.BlockSpec(memory_space=pltpu.VMEM)] * count


def body(volume, stem_weight, middle_weight, cotangent):
    spaces, filts = lax.axis_size("space"), lax.axis_size("filt")
    channels, planes, width, depth = volume.shape
    stem_cells = (planes // 2) * spaces * (width // 2) * filts * (depth // 2)
    middle_cells = stem_cells // 8
    limit = pltpu.CompilerParams(vmem_limit_bytes=48 * 1024 * 1024)

    raw = (volume, middle_weight.transpose(0, 2, 1), cotangent.reshape(16, 16, LANES))
    own, slab_x, packed = pl.pallas_call(
        regroup_kernel,
        out_shape=[
            jax.ShapeDtypeStruct((planes, 16 * width, LANES), BF16),
            jax.ShapeDtypeStruct((planes - 1, 16 * width, LANES), BF16),
            pltpu.VMEM((filts, 11, 16, LANES), BF16),
        ],
        in_specs=[pl.BlockSpec(memory_space=pltpu.HBM)] * 3,
        out_specs=whole(3),
        scratch_shapes=[
            pltpu.VMEM(volume.shape, BF16),
            pltpu.VMEM((27, 16, 32), BF16),
            pltpu.VMEM((16, 16, LANES), BF16),
            pltpu.SemaphoreType.DMA((2 + channels,)),
        ],
        compiler_params=limit,
        name="regroup",
    )(*[pltpu.with_memory_space_constraint(x, pltpu.HBM) for x in raw])
    slab_x = lax.ppermute(slab_x, "space", [(s - 1, s) for s in range(1, spaces)])
    gathered = exchange(packed)
    border = pl.pallas_call(
        border_kernel,
        out_shape=jax.ShapeDtypeStruct((7, 48, LANES), BF16),
        in_specs=whole(2),
        out_specs=whole(1)[0],
        compiler_params=limit,
        name="border",
    )(slab_x, own)
    border = lax.ppermute(border, "filt", [(f - 1, f) for f in range(1, filts)])

    stem_w = jnp.pad(stem_weight.reshape(108, 32).T, ((0, 0), (0, 20)))
    place = jnp.asarray(place_table(), BF16)
    weights, cols, slope, mid_cols, near_taps = pl.pallas_call(
        inner_kernel,
        out_shape=[
            jax.ShapeDtypeStruct((96, STEM_ROWS), BF16),
            jax.ShapeDtypeStruct((7, 48, 7 * LANES), BF16),
            jax.ShapeDtypeStruct((3, 64, 7 * LANES), F32),
            jax.ShapeDtypeStruct((864, 3 * LANES), BF16),
            jax.ShapeDtypeStruct((3, 96, LANES), BF16),
        ],
        in_specs=whole(4),
        out_specs=whole(5),
        compiler_params=limit,
        cost_estimate=pl.CostEstimate(flops=200_000_000, bytes_accessed=4_000_000, transcendentals=500_000),
        name="stem_inner",
    )(own, slab_x, stem_w, place)
    upper = pl.pallas_call(
        upper_kernel,
        out_shape=[
            jax.ShapeDtypeStruct((64, 3 * LANES), BF16),
            jax.ShapeDtypeStruct((64, 864), F32),
            jax.ShapeDtypeStruct((96, STEM_ROWS), F32),
            jax.ShapeDtypeStruct((64, 896), BF16),
            jax.ShapeDtypeStruct((192, LANES), BF16),
            jax.ShapeDtypeStruct((192, 2 * LANES), BF16),
        ],
        in_specs=whole(4),
        out_specs=whole(6),
        scratch_shapes=[pltpu.VMEM((3, 96, 7 * LANES), BF16)],
        compiler_params=limit,
        name="upper_cells",
    )(gathered, cols, slope, mid_cols)
    parts = pl.pallas_call(
        lower_kernel,
        out_shape=jax.ShapeDtypeStruct((filts, 13, 16, LANES), BF16),
        in_specs=whole(15),
        out_specs=whole(1)[0],
        scratch_shapes=[
            pltpu.VMEM((7, 48, 2 * LANES), BF16),
            pltpu.VMEM((864, LANES), BF16),
            pltpu.VMEM((3, 96, 3 * LANES), BF16),
        ],
        compiler_params=limit,
        cost_estimate=pl.CostEstimate(flops=600_000_000, bytes_accessed=8_000_000, transcendentals=500_000),
        name="lower_cells",
    )(own, slab_x, border, place, gathered, weights, cols, slope, near_taps, *upper)

    parts = exchange(parts)
    sums = pl.pallas_call(
        sum_kernel,
        out_shape=jax.ShapeDtypeStruct((spaces, 9, 16, LANES), BF16),
        in_specs=whole(1),
        out_specs=whole(1)[0],
        compiler_params=limit,
        name="sums",
    )(parts)
    around = [(s + 2) % spaces for s in range(spaces)]
    sums = lax.all_to_all(sums, "space", 0, 0, axis_index_groups=[around], tiled=True)
    features, middle, stem = pl.pallas_call(
        functools.partial(unpack_kernel, middle_cells**-0.5, stem_cells**-0.5),
        out_shape=[
            jax.ShapeDtypeStruct((16, 16, LANES), BF16),
            jax.ShapeDtypeStruct((27, 16, 32), F32),
            jax.ShapeDtypeStruct((27, 4, 32), F32),
        ],
        in_specs=whole(2),
        out_specs=[pl.BlockSpec(memory_space=pl.ANY)] * 3,
        scratch_shapes=[
            pltpu.VMEM((16, 16, LANES), BF16),
            pltpu.VMEM((27, 16, 32), F32),
            pltpu.VMEM((27, 4, 32), F32),
            pltpu.SemaphoreType.DMA((3,)),
        ],
        compiler_params=limit,
        name="unpack",
    )(sums, parts)
    return features.reshape(16, 1, 16, LANES), middle.transpose(0, 2, 1), stem


def solution(mesh):
    in_specs = (
        P(None, "space", "filt", None),
        P(),
        P(None, None, "filt"),
        P("filt", "space", None, None),
    )
    out_specs = (P("filt", "space", None, None), P(None, None, "filt"), P())
    return jax.shard_map(body, mesh=mesh, in_specs=in_specs, out_specs=out_specs, check_vma=False)
```

```python
import functools

import jax
import jax.numpy as jnp
import numpy as np
from jax import lax
from jax.experimental import pallas as pl
from jax.experimental.pallas import tpu as pltpu
from jax.sharding import PartitionSpec as P

F32 = jnp.float32
BF16 = jnp.bfloat16
LANES = 128
STEM_ROWS = 144


def nn(a, b):
    return lax.dot_general(a, b, (((1,), (0,)), ((), ())), preferred_element_type=F32)


def nt(a, b):
    return lax.dot_general(a, b, (((1,), (1,)), ((), ())), preferred_element_type=F32)


def place_table():
    table = np.zeros((3, LANES, STEM_ROWS), np.float32)
    for even_odd in range(2):
        for a in range(3):
            for b in range(3):
                for d in range(3):
                    q = 2 * even_odd + d - 1
                    group, phase = (2, 3) if q < 0 else (even_odd, q)
                    for c in range(4):
                        column = 48 * a + 16 * b + 4 * phase + c
                        table[group, 4 * (9 * a + 3 * b + d) + c, column] = 1.0
    return table


def rows_lanes(shape):
    return lax.broadcasted_iota(jnp.int32, shape, 0), lax.broadcasted_iota(jnp.int32, shape, 1)


def turn_matrix():
    row, column = rows_lanes((256, 256))
    source = lax.shift_left(row & 15, 4) + lax.shift_right_logical(row, 4)
    return (source == column).astype(F32).astype(BF16)


def regroup_kernel(volume_in, weight_in, cotangent_in, own, slab_x, packed, volume, weight, cotangent, sems):
    channels, planes, width, depth = volume.shape
    pairs = [(weight_in, weight), (cotangent_in, cotangent)]
    pairs += [(volume_in.at[c], volume.at[c]) for c in range(channels)]
    copies = [pltpu.make_async_copy(*pair, sems.at[k]) for k, pair in enumerate(pairs)]
    for copy in copies:
        copy.start()
    z, column = rows_lanes((depth, depth))
    source = lax.shift_left(column & (LANES - 1), 2) + lax.shift_right_logical(column, 7)
    select = (z == source).astype(F32).astype(BF16)
    turn = turn_matrix()

    blank = jnp.zeros((16, 32), BF16)
    copies[0].wait()
    taps = [weight[t] if t < 27 else blank for t in range(28)]
    for t in range(7):
        tile = jnp.concatenate(taps[4 * t : 4 * t + 4], axis=1)
        for f in range(packed.shape[0]):
            packed[f, t] = tile
    copies[1].wait()
    turned = nn(turn, cotangent[...].reshape(256, LANES)).astype(BF16)
    for k, f in enumerate(exchange_order(packed.shape[0])):
        for j in range(4):
            row = 16 * (4 * f + j)
            packed[k, 7 + j] = turned[row : row + 16]

    for copy in copies[2:]:
        copy.wait()
    picked = nn(volume[...].reshape(channels * planes * width, depth), select).astype(BF16)
    grouped = []
    for x in range(planes):
        parts = []
        for phase in range(4):
            for c in range(channels):
                start = (c * planes + x) * width
                parts.append(picked[start : start + width, phase * LANES : (phase + 1) * LANES])
        grouped.append(jnp.concatenate(parts, axis=0))
    turned = nn(turn, jnp.concatenate(grouped, axis=1)).astype(BF16)
    for x in range(planes):
        plane = turned[:, x * LANES : (x + 1) * LANES]
        own[x] = plane
        if x > 0:
            slab_x[x - 1] = plane


def border_kernel(slab_x, own, border):
    for x in range(3):
        border[x] = slab_x[x, -48:]
    for x in range(4):
        border[3 + x] = own[x, -48:]


def softplus_sigmoid(values):
    small = jnp.exp(-jnp.abs(values))
    inverse = 1.0 / (1.0 + small)
    soft = jnp.maximum(values, 0.0) + jnp.log(1.0 + small)
    return soft, jnp.where(values >= 0.0, inverse, small * inverse)


def roll_blocks(values, amount):
    blocks = []
    for start in range(0, values.shape[1], LANES):
        block = values[:, start : start + LANES]
        lane = lax.broadcasted_iota(jnp.int32, block.shape, 1)
        edge = 0 if amount == 1 else LANES - 1
        blocks.append(jnp.where(lane == edge, 0.0, pltpu.roll(block, amount % LANES, 1)))
    return jnp.concatenate(blocks, axis=1)


def fill_columns(cols, planes, count):
    for x, plane in enumerate(planes):
        for j in range(count):
            cols[x, :, pl.ds(j * LANES, LANES)] = plane[32 * j : 32 * j + 48]


def stem_forward(weights, cols, i, keep):
    pre = nn(weights, cols[2 * i : 2 * i + 3].reshape(STEM_ROWS, cols.shape[2]))
    pre = jnp.concatenate([pre[0:32] + roll_blocks(pre[64:96], 1), pre[32:64]], axis=0)
    soft, sig = softplus_sigmoid(pre)
    act = (0.3 * pre + 0.7 * soft) * keep
    taps = jnp.concatenate([roll_blocks(act[32:64], 1), act], axis=0).astype(BF16)
    return (0.3 + 0.7 * sig) * keep, taps


def keep_space():
    return jnp.where(lax.axis_index("space") > 0, 1.0, 0.0).astype(F32)


def fill_taps(mid_cols, part, i, j, first, count):
    for b in range(3):
        if (j - b) % 2 == 0 and first <= (j - b) // 2 < first + count:
            row = 96 * (3 * i + b)
            mid_cols[row : row + 96, pl.ds(((j - b) // 2 - first) * LANES, LANES)] = part


def inner_kernel(own, slab_x, stem_w, place, weights, cols, slope, mid_cols, near_taps):
    weights[...] = jnp.concatenate([nn(stem_w[...], place[g]) for g in range(3)], axis=0).astype(BF16)
    planes = [slab_x[x, 16:256] if x < 3 else own[x - 3, 16:256] for x in range(7)]
    fill_columns(cols, planes, 7)
    for i in range(3):
        slope[i], taps = stem_forward(weights[...], cols, i, keep_space() if i == 0 else 1.0)
        for j in range(2, 9):
            fill_taps(mid_cols, taps[:, (j - 2) * LANES : (j - 1) * LANES], i, j, 1, 3)
        near_taps[i] = taps[:, 0:LANES]


def middle_cells_step(mid_w, mid_cols, cotangent):
    pre = nn(mid_w[:, 0:864], mid_cols[...])
    soft, sig = softplus_sigmoid(pre)
    delta = cotangent.astype(F32) * (0.3 + 0.7 * sig)
    delta_low = delta.astype(BF16)
    mid_grad = nt(delta_low, mid_cols[...])
    both = jnp.concatenate([delta_low, roll_blocks(delta, -1).astype(BF16)], axis=0)
    return (0.3 * pre + 0.7 * soft).astype(BF16), mid_grad, both


def put_back(target, i, start, part):
    lanes = pl.ds(start, LANES)
    target[i, 0:64, lanes] = part.astype(BF16)
    target[i, 64:96, lanes] = roll_blocks(part[0:32], -1).astype(BF16)


def upper_kernel(
    gathered, cols, slope, mid_cols, features, mid_grad, stem_grad, mid_w, odd_w, even_w, stem_back,
):
    blocks = gathered.shape[0]
    order = exchange_order(blocks)
    for k, f in enumerate(order):
        for t in range(7):
            mid_w[16 * f : 16 * f + 16, t * LANES : (t + 1) * LANES] = gathered[k, t]
    cotangent = jnp.concatenate(
        [jnp.concatenate([gathered[order.index(f), 7 + j] for j in range(1, 4)], axis=1) for f in range(blocks)],
        axis=0,
    )
    features[...], mid_grad[...], both = middle_cells_step(mid_w, mid_cols, cotangent)

    turned = jnp.concatenate(
        [mid_w[:, t * LANES : (t + 1) * LANES].astype(F32).T for t in range(7)], axis=0
    ).astype(BF16)
    zero = jnp.zeros((32, blocks * 16), BF16)

    def block(a, b, d):
        row = 32 * (9 * a + 3 * b + d)
        return turned[row : row + 32]

    def wide(a, b):
        even = jnp.concatenate([block(a, b, 1), zero], axis=1)
        odd = jnp.concatenate([block(a, b, 2), block(a, b, 0)], axis=1)
        return jnp.concatenate([even, odd], axis=0)

    odd_w[...] = jnp.concatenate([wide(i, 1) for i in range(3)], axis=0)
    even_w[...] = jnp.concatenate(
        [jnp.concatenate([wide(i, 0), wide(i, 2)], axis=1) for i in range(3)], axis=0
    )
    nothing = jnp.zeros((2 * blocks * 16, LANES), BF16)
    pair = jnp.concatenate(
        [jnp.concatenate([both, nothing], axis=1), jnp.concatenate([nothing, both], axis=1)], axis=0
    )
    odd_back = nn(odd_w[...], both)
    even_back = nn(even_w[...], pair)
    total = jnp.zeros((96, STEM_ROWS), F32)
    for i in range(3):
        for j in range(7):
            source = even_back if j % 2 == 0 else odd_back
            part = source[64 * i : 64 * i + 64, (j // 2) * LANES : (j // 2 + 1) * LANES]
            put_back(stem_back, i, j * LANES, part * slope[i, :, pl.ds(j * LANES, LANES)])
        total += nt(stem_back[i], cols[2 * i : 2 * i + 3].reshape(STEM_ROWS, 7 * LANES))
    stem_grad[...] = total


def lower_kernel(
    own, slab_x, border, place, gathered, weights, cols, slope, near_taps, upper_features, upper_mid, upper_stem,
    mid_w, odd_w, even_w, parts, low_cols, mid_cols, low_back,
):
    blocks = gathered.shape[0]
    keep_y = jnp.where(lax.axis_index("filt") > 0, 1.0, 0.0).astype(F32)
    planes = [
        jnp.concatenate([border[x], slab_x[x, 0:32] if x < 3 else own[x - 3, 0:32]], axis=0)
        for x in range(7)
    ]
    fill_columns(low_cols, planes, 2)
    low_slope = []
    for i in range(3):
        keep = jnp.where(lax.broadcasted_iota(jnp.int32, (64, 2 * LANES), 1) < LANES, keep_y, 1.0)
        if i == 0:
            keep = keep * keep_space()
        one_slope, low_taps = stem_forward(weights[...], low_cols, i, keep)
        low_slope.append(one_slope)
        for j in range(2):
            fill_taps(mid_cols, low_taps[:, j * LANES : (j + 1) * LANES], i, j, 0, 1)
        fill_taps(mid_cols, near_taps[i], i, 2, 0, 1)
    order = exchange_order(blocks)
    cotangent = jnp.concatenate([gathered[order.index(f), 7] for f in range(blocks)], axis=0)
    features, mid_grad, both = middle_cells_step(mid_w, mid_cols, cotangent)

    back = [nn(even_w[:, 0:LANES], both), nn(odd_w[...], both), nn(even_w[:, LANES:], both)]
    stem_grad = upper_stem[...]
    for i in range(3):
        for j in range(2):
            part = back[j][64 * i : 64 * i + 64] * low_slope[i][:, j * LANES : (j + 1) * LANES]
            put_back(low_back, i, j * LANES, part)
        put_back(low_back, i, 2 * LANES, back[2][64 * i : 64 * i + 64] * slope[i, :, 0:LANES])
        low = low_cols[2 * i : 2 * i + 3].reshape(STEM_ROWS, 2 * LANES)
        near = cols[2 * i : 2 * i + 3, :, 0:LANES].reshape(STEM_ROWS, LANES)
        stem_grad += nt(low_back[i], jnp.concatenate([low, near], axis=1))
    high = stem_grad.astype(BF16)
    both = jnp.concatenate([high, (stem_grad - high.astype(F32)).astype(BF16)], axis=0)
    stem = 0.0
    for g in range(3):
        rows = jnp.concatenate([both[32 * g : 32 * g + 32], both[96 + 32 * g : 128 + 32 * g]], axis=0)
        taken = nt(rows, place[g])
        stem += taken[0:32] + taken[32:64]
    stem = stem.astype(BF16)

    middle = (mid_grad + upper_mid[...]).astype(BF16)
    middle = jnp.concatenate([middle, jnp.zeros((blocks * 16, 32), BF16)], axis=1)
    for k, f in enumerate(return_order(blocks)):
        rows = slice(16 * f, 16 * f + 16)
        for t in range(7):
            parts[k, t] = middle[rows, t * LANES : (t + 1) * LANES]
        for half in range(2):
            parts[k, 7 + half] = stem[16 * half : 16 * half + 16]
        parts[k, 9] = features[rows]
        for j in range(3):
            parts[k, 10 + j] = upper_features[rows, j * LANES : (j + 1) * LANES]


def sum_kernel(parts, sums):
    sums[...] = jnp.sum(parts[:, 0:9].astype(F32), axis=0).astype(BF16)


def unpack_kernel(
    middle_scale, stem_scale, sums, parts, features_out, middle_out, stem_out, features, middle, stem, sems,
):
    copies = [
        pltpu.make_async_copy(source, target, sems.at[k])
        for k, (source, target) in enumerate(
            [(middle, middle_out), (stem, stem_out), (features, features_out)]
        )
    ]
    total = jnp.sum(sums[...].astype(F32), axis=0)
    for t in range(27):
        start = 32 * (t % 4)
        middle[t] = total[t // 4, :, start : start + 32] * middle_scale
    copies[0].start()
    order = return_order(parts.shape[0])
    rows = [parts[order.index(f), 9 + j] for f in range(parts.shape[0]) for j in range(4)]
    features[...] = nn(turn_matrix(), jnp.concatenate(rows, axis=0)).astype(BF16).reshape(16, 16, LANES)
    copies[2].start()
    turned = jnp.concatenate([total[7], total[8]], axis=0).T * stem_scale
    for t in range(27):
        stem[t] = turned[4 * t : 4 * t + 4]
    copies[1].start()
    for copy in copies:
        copy.wait()


def exchange_order(filts):
    return sorted(range(filts), key=lambda f: (abs(f - filts // 2), f))


def return_order(filts):
    middle = filts // 2
    return [middle] + [f for f in range(filts) if f != middle]


def exchange(chunks, order):
    return lax.all_to_all(chunks, "filt", 0, 0, axis_index_groups=[order], tiled=True)


def whole(count):
    return [pl.BlockSpec(memory_space=pltpu.VMEM)] * count


def body(volume, stem_weight, middle_weight, cotangent):
    spaces, filts = lax.axis_size("space"), lax.axis_size("filt")
    channels, planes, width, depth = volume.shape
    stem_cells = (planes // 2) * spaces * (width // 2) * filts * (depth // 2)
    middle_cells = stem_cells // 8
    limit = pltpu.CompilerParams(vmem_limit_bytes=48 * 1024 * 1024)

    raw = (volume, middle_weight.transpose(0, 2, 1), cotangent.reshape(16, 16, LANES))
    own, slab_x, packed = pl.pallas_call(
        regroup_kernel,
        out_shape=[
            jax.ShapeDtypeStruct((planes, 16 * width, LANES), BF16),
            jax.ShapeDtypeStruct((planes - 1, 16 * width, LANES), BF16),
            pltpu.VMEM((filts, 11, 16, LANES), BF16),
        ],
        in_specs=[pl.BlockSpec(memory_space=pltpu.HBM)] * 3,
        out_specs=whole(3),
        scratch_shapes=[
            pltpu.VMEM(volume.shape, BF16),
            pltpu.VMEM((27, 16, 32), BF16),
            pltpu.VMEM((16, 16, LANES), BF16),
            pltpu.SemaphoreType.DMA((2 + channels,)),
        ],
        compiler_params=limit,
        name="regroup",
    )(*[pltpu.with_memory_space_constraint(x, pltpu.HBM) for x in raw])
    slab_x = lax.ppermute(slab_x, "space", [(s - 1, s) for s in range(1, spaces)])
    gathered = exchange(packed, exchange_order(filts))
    border = pl.pallas_call(
        border_kernel,
        out_shape=jax.ShapeDtypeStruct((7, 48, LANES), BF16),
        in_specs=whole(2),
        out_specs=whole(1)[0],
        compiler_params=limit,
        name="border",
    )(slab_x, own)
    border = lax.ppermute(border, "filt", [(f - 1, f) for f in range(1, filts)])

    stem_w = jnp.pad(stem_weight.reshape(108, 32).T, ((0, 0), (0, 20)))
    place = jnp.asarray(place_table(), BF16)
    weights, cols, slope, mid_cols, near_taps = pl.pallas_call(
        inner_kernel,
        out_shape=[
            jax.ShapeDtypeStruct((96, STEM_ROWS), BF16),
            jax.ShapeDtypeStruct((7, 48, 7 * LANES), BF16),
            jax.ShapeDtypeStruct((3, 64, 7 * LANES), F32),
            jax.ShapeDtypeStruct((864, 3 * LANES), BF16),
            jax.ShapeDtypeStruct((3, 96, LANES), BF16),
        ],
        in_specs=whole(4),
        out_specs=whole(5),
        compiler_params=limit,
        cost_estimate=pl.CostEstimate(flops=200_000_000, bytes_accessed=4_000_000, transcendentals=500_000),
        name="stem_inner",
    )(own, slab_x, stem_w, place)
    upper = pl.pallas_call(
        upper_kernel,
        out_shape=[
            jax.ShapeDtypeStruct((64, 3 * LANES), BF16),
            jax.ShapeDtypeStruct((64, 864), F32),
            jax.ShapeDtypeStruct((96, STEM_ROWS), F32),
            jax.ShapeDtypeStruct((64, 896), BF16),
            jax.ShapeDtypeStruct((192, LANES), BF16),
            jax.ShapeDtypeStruct((192, 2 * LANES), BF16),
        ],
        in_specs=whole(4),
        out_specs=whole(6),
        scratch_shapes=[pltpu.VMEM((3, 96, 7 * LANES), BF16)],
        compiler_params=limit,
        name="upper_cells",
    )(gathered, cols, slope, mid_cols)
    parts = pl.pallas_call(
        lower_kernel,
        out_shape=jax.ShapeDtypeStruct((filts, 13, 16, LANES), BF16),
        in_specs=whole(15),
        out_specs=whole(1)[0],
        scratch_shapes=[
            pltpu.VMEM((7, 48, 2 * LANES), BF16),
            pltpu.VMEM((864, LANES), BF16),
            pltpu.VMEM((3, 96, 3 * LANES), BF16),
        ],
        compiler_params=limit,
        cost_estimate=pl.CostEstimate(flops=600_000_000, bytes_accessed=8_000_000, transcendentals=500_000),
        name="lower_cells",
    )(own, slab_x, border, place, gathered, weights, cols, slope, near_taps, *upper)

    parts = exchange(parts, return_order(filts))
    sums = pl.pallas_call(
        sum_kernel,
        out_shape=jax.ShapeDtypeStruct((9, 16, LANES), BF16),
        in_specs=whole(1),
        out_specs=whole(1)[0],
        compiler_params=limit,
        name="sums",
    )(parts)
    sums = lax.all_gather(sums, "space")
    features, middle, stem = pl.pallas_call(
        functools.partial(unpack_kernel, middle_cells**-0.5, stem_cells**-0.5),
        out_shape=[
            jax.ShapeDtypeStruct((16, 16, LANES), BF16),
            jax.ShapeDtypeStruct((27, 16, 32), F32),
            jax.ShapeDtypeStruct((27, 4, 32), F32),
        ],
        in_specs=whole(2),
        out_specs=[pl.BlockSpec(memory_space=pl.ANY)] * 3,
        scratch_shapes=[
            pltpu.VMEM((16, 16, LANES), BF16),
            pltpu.VMEM((27, 16, 32), F32),
            pltpu.VMEM((27, 4, 32), F32),
            pltpu.SemaphoreType.DMA((3,)),
        ],
        compiler_params=limit,
        name="unpack",
    )(sums, parts)
    return features.reshape(16, 1, 16, LANES), middle.transpose(0, 2, 1), stem


def solution(mesh):
    in_specs = (
        P(None, "space", "filt", None),
        P(),
        P(None, None, "filt"),
        P("filt", "space", None, None),
    )
    out_specs = (P("filt", "space", None, None), P(None, None, "filt"), P())
    return jax.shard_map(body, mesh=mesh, in_specs=in_specs, out_specs=out_specs, check_vma=False)
```

```python
import functools

import jax
import jax.numpy as jnp
import numpy as np
from jax import lax
from jax.experimental import pallas as pl
from jax.experimental.pallas import tpu as pltpu
from jax.sharding import PartitionSpec as P

F32 = jnp.float32
BF16 = jnp.bfloat16
LANES = 128
STEM_ROWS = 144


def nn(a, b):
    return lax.dot_general(a, b, (((1,), (0,)), ((), ())), preferred_element_type=F32)


def nt(a, b):
    return lax.dot_general(a, b, (((1,), (1,)), ((), ())), preferred_element_type=F32)


def place_table():
    table = np.zeros((3, LANES, STEM_ROWS), np.float32)
    for even_odd in range(2):
        for a in range(3):
            for b in range(3):
                for d in range(3):
                    q = 2 * even_odd + d - 1
                    group, phase = (2, 3) if q < 0 else (even_odd, q)
                    for c in range(4):
                        column = 48 * a + 16 * b + 4 * phase + c
                        table[group, 4 * (9 * a + 3 * b + d) + c, column] = 1.0
    return table


def rows_lanes(shape):
    return lax.broadcasted_iota(jnp.int32, shape, 0), lax.broadcasted_iota(jnp.int32, shape, 1)


def turn_matrix():
    row, column = rows_lanes((256, 256))
    source = lax.shift_left(row & 15, 4) + lax.shift_right_logical(row, 4)
    return (source == column).astype(F32).astype(BF16)


def regroup_kernel(volume_in, weight_in, cotangent_in, own, slab_x, packed, volume, weight, cotangent, sems):
    channels, planes, width, depth = volume.shape
    pairs = [(weight_in, weight), (cotangent_in, cotangent)]
    pairs += [(volume_in.at[c], volume.at[c]) for c in range(channels)]
    copies = [pltpu.make_async_copy(*pair, sems.at[k]) for k, pair in enumerate(pairs)]
    for copy in copies:
        copy.start()
    z, column = rows_lanes((depth, depth))
    source = lax.shift_left(column & (LANES - 1), 2) + lax.shift_right_logical(column, 7)
    select = (z == source).astype(F32).astype(BF16)
    turn = turn_matrix()

    for copy in copies:
        copy.wait()

    picked = nn(volume[...].reshape(channels * planes * width, depth), select).astype(BF16)
    grouped = []
    for x in range(planes):
        parts = []
        for phase in range(4):
            for c in range(channels):
                start = (c * planes + x) * width
                parts.append(picked[start : start + width, phase * LANES : (phase + 1) * LANES])
        grouped.append(jnp.concatenate(parts, axis=0))
    grouped.append(cotangent[...].reshape(256, LANES))
    turned = nn(turn, jnp.concatenate(grouped, axis=1)).astype(BF16)
    for x in range(planes):
        plane = turned[:, x * LANES : (x + 1) * LANES]
        own[x] = plane
        if x > 0:
            slab_x[x - 1] = plane
    blank = jnp.zeros((16, 32), BF16)
    taps = [weight[t] if t < 27 else blank for t in range(28)]
    for t in range(7):
        tile = jnp.concatenate(taps[4 * t : 4 * t + 4], axis=1)
        for f in range(packed.shape[0]):
            packed[f, t] = tile
    for k, f in enumerate(exchange_order(packed.shape[0])):
        for j in range(4):
            row = 16 * (4 * f + j)
            packed[k, 7 + j] = turned[row : row + 16, planes * LANES :]


def border_kernel(slab_x, own, border):
    for x in range(3):
        border[x] = slab_x[x, -48:]
    for x in range(4):
        border[3 + x] = own[x, -48:]


def softplus_sigmoid(values):
    small = jnp.exp(-jnp.abs(values))
    inverse = 1.0 / (1.0 + small)
    soft = jnp.maximum(values, 0.0) + jnp.log(1.0 + small)
    return soft, jnp.where(values >= 0.0, inverse, small * inverse)


def roll_blocks(values, amount):
    blocks = []
    for start in range(0, values.shape[1], LANES):
        block = values[:, start : start + LANES]
        lane = lax.broadcasted_iota(jnp.int32, block.shape, 1)
        edge = 0 if amount == 1 else LANES - 1
        blocks.append(jnp.where(lane == edge, 0.0, pltpu.roll(block, amount % LANES, 1)))
    return jnp.concatenate(blocks, axis=1)


def fill_columns(cols, planes, count):
    for x, plane in enumerate(planes):
        for j in range(count):
            cols[x, :, pl.ds(j * LANES, LANES)] = plane[32 * j : 32 * j + 48]


def stem_forward(weights, cols, i, keep):
    pre = nn(weights, cols[2 * i : 2 * i + 3].reshape(STEM_ROWS, cols.shape[2]))
    pre = jnp.concatenate([pre[0:32] + roll_blocks(pre[64:96], 1), pre[32:64]], axis=0)
    soft, sig = softplus_sigmoid(pre)
    act = (0.3 * pre + 0.7 * soft) * keep
    taps = jnp.concatenate([roll_blocks(act[32:64], 1), act], axis=0).astype(BF16)
    return (0.3 + 0.7 * sig) * keep, taps


def keep_space():
    return jnp.where(lax.axis_index("space") > 0, 1.0, 0.0).astype(F32)


def fill_taps(mid_cols, part, i, j, first, count):
    for b in range(3):
        if (j - b) % 2 == 0 and first <= (j - b) // 2 < first + count:
            row = 96 * (3 * i + b)
            mid_cols[row : row + 96, pl.ds(((j - b) // 2 - first) * LANES, LANES)] = part


def inner_kernel(own, slab_x, stem_w, place, weights, cols, slope, mid_cols, near_taps):
    weights[...] = jnp.concatenate([nn(stem_w[...], place[g]) for g in range(3)], axis=0).astype(BF16)
    planes = [slab_x[x, 16:256] if x < 3 else own[x - 3, 16:256] for x in range(7)]
    fill_columns(cols, planes, 7)
    for i in range(3):
        slope[i], taps = stem_forward(weights[...], cols, i, keep_space() if i == 0 else 1.0)
        for j in range(2, 9):
            fill_taps(mid_cols, taps[:, (j - 2) * LANES : (j - 1) * LANES], i, j, 1, 3)
        near_taps[i] = taps[:, 0:LANES]


def middle_cells_step(mid_w, mid_cols, cotangent):
    pre = nn(mid_w[:, 0:864], mid_cols[...])
    soft, sig = softplus_sigmoid(pre)
    delta = cotangent.astype(F32) * (0.3 + 0.7 * sig)
    delta_low = delta.astype(BF16)
    mid_grad = nt(delta_low, mid_cols[...])
    both = jnp.concatenate([delta_low, roll_blocks(delta, -1).astype(BF16)], axis=0)
    return (0.3 * pre + 0.7 * soft).astype(BF16), mid_grad, both


def put_back(target, i, start, part):
    lanes = pl.ds(start, LANES)
    target[i, 0:64, lanes] = part.astype(BF16)
    target[i, 64:96, lanes] = roll_blocks(part[0:32], -1).astype(BF16)


def upper_kernel(
    gathered, cols, slope, mid_cols, features, mid_grad, stem_grad, mid_w, odd_w, even_w, stem_back,
):
    blocks = gathered.shape[0]
    order = exchange_order(blocks)
    for k, f in enumerate(order):
        for t in range(7):
            mid_w[16 * f : 16 * f + 16, t * LANES : (t + 1) * LANES] = gathered[k, t]
    cotangent = jnp.concatenate(
        [jnp.concatenate([gathered[order.index(f), 7 + j] for j in range(1, 4)], axis=1) for f in range(blocks)],
        axis=0,
    )
    features[...], mid_grad[...], both = middle_cells_step(mid_w, mid_cols, cotangent)

    turned = jnp.concatenate(
        [mid_w[:, t * LANES : (t + 1) * LANES].astype(F32).T for t in range(7)], axis=0
    ).astype(BF16)
    zero = jnp.zeros((32, blocks * 16), BF16)

    def block(a, b, d):
        row = 32 * (9 * a + 3 * b + d)
        return turned[row : row + 32]

    def wide(a, b):
        even = jnp.concatenate([block(a, b, 1), zero], axis=1)
        odd = jnp.concatenate([block(a, b, 2), block(a, b, 0)], axis=1)
        return jnp.concatenate([even, odd], axis=0)

    odd_w[...] = jnp.concatenate([wide(i, 1) for i in range(3)], axis=0)
    even_w[...] = jnp.concatenate(
        [jnp.concatenate([wide(i, 0), wide(i, 2)], axis=1) for i in range(3)], axis=0
    )
    nothing = jnp.zeros((2 * blocks * 16, LANES), BF16)
    pair = jnp.concatenate(
        [jnp.concatenate([both, nothing], axis=1), jnp.concatenate([nothing, both], axis=1)], axis=0
    )
    odd_back = nn(odd_w[...], both)
    even_back = nn(even_w[...], pair)
    total = jnp.zeros((96, STEM_ROWS), F32)
    for i in range(3):
        for j in range(7):
            source = even_back if j % 2 == 0 else odd_back
            part = source[64 * i : 64 * i + 64, (j // 2) * LANES : (j // 2 + 1) * LANES]
            put_back(stem_back, i, j * LANES, part * slope[i, :, pl.ds(j * LANES, LANES)])
        total += nt(stem_back[i], cols[2 * i : 2 * i + 3].reshape(STEM_ROWS, 7 * LANES))
    stem_grad[...] = total


def lower_kernel(
    own, slab_x, border, place, gathered, weights, cols, slope, near_taps, upper_features, upper_mid, upper_stem,
    mid_w, odd_w, even_w, parts, low_cols, mid_cols, low_back,
):
    blocks = gathered.shape[0]
    keep_y = jnp.where(lax.axis_index("filt") > 0, 1.0, 0.0).astype(F32)
    planes = [
        jnp.concatenate([border[x], slab_x[x, 0:32] if x < 3 else own[x - 3, 0:32]], axis=0)
        for x in range(7)
    ]
    fill_columns(low_cols, planes, 2)
    low_slope = []
    for i in range(3):
        keep = jnp.where(lax.broadcasted_iota(jnp.int32, (64, 2 * LANES), 1) < LANES, keep_y, 1.0)
        if i == 0:
            keep = keep * keep_space()
        one_slope, low_taps = stem_forward(weights[...], low_cols, i, keep)
        low_slope.append(one_slope)
        for j in range(2):
            fill_taps(mid_cols, low_taps[:, j * LANES : (j + 1) * LANES], i, j, 0, 1)
        fill_taps(mid_cols, near_taps[i], i, 2, 0, 1)
    order = exchange_order(blocks)
    cotangent = jnp.concatenate([gathered[order.index(f), 7] for f in range(blocks)], axis=0)
    features, mid_grad, both = middle_cells_step(mid_w, mid_cols, cotangent)

    back = [nn(even_w[:, 0:LANES], both), nn(odd_w[...], both), nn(even_w[:, LANES:], both)]
    stem_grad = upper_stem[...]
    for i in range(3):
        for j in range(2):
            part = back[j][64 * i : 64 * i + 64] * low_slope[i][:, j * LANES : (j + 1) * LANES]
            put_back(low_back, i, j * LANES, part)
        put_back(low_back, i, 2 * LANES, back[2][64 * i : 64 * i + 64] * slope[i, :, 0:LANES])
        low = low_cols[2 * i : 2 * i + 3].reshape(STEM_ROWS, 2 * LANES)
        near = cols[2 * i : 2 * i + 3, :, 0:LANES].reshape(STEM_ROWS, LANES)
        stem_grad += nt(low_back[i], jnp.concatenate([low, near], axis=1))
    high = stem_grad.astype(BF16)
    both = jnp.concatenate([high, (stem_grad - high.astype(F32)).astype(BF16)], axis=0)
    stem = 0.0
    for g in range(3):
        rows = jnp.concatenate([both[32 * g : 32 * g + 32], both[96 + 32 * g : 128 + 32 * g]], axis=0)
        taken = nt(rows, place[g])
        stem += taken[0:32] + taken[32:64]
    stem = stem.astype(BF16)

    middle = (mid_grad + upper_mid[...]).astype(BF16)
    middle = jnp.concatenate([middle, jnp.zeros((blocks * 16, 32), BF16)], axis=1)
    for k, f in enumerate(order):
        rows = slice(16 * f, 16 * f + 16)
        for t in range(7):
            parts[k, t] = middle[rows, t * LANES : (t + 1) * LANES]
        for half in range(2):
            parts[k, 7 + half] = stem[16 * half : 16 * half + 16]
        parts[k, 9] = features[rows]
        for j in range(3):
            parts[k, 10 + j] = upper_features[rows, j * LANES : (j + 1) * LANES]


def sum_kernel(parts, sums):
    sums[...] = jnp.sum(parts[:, 0:9].astype(F32), axis=0).astype(BF16)


def unpack_kernel(
    middle_scale, stem_scale, sums, parts, features_out, middle_out, stem_out, features, middle, stem, sems,
):
    copies = [
        pltpu.make_async_copy(source, target, sems.at[k])
        for k, (source, target) in enumerate(
            [(middle, middle_out), (stem, stem_out), (features, features_out)]
        )
    ]
    total = jnp.sum(sums[...].astype(F32), axis=0)
    for t in range(27):
        start = 32 * (t % 4)
        middle[t] = total[t // 4, :, start : start + 32] * middle_scale
    copies[0].start()
    order = exchange_order(parts.shape[0])
    rows = [parts[order.index(f), 9 + j] for f in range(parts.shape[0]) for j in range(4)]
    features[...] = nn(turn_matrix(), jnp.concatenate(rows, axis=0)).astype(BF16).reshape(16, 16, LANES)
    copies[2].start()
    turned = jnp.concatenate([total[7], total[8]], axis=0).T * stem_scale
    for t in range(27):
        stem[t] = turned[4 * t : 4 * t + 4]
    copies[1].start()
    for copy in copies:
        copy.wait()


def exchange_order(filts):
    return sorted(range(filts), key=lambda f: (abs(f - filts // 2), f))


def exchange(chunks):
    groups = [exchange_order(lax.axis_size("filt"))]
    return lax.all_to_all(chunks, "filt", 0, 0, axis_index_groups=groups, tiled=True)


def whole(count):
    return [pl.BlockSpec(memory_space=pltpu.VMEM)] * count


def body(volume, stem_weight, middle_weight, cotangent):
    spaces, filts = lax.axis_size("space"), lax.axis_size("filt")
    channels, planes, width, depth = volume.shape
    stem_cells = (planes // 2) * spaces * (width // 2) * filts * (depth // 2)
    middle_cells = stem_cells // 8
    limit = pltpu.CompilerParams(vmem_limit_bytes=48 * 1024 * 1024)

    raw = (volume, middle_weight.transpose(0, 2, 1), cotangent.reshape(16, 16, LANES))
    own, slab_x, packed = pl.pallas_call(
        regroup_kernel,
        out_shape=[
            jax.ShapeDtypeStruct((planes, 16 * width, LANES), BF16),
            jax.ShapeDtypeStruct((planes - 1, 16 * width, LANES), BF16),
            pltpu.VMEM((filts, 11, 16, LANES), BF16),
        ],
        in_specs=[pl.BlockSpec(memory_space=pltpu.HBM)] * 3,
        out_specs=whole(3),
        scratch_shapes=[
            pltpu.VMEM(volume.shape, BF16),
            pltpu.VMEM((27, 16, 32), BF16),
            pltpu.VMEM((16, 16, LANES), BF16),
            pltpu.SemaphoreType.DMA((2 + channels,)),
        ],
        compiler_params=limit,
        name="regroup",
    )(*[pltpu.with_memory_space_constraint(x, pltpu.HBM) for x in raw])
    slab_x = lax.ppermute(slab_x, "space", [(s - 1, s) for s in range(1, spaces)])
    gathered = exchange(packed)
    border = pl.pallas_call(
        border_kernel,
        out_shape=jax.ShapeDtypeStruct((7, 48, LANES), BF16),
        in_specs=whole(2),
        out_specs=whole(1)[0],
        compiler_params=limit,
        name="border",
    )(slab_x, own)
    border = lax.ppermute(border, "filt", [(f - 1, f) for f in range(1, filts)])

    stem_w = jnp.pad(stem_weight.reshape(108, 32).T, ((0, 0), (0, 20)))
    place = jnp.asarray(place_table(), BF16)
    weights, cols, slope, mid_cols, near_taps = pl.pallas_call(
        inner_kernel,
        out_shape=[
            jax.ShapeDtypeStruct((96, STEM_ROWS), BF16),
            jax.ShapeDtypeStruct((7, 48, 7 * LANES), BF16),
            jax.ShapeDtypeStruct((3, 64, 7 * LANES), F32),
            jax.ShapeDtypeStruct((864, 3 * LANES), BF16),
            jax.ShapeDtypeStruct((3, 96, LANES), BF16),
        ],
        in_specs=whole(4),
        out_specs=whole(5),
        compiler_params=limit,
        cost_estimate=pl.CostEstimate(flops=200_000_000, bytes_accessed=4_000_000, transcendentals=500_000),
        name="stem_inner",
    )(own, slab_x, stem_w, place)
    upper = pl.pallas_call(
        upper_kernel,
        out_shape=[
            jax.ShapeDtypeStruct((64, 3 * LANES), BF16),
            jax.ShapeDtypeStruct((64, 864), F32),
            jax.ShapeDtypeStruct((96, STEM_ROWS), F32),
            jax.ShapeDtypeStruct((64, 896), BF16),
            jax.ShapeDtypeStruct((192, LANES), BF16),
            jax.ShapeDtypeStruct((192, 2 * LANES), BF16),
        ],
        in_specs=whole(4),
        out_specs=whole(6),
        scratch_shapes=[pltpu.VMEM((3, 96, 7 * LANES), BF16)],
        compiler_params=limit,
        name="upper_cells",
    )(gathered, cols, slope, mid_cols)
    parts = pl.pallas_call(
        lower_kernel,
        out_shape=jax.ShapeDtypeStruct((filts, 13, 16, LANES), BF16),
        in_specs=whole(15),
        out_specs=whole(1)[0],
        scratch_shapes=[
            pltpu.VMEM((7, 48, 2 * LANES), BF16),
            pltpu.VMEM((864, LANES), BF16),
            pltpu.VMEM((3, 96, 3 * LANES), BF16),
        ],
        compiler_params=limit,
        cost_estimate=pl.CostEstimate(flops=600_000_000, bytes_accessed=8_000_000, transcendentals=500_000),
        name="lower_cells",
    )(own, slab_x, border, place, gathered, weights, cols, slope, near_taps, *upper)

    parts = exchange(parts)
    sums = pl.pallas_call(
        sum_kernel,
        out_shape=jax.ShapeDtypeStruct((9, 16, LANES), BF16),
        in_specs=whole(1),
        out_specs=whole(1)[0],
        compiler_params=limit,
        name="sums",
    )(parts)
    sums = lax.all_gather(sums, "space")
    features, middle, stem = pl.pallas_call(
        functools.partial(unpack_kernel, middle_cells**-0.5, stem_cells**-0.5),
        out_shape=[
            jax.ShapeDtypeStruct((16, 16, LANES), BF16),
            jax.ShapeDtypeStruct((27, 16, 32), F32),
            jax.ShapeDtypeStruct((27, 4, 32), F32),
        ],
        in_specs=whole(2),
        out_specs=[pl.BlockSpec(memory_space=pl.ANY)] * 3,
        scratch_shapes=[
            pltpu.VMEM((16, 16, LANES), BF16),
            pltpu.VMEM((27, 16, 32), F32),
            pltpu.VMEM((27, 4, 32), F32),
            pltpu.SemaphoreType.DMA((3,)),
        ],
        compiler_params=limit,
        name="unpack",
    )(sums, parts)
    return features.reshape(16, 1, 16, LANES), middle.transpose(0, 2, 1), stem


def solution(mesh):
    in_specs = (
        P(None, "space", "filt", None),
        P(),
        P(None, None, "filt"),
        P("filt", "space", None, None),
    )
    out_specs = (P("filt", "space", None, None), P(None, None, "filt"), P())
    return jax.shard_map(body, mesh=mesh, in_specs=in_specs, out_specs=out_specs, check_vma=False)
```

```python
import functools

import jax
import jax.numpy as jnp
import numpy as np
from jax import lax
from jax.experimental import pallas as pl
from jax.experimental.pallas import tpu as pltpu
from jax.sharding import PartitionSpec as P

F32 = jnp.float32
BF16 = jnp.bfloat16
LANES = 128
STEM_ROWS = 144


def nn(a, b):
    return lax.dot_general(a, b, (((1,), (0,)), ((), ())), preferred_element_type=F32)


def nt(a, b):
    return lax.dot_general(a, b, (((1,), (1,)), ((), ())), preferred_element_type=F32)


def place_table():
    table = np.zeros((3, LANES, STEM_ROWS), np.float32)
    for even_odd in range(2):
        for a in range(3):
            for b in range(3):
                for d in range(3):
                    q = 2 * even_odd + d - 1
                    group, phase = (2, 3) if q < 0 else (even_odd, q)
                    for c in range(4):
                        column = 48 * a + 16 * b + 4 * phase + c
                        table[group, 4 * (9 * a + 3 * b + d) + c, column] = 1.0
    return table


def rows_lanes(shape):
    return lax.broadcasted_iota(jnp.int32, shape, 0), lax.broadcasted_iota(jnp.int32, shape, 1)


def turn_matrix():
    row, column = rows_lanes((256, 256))
    source = lax.shift_left(row & 15, 4) + lax.shift_right_logical(row, 4)
    return (source == column).astype(F32).astype(BF16)


def regroup_kernel(volume_in, weight_in, cotangent_in, own, slab_x, packed, volume, weight, cotangent, sems):
    channels, planes, width, depth = volume.shape
    pairs = [(weight_in, weight), (cotangent_in, cotangent)]
    pairs += [(volume_in.at[c], volume.at[c]) for c in range(channels)]
    copies = [pltpu.make_async_copy(*pair, sems.at[k]) for k, pair in enumerate(pairs)]
    for copy in copies[2:] + copies[:2]:
        copy.start()
    z, column = rows_lanes((depth, depth))
    source = lax.shift_left(column & (LANES - 1), 2) + lax.shift_right_logical(column, 7)
    select = (z == source).astype(F32).astype(BF16)
    turn = turn_matrix()

    blank = jnp.zeros((16, 32), BF16)
    copies[0].wait()
    taps = [weight[t] if t < 27 else blank for t in range(28)]
    for t in range(7):
        tile = jnp.concatenate(taps[4 * t : 4 * t + 4], axis=1)
        for f in range(packed.shape[0]):
            packed[f, t] = tile
    copies[1].wait()
    turned = nn(turn, cotangent[...].reshape(256, LANES)).astype(BF16)
    for k, f in enumerate(exchange_order(packed.shape[0])):
        for j in range(4):
            row = 16 * (4 * f + j)
            packed[k, 7 + j] = turned[row : row + 16]

    for copy in copies[2:]:
        copy.wait()
    picked = nn(volume[...].reshape(channels * planes * width, depth), select).astype(BF16)
    grouped = []
    for x in range(planes):
        parts = []
        for phase in range(4):
            for c in range(channels):
                start = (c * planes + x) * width
                parts.append(picked[start : start + width, phase * LANES : (phase + 1) * LANES])
        grouped.append(jnp.concatenate(parts, axis=0))
    turned = nn(turn, jnp.concatenate(grouped, axis=1)).astype(BF16)
    for x in range(planes):
        plane = turned[:, x * LANES : (x + 1) * LANES]
        own[x] = plane
        if x > 0:
            slab_x[x - 1] = plane


def border_kernel(slab_x, own, border):
    for x in range(3):
        border[x] = slab_x[x, -48:]
    for x in range(4):
        border[3 + x] = own[x, -48:]


def softplus_sigmoid(values):
    small = jnp.exp(-jnp.abs(values))
    inverse = 1.0 / (1.0 + small)
    soft = jnp.maximum(values, 0.0) + jnp.log(1.0 + small)
    return soft, jnp.where(values >= 0.0, inverse, small * inverse)


def roll_blocks(values, amount):
    blocks = []
    for start in range(0, values.shape[1], LANES):
        block = values[:, start : start + LANES]
        lane = lax.broadcasted_iota(jnp.int32, block.shape, 1)
        edge = 0 if amount == 1 else LANES - 1
        blocks.append(jnp.where(lane == edge, 0.0, pltpu.roll(block, amount % LANES, 1)))
    return jnp.concatenate(blocks, axis=1)


def fill_columns(cols, planes, count):
    for x, plane in enumerate(planes):
        for j in range(count):
            cols[x, :, pl.ds(j * LANES, LANES)] = plane[32 * j : 32 * j + 48]


def stem_forward(weights, cols, i, keep):
    pre = nn(weights, cols[2 * i : 2 * i + 3].reshape(STEM_ROWS, cols.shape[2]))
    pre = jnp.concatenate([pre[0:32] + roll_blocks(pre[64:96], 1), pre[32:64]], axis=0)
    soft, sig = softplus_sigmoid(pre)
    act = (0.3 * pre + 0.7 * soft) * keep
    taps = jnp.concatenate([roll_blocks(act[32:64], 1), act], axis=0).astype(BF16)
    return (0.3 + 0.7 * sig) * keep, taps


def keep_space():
    return jnp.where(lax.axis_index("space") > 0, 1.0, 0.0).astype(F32)


def fill_taps(mid_cols, part, i, j, first, count):
    for b in range(3):
        if (j - b) % 2 == 0 and first <= (j - b) // 2 < first + count:
            row = 96 * (3 * i + b)
            mid_cols[row : row + 96, pl.ds(((j - b) // 2 - first) * LANES, LANES)] = part


def inner_kernel(own, slab_x, stem_w, place, weights, cols, slope, mid_cols, near_taps):
    weights[...] = jnp.concatenate([nn(stem_w[...], place[g]) for g in range(3)], axis=0).astype(BF16)
    planes = [slab_x[x, 16:256] if x < 3 else own[x - 3, 16:256] for x in range(7)]
    fill_columns(cols, planes, 7)
    for i in range(3):
        slope[i], taps = stem_forward(weights[...], cols, i, keep_space() if i == 0 else 1.0)
        for j in range(2, 9):
            fill_taps(mid_cols, taps[:, (j - 2) * LANES : (j - 1) * LANES], i, j, 1, 3)
        near_taps[i] = taps[:, 0:LANES]


def middle_cells_step(mid_w, mid_cols, cotangent):
    pre = nn(mid_w[:, 0:864], mid_cols[...])
    soft, sig = softplus_sigmoid(pre)
    delta = cotangent.astype(F32) * (0.3 + 0.7 * sig)
    delta_low = delta.astype(BF16)
    mid_grad = nt(delta_low, mid_cols[...])
    both = jnp.concatenate([delta_low, roll_blocks(delta, -1).astype(BF16)], axis=0)
    return (0.3 * pre + 0.7 * soft).astype(BF16), mid_grad, both


def put_back(target, i, start, part):
    lanes = pl.ds(start, LANES)
    target[i, 0:64, lanes] = part.astype(BF16)
    target[i, 64:96, lanes] = roll_blocks(part[0:32], -1).astype(BF16)


def upper_kernel(
    gathered, cols, slope, mid_cols, features, mid_grad, stem_grad, mid_w, odd_w, even_w, stem_back,
):
    blocks = gathered.shape[0]
    order = exchange_order(blocks)
    for k, f in enumerate(order):
        for t in range(7):
            mid_w[16 * f : 16 * f + 16, t * LANES : (t + 1) * LANES] = gathered[k, t]
    cotangent = jnp.concatenate(
        [jnp.concatenate([gathered[order.index(f), 7 + j] for j in range(1, 4)], axis=1) for f in range(blocks)],
        axis=0,
    )
    features[...], mid_grad[...], both = middle_cells_step(mid_w, mid_cols, cotangent)

    turned = jnp.concatenate(
        [mid_w[:, t * LANES : (t + 1) * LANES].astype(F32).T for t in range(7)], axis=0
    ).astype(BF16)
    zero = jnp.zeros((32, blocks * 16), BF16)

    def block(a, b, d):
        row = 32 * (9 * a + 3 * b + d)
        return turned[row : row + 32]

    def wide(a, b):
        even = jnp.concatenate([block(a, b, 1), zero], axis=1)
        odd = jnp.concatenate([block(a, b, 2), block(a, b, 0)], axis=1)
        return jnp.concatenate([even, odd], axis=0)

    odd_w[...] = jnp.concatenate([wide(i, 1) for i in range(3)], axis=0)
    even_w[...] = jnp.concatenate(
        [jnp.concatenate([wide(i, 0), wide(i, 2)], axis=1) for i in range(3)], axis=0
    )
    nothing = jnp.zeros((2 * blocks * 16, LANES), BF16)
    pair = jnp.concatenate(
        [jnp.concatenate([both, nothing], axis=1), jnp.concatenate([nothing, both], axis=1)], axis=0
    )
    odd_back = nn(odd_w[...], both)
    even_back = nn(even_w[...], pair)
    total = jnp.zeros((96, STEM_ROWS), F32)
    for i in range(3):
        for j in range(7):
            source = even_back if j % 2 == 0 else odd_back
            part = source[64 * i : 64 * i + 64, (j // 2) * LANES : (j // 2 + 1) * LANES]
            put_back(stem_back, i, j * LANES, part * slope[i, :, pl.ds(j * LANES, LANES)])
        total += nt(stem_back[i], cols[2 * i : 2 * i + 3].reshape(STEM_ROWS, 7 * LANES))
    stem_grad[...] = total


def lower_kernel(
    own, slab_x, border, place, gathered, weights, cols, slope, near_taps, upper_features, upper_mid, upper_stem,
    mid_w, odd_w, even_w, parts, low_cols, mid_cols, low_back,
):
    blocks = gathered.shape[0]
    keep_y = jnp.where(lax.axis_index("filt") > 0, 1.0, 0.0).astype(F32)
    planes = [
        jnp.concatenate([border[x], slab_x[x, 0:32] if x < 3 else own[x - 3, 0:32]], axis=0)
        for x in range(7)
    ]
    fill_columns(low_cols, planes, 2)
    low_slope = []
    for i in range(3):
        keep = jnp.where(lax.broadcasted_iota(jnp.int32, (64, 2 * LANES), 1) < LANES, keep_y, 1.0)
        if i == 0:
            keep = keep * keep_space()
        one_slope, low_taps = stem_forward(weights[...], low_cols, i, keep)
        low_slope.append(one_slope)
        for j in range(2):
            fill_taps(mid_cols, low_taps[:, j * LANES : (j + 1) * LANES], i, j, 0, 1)
        fill_taps(mid_cols, near_taps[i], i, 2, 0, 1)
    order = exchange_order(blocks)
    cotangent = jnp.concatenate([gathered[order.index(f), 7] for f in range(blocks)], axis=0)
    features, mid_grad, both = middle_cells_step(mid_w, mid_cols, cotangent)

    back = [nn(even_w[:, 0:LANES], both), nn(odd_w[...], both), nn(even_w[:, LANES:], both)]
    stem_grad = upper_stem[...]
    for i in range(3):
        for j in range(2):
            part = back[j][64 * i : 64 * i + 64] * low_slope[i][:, j * LANES : (j + 1) * LANES]
            put_back(low_back, i, j * LANES, part)
        put_back(low_back, i, 2 * LANES, back[2][64 * i : 64 * i + 64] * slope[i, :, 0:LANES])
        low = low_cols[2 * i : 2 * i + 3].reshape(STEM_ROWS, 2 * LANES)
        near = cols[2 * i : 2 * i + 3, :, 0:LANES].reshape(STEM_ROWS, LANES)
        stem_grad += nt(low_back[i], jnp.concatenate([low, near], axis=1))
    high = stem_grad.astype(BF16)
    both = jnp.concatenate([high, (stem_grad - high.astype(F32)).astype(BF16)], axis=0)
    stem = 0.0
    for g in range(3):
        rows = jnp.concatenate([both[32 * g : 32 * g + 32], both[96 + 32 * g : 128 + 32 * g]], axis=0)
        taken = nt(rows, place[g])
        stem += taken[0:32] + taken[32:64]
    stem = stem.astype(BF16)

    middle = (mid_grad + upper_mid[...]).astype(BF16)
    middle = jnp.concatenate([middle, jnp.zeros((blocks * 16, 32), BF16)], axis=1)
    for k, f in enumerate(order):
        rows = slice(16 * f, 16 * f + 16)
        for t in range(7):
            parts[k, t] = middle[rows, t * LANES : (t + 1) * LANES]
        for half in range(2):
            parts[k, 7 + half] = stem[16 * half : 16 * half + 16]
        parts[k, 9] = features[rows]
        for j in range(3):
            parts[k, 10 + j] = upper_features[rows, j * LANES : (j + 1) * LANES]


def sum_kernel(parts, sums):
    sums[...] = jnp.sum(parts[:, 0:9].astype(F32), axis=0).astype(BF16)


def unpack_kernel(
    middle_scale, stem_scale, sums, parts, features_out, middle_out, stem_out, features, middle, stem, sems,
):
    copies = [
        pltpu.make_async_copy(source, target, sems.at[k])
        for k, (source, target) in enumerate(
            [(middle, middle_out), (stem, stem_out), (features, features_out)]
        )
    ]
    total = jnp.sum(sums[...].astype(F32), axis=0)
    for t in range(27):
        start = 32 * (t % 4)
        middle[t] = total[t // 4, :, start : start + 32] * middle_scale
    copies[0].start()
    order = exchange_order(parts.shape[0])
    rows = [parts[order.index(f), 9 + j] for f in range(parts.shape[0]) for j in range(4)]
    features[...] = nn(turn_matrix(), jnp.concatenate(rows, axis=0)).astype(BF16).reshape(16, 16, LANES)
    copies[2].start()
    turned = jnp.concatenate([total[7], total[8]], axis=0).T * stem_scale
    for t in range(27):
        stem[t] = turned[4 * t : 4 * t + 4]
    copies[1].start()
    for copy in copies:
        copy.wait()


def exchange_order(filts):
    return sorted(range(filts), key=lambda f: (abs(f - filts // 2), f))


def exchange(chunks):
    groups = [exchange_order(lax.axis_size("filt"))]
    return lax.all_to_all(chunks, "filt", 0, 0, axis_index_groups=groups, tiled=True)


def whole(count):
    return [pl.BlockSpec(memory_space=pltpu.VMEM)] * count


def body(volume, stem_weight, middle_weight, cotangent):
    spaces, filts = lax.axis_size("space"), lax.axis_size("filt")
    channels, planes, width, depth = volume.shape
    stem_cells = (planes // 2) * spaces * (width // 2) * filts * (depth // 2)
    middle_cells = stem_cells // 8
    limit = pltpu.CompilerParams(vmem_limit_bytes=48 * 1024 * 1024)

    raw = (volume, middle_weight.transpose(0, 2, 1), cotangent.reshape(16, 16, LANES))
    own, slab_x, packed = pl.pallas_call(
        regroup_kernel,
        out_shape=[
            jax.ShapeDtypeStruct((planes, 16 * width, LANES), BF16),
            jax.ShapeDtypeStruct((planes - 1, 16 * width, LANES), BF16),
            pltpu.VMEM((filts, 11, 16, LANES), BF16),
        ],
        in_specs=[pl.BlockSpec(memory_space=pltpu.HBM)] * 3,
        out_specs=whole(3),
        scratch_shapes=[
            pltpu.VMEM(volume.shape, BF16),
            pltpu.VMEM((27, 16, 32), BF16),
            pltpu.VMEM((16, 16, LANES), BF16),
            pltpu.SemaphoreType.DMA((2 + channels,)),
        ],
        compiler_params=limit,
        name="regroup",
    )(*[pltpu.with_memory_space_constraint(x, pltpu.HBM) for x in raw])
    slab_x = lax.ppermute(slab_x, "space", [(s - 1, s) for s in range(1, spaces)])
    gathered = exchange(packed)
    border = pl.pallas_call(
        border_kernel,
        out_shape=jax.ShapeDtypeStruct((7, 48, LANES), BF16),
        in_specs=whole(2),
        out_specs=whole(1)[0],
        compiler_params=limit,
        name="border",
    )(slab_x, own)
    border = lax.ppermute(border, "filt", [(f - 1, f) for f in range(1, filts)])

    stem_w = jnp.pad(stem_weight.reshape(108, 32).T, ((0, 0), (0, 20)))
    place = jnp.asarray(place_table(), BF16)
    weights, cols, slope, mid_cols, near_taps = pl.pallas_call(
        inner_kernel,
        out_shape=[
            jax.ShapeDtypeStruct((96, STEM_ROWS), BF16),
            jax.ShapeDtypeStruct((7, 48, 7 * LANES), BF16),
            jax.ShapeDtypeStruct((3, 64, 7 * LANES), F32),
            jax.ShapeDtypeStruct((864, 3 * LANES), BF16),
            jax.ShapeDtypeStruct((3, 96, LANES), BF16),
        ],
        in_specs=whole(4),
        out_specs=whole(5),
        compiler_params=limit,
        cost_estimate=pl.CostEstimate(flops=200_000_000, bytes_accessed=4_000_000, transcendentals=500_000),
        name="stem_inner",
    )(own, slab_x, stem_w, place)
    upper = pl.pallas_call(
        upper_kernel,
        out_shape=[
            jax.ShapeDtypeStruct((64, 3 * LANES), BF16),
            jax.ShapeDtypeStruct((64, 864), F32),
            jax.ShapeDtypeStruct((96, STEM_ROWS), F32),
            jax.ShapeDtypeStruct((64, 896), BF16),
            jax.ShapeDtypeStruct((192, LANES), BF16),
            jax.ShapeDtypeStruct((192, 2 * LANES), BF16),
        ],
        in_specs=whole(4),
        out_specs=whole(6),
        scratch_shapes=[pltpu.VMEM((3, 96, 7 * LANES), BF16)],
        compiler_params=limit,
        name="upper_cells",
    )(gathered, cols, slope, mid_cols)
    parts = pl.pallas_call(
        lower_kernel,
        out_shape=jax.ShapeDtypeStruct((filts, 13, 16, LANES), BF16),
        in_specs=whole(15),
        out_specs=whole(1)[0],
        scratch_shapes=[
            pltpu.VMEM((7, 48, 2 * LANES), BF16),
            pltpu.VMEM((864, LANES), BF16),
            pltpu.VMEM((3, 96, 3 * LANES), BF16),
        ],
        compiler_params=limit,
        cost_estimate=pl.CostEstimate(flops=600_000_000, bytes_accessed=8_000_000, transcendentals=500_000),
        name="lower_cells",
    )(own, slab_x, border, place, gathered, weights, cols, slope, near_taps, *upper)

    parts = exchange(parts)
    sums = pl.pallas_call(
        sum_kernel,
        out_shape=jax.ShapeDtypeStruct((9, 16, LANES), BF16),
        in_specs=whole(1),
        out_specs=whole(1)[0],
        compiler_params=limit,
        name="sums",
    )(parts)
    sums = lax.all_gather(sums, "space")
    features, middle, stem = pl.pallas_call(
        functools.partial(unpack_kernel, middle_cells**-0.5, stem_cells**-0.5),
        out_shape=[
            jax.ShapeDtypeStruct((16, 16, LANES), BF16),
            jax.ShapeDtypeStruct((27, 16, 32), F32),
            jax.ShapeDtypeStruct((27, 4, 32), F32),
        ],
        in_specs=whole(2),
        out_specs=[pl.BlockSpec(memory_space=pl.ANY)] * 3,
        scratch_shapes=[
            pltpu.VMEM((16, 16, LANES), BF16),
            pltpu.VMEM((27, 16, 32), F32),
            pltpu.VMEM((27, 4, 32), F32),
            pltpu.SemaphoreType.DMA((3,)),
        ],
        compiler_params=limit,
        name="unpack",
    )(sums, parts)
    return features.reshape(16, 1, 16, LANES), middle.transpose(0, 2, 1), stem


def solution(mesh):
    in_specs = (
        P(None, "space", "filt", None),
        P(),
        P(None, None, "filt"),
        P("filt", "space", None, None),
    )
    out_specs = (P("filt", "space", None, None), P(None, None, "filt"), P())
    return jax.shard_map(body, mesh=mesh, in_specs=in_specs, out_specs=out_specs, check_vma=False)
```

```python
import functools

import jax
import jax.numpy as jnp
import numpy as np
from jax import lax
from jax.experimental import pallas as pl
from jax.experimental.pallas import tpu as pltpu
from jax.sharding import PartitionSpec as P

F32 = jnp.float32
BF16 = jnp.bfloat16
LANES = 128
STEM_ROWS = 144


def nn(a, b):
    return lax.dot_general(a, b, (((1,), (0,)), ((), ())), preferred_element_type=F32)


def nt(a, b):
    return lax.dot_general(a, b, (((1,), (1,)), ((), ())), preferred_element_type=F32)


def place_table():
    table = np.zeros((3, LANES, STEM_ROWS), np.float32)
    for even_odd in range(2):
        for a in range(3):
            for b in range(3):
                for d in range(3):
                    q = 2 * even_odd + d - 1
                    group, phase = (2, 3) if q < 0 else (even_odd, q)
                    for c in range(4):
                        column = 48 * a + 16 * b + 4 * phase + c
                        table[group, 4 * (9 * a + 3 * b + d) + c, column] = 1.0
    return table


def rows_lanes(shape):
    return lax.broadcasted_iota(jnp.int32, shape, 0), lax.broadcasted_iota(jnp.int32, shape, 1)


def turn_matrix():
    row, column = rows_lanes((256, 256))
    source = lax.shift_left(row & 15, 4) + lax.shift_right_logical(row, 4)
    return (source == column).astype(F32).astype(BF16)


def depth_phases(rows):
    count = rows.shape[0]
    z, column = rows_lanes((256, 256))
    source = lax.shift_left(column & 63, 2) + lax.shift_right_logical(column, 6)
    select = (z == source).astype(F32).astype(BF16)
    halves = jnp.concatenate([rows[:, 0:256], rows[:, 256:512]], axis=0)
    picked = nn(halves, select)
    return [
        jnp.concatenate([picked[h * count : (h + 1) * count, 64 * p : 64 * p + 64] for h in range(2)], axis=1)
        for p in range(4)
    ]


def regroup_kernel(volume_in, weight_in, cotangent_in, own, slab_x, packed, volume, weight, cotangent, sems):
    channels, planes, width, depth = volume.shape
    pairs = [(weight_in, weight), (cotangent_in, cotangent)]
    pairs += [(volume_in.at[c], volume.at[c]) for c in range(channels)]
    copies = [pltpu.make_async_copy(*pair, sems.at[k]) for k, pair in enumerate(pairs)]
    for copy in copies:
        copy.start()
    turn = turn_matrix()

    blank = jnp.zeros((16, 32), BF16)
    copies[0].wait()
    taps = [weight[t] if t < 27 else blank for t in range(28)]
    for t in range(7):
        tile = jnp.concatenate(taps[4 * t : 4 * t + 4], axis=1)
        for f in range(packed.shape[0]):
            packed[f, t] = tile
    copies[1].wait()
    turned = nn(turn, cotangent[...].reshape(256, LANES)).astype(BF16)
    for k, f in enumerate(exchange_order(packed.shape[0])):
        for j in range(4):
            row = 16 * (4 * f + j)
            packed[k, 7 + j] = turned[row : row + 16]

    for copy in copies[2:]:
        copy.wait()
    phases = [part.astype(BF16) for part in depth_phases(volume[...].reshape(channels * planes * width, depth))]
    grouped = []
    for x in range(planes):
        parts = []
        for phase in phases:
            for c in range(channels):
                start = (c * planes + x) * width
                parts.append(phase[start : start + width])
        grouped.append(jnp.concatenate(parts, axis=0))
    turned = nn(turn, jnp.concatenate(grouped, axis=1)).astype(BF16)
    for x in range(planes):
        plane = turned[:, x * LANES : (x + 1) * LANES]
        own[x] = plane
        if x > 0:
            slab_x[x - 1] = plane


def border_kernel(slab_x, own, border):
    for x in range(3):
        border[x] = slab_x[x, -48:]
    for x in range(4):
        border[3 + x] = own[x, -48:]


def softplus_sigmoid(values):
    small = jnp.exp(-jnp.abs(values))
    inverse = 1.0 / (1.0 + small)
    soft = jnp.maximum(values, 0.0) + jnp.log(1.0 + small)
    return soft, jnp.where(values >= 0.0, inverse, small * inverse)


def roll_blocks(values, amount):
    blocks = []
    for start in range(0, values.shape[1], LANES):
        block = values[:, start : start + LANES]
        lane = lax.broadcasted_iota(jnp.int32, block.shape, 1)
        edge = 0 if amount == 1 else LANES - 1
        blocks.append(jnp.where(lane == edge, 0.0, pltpu.roll(block, amount % LANES, 1)))
    return jnp.concatenate(blocks, axis=1)


def fill_columns(cols, planes, count):
    for x, plane in enumerate(planes):
        for j in range(count):
            cols[x, :, pl.ds(j * LANES, LANES)] = plane[32 * j : 32 * j + 48]


def stem_forward(weights, cols, i, keep):
    pre = nn(weights, cols[2 * i : 2 * i + 3].reshape(STEM_ROWS, cols.shape[2]))
    pre = jnp.concatenate([pre[0:32] + roll_blocks(pre[64:96], 1), pre[32:64]], axis=0)
    soft, sig = softplus_sigmoid(pre)
    act = (0.3 * pre + 0.7 * soft) * keep
    taps = jnp.concatenate([roll_blocks(act[32:64], 1), act], axis=0).astype(BF16)
    return (0.3 + 0.7 * sig) * keep, taps


def keep_space():
    return jnp.where(lax.axis_index("space") > 0, 1.0, 0.0).astype(F32)


def fill_taps(mid_cols, part, i, j, first, count):
    for b in range(3):
        if (j - b) % 2 == 0 and first <= (j - b) // 2 < first + count:
            row = 96 * (3 * i + b)
            mid_cols[row : row + 96, pl.ds(((j - b) // 2 - first) * LANES, LANES)] = part


def inner_kernel(own, slab_x, stem_w, place, weights, cols, slope, mid_cols, near_taps):
    weights[...] = jnp.concatenate([nn(stem_w[...], place[g]) for g in range(3)], axis=0).astype(BF16)
    planes = [slab_x[x, 16:256] if x < 3 else own[x - 3, 16:256] for x in range(7)]
    fill_columns(cols, planes, 7)
    for i in range(3):
        slope[i], taps = stem_forward(weights[...], cols, i, keep_space() if i == 0 else 1.0)
        for j in range(2, 9):
            fill_taps(mid_cols, taps[:, (j - 2) * LANES : (j - 1) * LANES], i, j, 1, 3)
        near_taps[i] = taps[:, 0:LANES]


def middle_cells_step(mid_w, mid_cols, cotangent):
    pre = nn(mid_w[:, 0:864], mid_cols[...])
    soft, sig = softplus_sigmoid(pre)
    delta = cotangent.astype(F32) * (0.3 + 0.7 * sig)
    delta_low = delta.astype(BF16)
    mid_grad = nt(delta_low, mid_cols[...])
    both = jnp.concatenate([delta_low, roll_blocks(delta, -1).astype(BF16)], axis=0)
    return (0.3 * pre + 0.7 * soft).astype(BF16), mid_grad, both


def put_back(target, i, start, part):
    lanes = pl.ds(start, LANES)
    target[i, 0:64, lanes] = part.astype(BF16)
    target[i, 64:96, lanes] = roll_blocks(part[0:32], -1).astype(BF16)


def upper_kernel(
    gathered, cols, slope, mid_cols, features, mid_grad, stem_grad, mid_w, odd_w, even_w, stem_back,
):
    blocks = gathered.shape[0]
    order = exchange_order(blocks)
    for k, f in enumerate(order):
        for t in range(7):
            mid_w[16 * f : 16 * f + 16, t * LANES : (t + 1) * LANES] = gathered[k, t]
    cotangent = jnp.concatenate(
        [jnp.concatenate([gathered[order.index(f), 7 + j] for j in range(1, 4)], axis=1) for f in range(blocks)],
        axis=0,
    )
    features[...], mid_grad[...], both = middle_cells_step(mid_w, mid_cols, cotangent)

    turned = jnp.concatenate(
        [mid_w[:, t * LANES : (t + 1) * LANES].astype(F32).T for t in range(7)], axis=0
    ).astype(BF16)
    zero = jnp.zeros((32, blocks * 16), BF16)

    def block(a, b, d):
        row = 32 * (9 * a + 3 * b + d)
        return turned[row : row + 32]

    def wide(a, b):
        even = jnp.concatenate([block(a, b, 1), zero], axis=1)
        odd = jnp.concatenate([block(a, b, 2), block(a, b, 0)], axis=1)
        return jnp.concatenate([even, odd], axis=0)

    odd_w[...] = jnp.concatenate([wide(i, 1) for i in range(3)], axis=0)
    even_w[...] = jnp.concatenate(
        [jnp.concatenate([wide(i, 0), wide(i, 2)], axis=1) for i in range(3)], axis=0
    )
    nothing = jnp.zeros((2 * blocks * 16, LANES), BF16)
    pair = jnp.concatenate(
        [jnp.concatenate([both, nothing], axis=1), jnp.concatenate([nothing, both], axis=1)], axis=0
    )
    odd_back = nn(odd_w[...], both)
    even_back = nn(even_w[...], pair)
    total = jnp.zeros((96, STEM_ROWS), F32)
    for i in range(3):
        for j in range(7):
            source = even_back if j % 2 == 0 else odd_back
            part = source[64 * i : 64 * i + 64, (j // 2) * LANES : (j // 2 + 1) * LANES]
            put_back(stem_back, i, j * LANES, part * slope[i, :, pl.ds(j * LANES, LANES)])
        total += nt(stem_back[i], cols[2 * i : 2 * i + 3].reshape(STEM_ROWS, 7 * LANES))
    stem_grad[...] = total


def lower_kernel(
    own, slab_x, border, place, gathered, weights, cols, slope, near_taps, upper_features, upper_mid, upper_stem,
    mid_w, odd_w, even_w, parts, low_cols, mid_cols, low_back,
):
    blocks = gathered.shape[0]
    keep_y = jnp.where(lax.axis_index("filt") > 0, 1.0, 0.0).astype(F32)
    planes = [
        jnp.concatenate([border[x], slab_x[x, 0:32] if x < 3 else own[x - 3, 0:32]], axis=0)
        for x in range(7)
    ]
    fill_columns(low_cols, planes, 2)
    low_slope = []
    for i in range(3):
        keep = jnp.where(lax.broadcasted_iota(jnp.int32, (64, 2 * LANES), 1) < LANES, keep_y, 1.0)
        if i == 0:
            keep = keep * keep_space()
        one_slope, low_taps = stem_forward(weights[...], low_cols, i, keep)
        low_slope.append(one_slope)
        for j in range(2):
            fill_taps(mid_cols, low_taps[:, j * LANES : (j + 1) * LANES], i, j, 0, 1)
        fill_taps(mid_cols, near_taps[i], i, 2, 0, 1)
    order = exchange_order(blocks)
    cotangent = jnp.concatenate([gathered[order.index(f), 7] for f in range(blocks)], axis=0)
    features, mid_grad, both = middle_cells_step(mid_w, mid_cols, cotangent)

    back = [nn(even_w[:, 0:LANES], both), nn(odd_w[...], both), nn(even_w[:, LANES:], both)]
    stem_grad = upper_stem[...]
    for i in range(3):
        for j in range(2):
            part = back[j][64 * i : 64 * i + 64] * low_slope[i][:, j * LANES : (j + 1) * LANES]
            put_back(low_back, i, j * LANES, part)
        put_back(low_back, i, 2 * LANES, back[2][64 * i : 64 * i + 64] * slope[i, :, 0:LANES])
        low = low_cols[2 * i : 2 * i + 3].reshape(STEM_ROWS, 2 * LANES)
        near = cols[2 * i : 2 * i + 3, :, 0:LANES].reshape(STEM_ROWS, LANES)
        stem_grad += nt(low_back[i], jnp.concatenate([low, near], axis=1))
    high = stem_grad.astype(BF16)
    both = jnp.concatenate([high, (stem_grad - high.astype(F32)).astype(BF16)], axis=0)
    stem = 0.0
    for g in range(3):
        rows = jnp.concatenate([both[32 * g : 32 * g + 32], both[96 + 32 * g : 128 + 32 * g]], axis=0)
        taken = nt(rows, place[g])
        stem += taken[0:32] + taken[32:64]
    stem = stem.astype(BF16)

    middle = (mid_grad + upper_mid[...]).astype(BF16)
    middle = jnp.concatenate([middle, jnp.zeros((blocks * 16, 32), BF16)], axis=1)
    for k, f in enumerate(order):
        rows = slice(16 * f, 16 * f + 16)
        for t in range(7):
            parts[k, t] = middle[rows, t * LANES : (t + 1) * LANES]
        for half in range(2):
            parts[k, 7 + half] = stem[16 * half : 16 * half + 16]
        parts[k, 9] = features[rows]
        for j in range(3):
            parts[k, 10 + j] = upper_features[rows, j * LANES : (j + 1) * LANES]


def sum_kernel(parts, sums):
    sums[...] = jnp.sum(parts[:, 0:9].astype(F32), axis=0).astype(BF16)


def unpack_kernel(
    middle_scale, stem_scale, sums, parts, features_out, middle_out, stem_out, features, middle, stem, sems,
):
    copies = [
        pltpu.make_async_copy(source, target, sems.at[k])
        for k, (source, target) in enumerate(
            [(middle, middle_out), (stem, stem_out), (features, features_out)]
        )
    ]
    total = jnp.sum(sums[...].astype(F32), axis=0)
    for t in range(27):
        start = 32 * (t % 4)
        middle[t] = total[t // 4, :, start : start + 32] * middle_scale
    copies[0].start()
    order = exchange_order(parts.shape[0])
    rows = [parts[order.index(f), 9 + j] for f in range(parts.shape[0]) for j in range(4)]
    features[...] = nn(turn_matrix(), jnp.concatenate(rows, axis=0)).astype(BF16).reshape(16, 16, LANES)
    copies[2].start()
    turned = jnp.concatenate([total[7], total[8]], axis=0).T * stem_scale
    for t in range(27):
        stem[t] = turned[4 * t : 4 * t + 4]
    copies[1].start()
    for copy in copies:
        copy.wait()


def exchange_order(filts):
    return sorted(range(filts), key=lambda f: (abs(f - filts // 2), f))


def exchange(chunks):
    groups = [exchange_order(lax.axis_size("filt"))]
    return lax.all_to_all(chunks, "filt", 0, 0, axis_index_groups=groups, tiled=True)


def whole(count):
    return [pl.BlockSpec(memory_space=pltpu.VMEM)] * count


def body(volume, stem_weight, middle_weight, cotangent):
    spaces, filts = lax.axis_size("space"), lax.axis_size("filt")
    channels, planes, width, depth = volume.shape
    stem_cells = (planes // 2) * spaces * (width // 2) * filts * (depth // 2)
    middle_cells = stem_cells // 8
    limit = pltpu.CompilerParams(vmem_limit_bytes=48 * 1024 * 1024)

    raw = (volume, middle_weight.transpose(0, 2, 1), cotangent.reshape(16, 16, LANES))
    own, slab_x, packed = pl.pallas_call(
        regroup_kernel,
        out_shape=[
            jax.ShapeDtypeStruct((planes, 16 * width, LANES), BF16),
            jax.ShapeDtypeStruct((planes - 1, 16 * width, LANES), BF16),
            pltpu.VMEM((filts, 11, 16, LANES), BF16),
        ],
        in_specs=[pl.BlockSpec(memory_space=pltpu.HBM)] * 3,
        out_specs=whole(3),
        scratch_shapes=[
            pltpu.VMEM(volume.shape, BF16),
            pltpu.VMEM((27, 16, 32), BF16),
            pltpu.VMEM((16, 16, LANES), BF16),
            pltpu.SemaphoreType.DMA((2 + channels,)),
        ],
        compiler_params=limit,
        name="regroup",
    )(*[pltpu.with_memory_space_constraint(x, pltpu.HBM) for x in raw])
    slab_x = lax.ppermute(slab_x, "space", [(s - 1, s) for s in range(1, spaces)])
    gathered = exchange(packed)
    border = pl.pallas_call(
        border_kernel,
        out_shape=jax.ShapeDtypeStruct((7, 48, LANES), BF16),
        in_specs=whole(2),
        out_specs=whole(1)[0],
        compiler_params=limit,
        name="border",
    )(slab_x, own)
    border = lax.ppermute(border, "filt", [(f - 1, f) for f in range(1, filts)])

    stem_w = jnp.pad(stem_weight.reshape(108, 32).T, ((0, 0), (0, 20)))
    place = jnp.asarray(place_table(), BF16)
    weights, cols, slope, mid_cols, near_taps = pl.pallas_call(
        inner_kernel,
        out_shape=[
            jax.ShapeDtypeStruct((96, STEM_ROWS), BF16),
            jax.ShapeDtypeStruct((7, 48, 7 * LANES), BF16),
            jax.ShapeDtypeStruct((3, 64, 7 * LANES), F32),
            jax.ShapeDtypeStruct((864, 3 * LANES), BF16),
            jax.ShapeDtypeStruct((3, 96, LANES), BF16),
        ],
        in_specs=whole(4),
        out_specs=whole(5),
        compiler_params=limit,
        cost_estimate=pl.CostEstimate(flops=200_000_000, bytes_accessed=4_000_000, transcendentals=500_000),
        name="stem_inner",
    )(own, slab_x, stem_w, place)
    upper = pl.pallas_call(
        upper_kernel,
        out_shape=[
            jax.ShapeDtypeStruct((64, 3 * LANES), BF16),
            jax.ShapeDtypeStruct((64, 864), F32),
            jax.ShapeDtypeStruct((96, STEM_ROWS), F32),
            jax.ShapeDtypeStruct((64, 896), BF16),
            jax.ShapeDtypeStruct((192, LANES), BF16),
            jax.ShapeDtypeStruct((192, 2 * LANES), BF16),
        ],
        in_specs=whole(4),
        out_specs=whole(6),
        scratch_shapes=[pltpu.VMEM((3, 96, 7 * LANES), BF16)],
        compiler_params=limit,
        name="upper_cells",
    )(gathered, cols, slope, mid_cols)
    parts = pl.pallas_call(
        lower_kernel,
        out_shape=jax.ShapeDtypeStruct((filts, 13, 16, LANES), BF16),
        in_specs=whole(15),
        out_specs=whole(1)[0],
        scratch_shapes=[
            pltpu.VMEM((7, 48, 2 * LANES), BF16),
            pltpu.VMEM((864, LANES), BF16),
            pltpu.VMEM((3, 96, 3 * LANES), BF16),
        ],
        compiler_params=limit,
        cost_estimate=pl.CostEstimate(flops=600_000_000, bytes_accessed=8_000_000, transcendentals=500_000),
        name="lower_cells",
    )(own, slab_x, border, place, gathered, weights, cols, slope, near_taps, *upper)

    parts = exchange(parts)
    sums = pl.pallas_call(
        sum_kernel,
        out_shape=jax.ShapeDtypeStruct((9, 16, LANES), BF16),
        in_specs=whole(1),
        out_specs=whole(1)[0],
        compiler_params=limit,
        name="sums",
    )(parts)
    sums = lax.all_gather(sums, "space")
    features, middle, stem = pl.pallas_call(
        functools.partial(unpack_kernel, middle_cells**-0.5, stem_cells**-0.5),
        out_shape=[
            jax.ShapeDtypeStruct((16, 16, LANES), BF16),
            jax.ShapeDtypeStruct((27, 16, 32), F32),
            jax.ShapeDtypeStruct((27, 4, 32), F32),
        ],
        in_specs=whole(2),
        out_specs=[pl.BlockSpec(memory_space=pl.ANY)] * 3,
        scratch_shapes=[
            pltpu.VMEM((16, 16, LANES), BF16),
            pltpu.VMEM((27, 16, 32), F32),
            pltpu.VMEM((27, 4, 32), F32),
            pltpu.SemaphoreType.DMA((3,)),
        ],
        compiler_params=limit,
        name="unpack",
    )(sums, parts)
    return features.reshape(16, 1, 16, LANES), middle.transpose(0, 2, 1), stem


def solution(mesh):
    in_specs = (
        P(None, "space", "filt", None),
        P(),
        P(None, None, "filt"),
        P("filt", "space", None, None),
    )
    out_specs = (P("filt", "space", None, None), P(None, None, "filt"), P())
    return jax.shard_map(body, mesh=mesh, in_specs=in_specs, out_specs=out_specs, check_vma=False)
```
